32 devices in a mesh: dp: 8 (over z, x), fsdp: 4 (over y, core).
Axes of the slice: x: 2, y: 2, z: 4, core: 2. Of those that a mesh axis runs over, the one named last changes fastest.
Arguments:
- tokens: bfloat16 [4, 64, 512, 512], P(None, ('dp', 'fsdp'))
- memory_state: bfloat16 [4, 64, 20, 512], P(None, ('dp', 'fsdp')), may hold values from -6 to 6
- cotangent: bfloat16 [4, 64, 532, 512], P(None, ('dp', 'fsdp')), may hold values from -6 to 6
- in_weight: float32 [512, 1536], P(('dp', 'fsdp')), may hold values from -0.25 to 0.25
- in_first: float32 [512, 1536], P(('dp', 'fsdp')), may hold values from -0.0034179688 to 0.0034179688
- in_second: float32 [512, 1536], P(('dp', 'fsdp')), may hold values from 3.1624432e-07 to 1.2649773e-06
- out_weight: float32 [512, 512], P(None, ('dp', 'fsdp')), may hold values from -1 to 1
- out_first: float32 [512, 512], P(None, ('dp', 'fsdp')), may hold values from -0.0034179688 to 0.0034179688
- out_second: float32 [512, 512], P(None, ('dp', 'fsdp')), may hold values from 3.1624432e-07 to 1.2649773e-06
- up_weight: float32 [512, 2048], P(('dp', 'fsdp')), may hold values from -0.25 to 0.25
- up_first: float32 [512, 2048], P(('dp', 'fsdp')), may hold values from -0.0034179688 to 0.0034179688
- up_second: float32 [512, 2048], P(('dp', 'fsdp')), may hold values from 3.1624432e-07 to 1.2649773e-06
- down_weight: float32 [2048, 512], P(None, ('dp', 'fsdp')), may hold values from -0.125 to 0.125
- down_first: float32 [2048, 512], P(None, ('dp', 'fsdp')), may hold values from -0.0034179688 to 0.0034179688
- down_second: float32 [2048, 512], P(None, ('dp', 'fsdp')), may hold values from 3.1624432e-07 to 1.2649773e-06
- vectors: float32 [8, 512], P(None, ('dp', 'fsdp'))
- vectors_first: float32 [8, 512], P(None, ('dp', 'fsdp')), may hold values from -0.0034179688 to 0.0034179688
- vectors_second: float32 [8, 512], P(None, ('dp', 'fsdp')), may hold values from 3.1624432e-07 to 1.2649773e-06
- up_bias: float32 [2048], P(('dp', 'fsdp')), may hold values from -1.75 to 1.75
- up_bias_first: float32 [2048], P(('dp', 'fsdp')), may hold values from -0.0034179688 to 0.0034179688
- up_bias_second: float32 [2048], P(('dp', 'fsdp')), may hold values from 3.1624432e-07 to 1.2649773e-06
- memory_embed: float32 [20, 512], P(None, ('dp', 'fsdp')), may hold values from -6 to 6
- memory_first: float32 [20, 512], P(None, ('dp', 'fsdp')), may hold values from -0.00061035156 to 0.00061035156
- memory_second: float32 [20, 512], P(None, ('dp', 'fsdp')), may hold values from 1.18888845e-08 to 4.7555538e-08
Outputs:
- output: bfloat16 [4, 64, 532, 512], P(None, ('dp', 'fsdp'))
- input_grad: float32 [4, 64, 512, 512], P(None, ('dp', 'fsdp'))
- in_weight_new: float32 [512, 1536], P(('dp', 'fsdp'))
- in_first_new: float32 [512, 1536], P(('dp', 'fsdp'))
- in_second_new: float32 [512, 1536], P(('dp', 'fsdp'))
- out_weight_new: float32 [512, 512], P(None, ('dp', 'fsdp'))
- out_first_new: float32 [512, 512], P(None, ('dp', 'fsdp'))
- out_second_new: float32 [512, 512], P(None, ('dp', 'fsdp'))
- up_weight_new: float32 [512, 2048], P(('dp', 'fsdp'))
- up_first_new: float32 [512, 2048], P(('dp', 'fsdp'))
- up_second_new: float32 [512, 2048], P(('dp', 'fsdp'))
- down_weight_new: float32 [2048, 512], P(None, ('dp', 'fsdp'))
- down_first_new: float32 [2048, 512], P(None, ('dp', 'fsdp'))
- down_second_new: float32 [2048, 512], P(None, ('dp', 'fsdp'))
- vectors_new: float32 [8, 512], P(None, ('dp', 'fsdp'))
- vectors_first_new: float32 [8, 512], P(None, ('dp', 'fsdp'))
- vectors_second_new: float32 [8, 512], P(None, ('dp', 'fsdp'))
- up_bias_new: float32 [2048], P(('dp', 'fsdp'))
- up_bias_first_new: float32 [2048], P(('dp', 'fsdp'))
- up_bias_second_new: float32 [2048], P(('dp', 'fsdp'))
- memory_embed_new: float32 [20, 512], P(None, ('dp', 'fsdp'))
- memory_first_new: float32 [20, 512], P(None, ('dp', 'fsdp'))
- memory_second_new: float32 [20, 512], P(None, ('dp', 'fsdp'))
- grad_norm: float32 [], replicated
The draws below stay inside these ranges and needn't reach their ends.
All inputs are finite; a program needn't handle non-finite values.
Results may differ from the reference program's by a relative error of at most 0.012.
The reference program's roundings to bfloat16 on the way count: a program that leaves them out, or rounds other values in their place, can miss the bound.
Values may be sent and summed in bfloat16 or wider, within the bound.
No kernel may reach another device: no remote copies, remote signals or barrier semaphores. Data moves between devices by JAX's collectives and lax.ppermute only.
A program may use at most 192 MiB of HBM per device.

```python
import math
import jax
import jax.numpy as jnp
from jax import lax

D = 512
FF = 2048
MEM = 20
SEQ = 512
MB = 4
STEP = 7
HDIM = 64
SPANS = 64
NPARAM = 3162112


def draw_tokens(key, part):
    key = jax.random.fold_in(key, 11)
    place = jnp.arange(D, dtype=jnp.float32) / (D - 1)
    ramp = 1.0 + 0.75 * place
    base = jnp.clip(jax.random.normal(key, (MB, SPANS, SEQ, D), jnp.float32), -6.0, 6.0)
    return (base * ramp).astype(jnp.bfloat16)


def draw_vectors(key, part):
    key = jax.random.fold_in(key, 23)
    place = jnp.arange(D, dtype=jnp.float32) / (D - 1)
    ramp = 1.0 + 0.7 * place
    noise = jnp.clip(jax.random.normal(key, (8, D), jnp.float32), -3.0, 3.0)
    biases = 0.3 * noise
    gains = ramp * (1.0 + 0.1 * noise)
    rows = [biases[0], biases[1], biases[2], biases[3], gains[4], biases[5], gains[6], biases[7]]
    return jnp.stack(rows).astype(jnp.float32)


def levels(own_key, dims, shards, low, top_value):
    def one(dim, blocks):
        heights = jax.random.uniform(jax.random.fold_in(jax.random.fold_in(own_key, 6), dim), (blocks,), jnp.float32, low / len(shards), top_value / len(shards))
        return jnp.repeat(jnp.exp(heights), dims[dim] // blocks).reshape((-1,) + (1,) * (len(dims) - dim - 1))

    factor_of = one(*shards[0])
    for cut in shards[1:]:
        factor_of = factor_of * one(*cut)
    return factor_of


def gaussian(own_key, shape, scale, reach, cuts=(), kind=jnp.bfloat16):
    entries = scale * jax.random.normal(own_key, shape, jnp.float32)
    if cuts:
        entries = entries * levels(own_key, shape, cuts, -0.22, 0.18)
    return jnp.clip(entries, -reach, reach).astype(kind)


def setup_inputs(seed: int = 0) -> dict:
    seeds = jax.random.split(jax.random.key(seed), 25)
    tokens = draw_tokens(jax.random.fold_in(seeds[24], 71), 0)
    memory_state = gaussian(seeds[1], (MB, SPANS, MEM, D), 1.0, 6.0, ((1, 32),))
    cotangent = gaussian(seeds[2], (MB, SPANS, MEM + SEQ, D), 1.0, 6.0, ((1, 32),))
    in_weight = gaussian(seeds[3], (D, 3 * D), D ** -0.5, 0.25, ((0, 32),), jnp.float32)
    in_first = gaussian(seeds[4], (D, 3 * D), (NPARAM ** -0.5), 0.0034179688, ((0, 32),), jnp.float32)
    in_second = jnp.clip(jnp.exp(math.log(1.264977299797465e-06) - 1.3862944 * jax.random.uniform(seeds[5], (D, 3 * D), jnp.float32) ** levels(seeds[5], (D, 3 * D), ((0, 32),), -0.2, 0.2)), 3.1624432494936627e-07, 1.264977299797465e-06)
    out_weight = gaussian(seeds[6], (D, D), (D * 32 // (MEM + SEQ)) ** -0.5, 1.0, ((1, 32),), jnp.float32)
    out_first = gaussian(seeds[7], (D, D), (NPARAM ** -0.5), 0.0034179688, ((1, 32),), jnp.float32)
    out_second = jnp.clip(jnp.exp(math.log(1.264977299797465e-06) - 1.3862944 * jax.random.uniform(seeds[8], (D, D), jnp.float32) ** levels(seeds[8], (D, D), ((1, 32),), -0.2, 0.2)), 3.1624432494936627e-07, 1.264977299797465e-06)
    up_weight = gaussian(seeds[9], (D, FF), D ** -0.5, 0.25, ((0, 32),), jnp.float32)
    up_first = gaussian(seeds[10], (D, FF), (NPARAM ** -0.5), 0.0034179688, ((0, 32),), jnp.float32)
    up_second = jnp.clip(jnp.exp(math.log(1.264977299797465e-06) - 1.3862944 * jax.random.uniform(seeds[11], (D, FF), jnp.float32) ** levels(seeds[11], (D, FF), ((0, 32),), -0.2, 0.2)), 3.1624432494936627e-07, 1.264977299797465e-06)
    down_weight = gaussian(seeds[12], (FF, D), FF ** -0.5, 0.125, ((1, 32),), jnp.float32)
    down_first = gaussian(seeds[13], (FF, D), (NPARAM ** -0.5), 0.0034179688, ((1, 32),), jnp.float32)
    down_second = jnp.clip(jnp.exp(math.log(1.264977299797465e-06) - 1.3862944 * jax.random.uniform(seeds[14], (FF, D), jnp.float32) ** levels(seeds[14], (FF, D), ((1, 32),), -0.2, 0.2)), 3.1624432494936627e-07, 1.264977299797465e-06)
    vectors = draw_vectors(jax.random.fold_in(seeds[24], 71), 0)
    vectors_first = gaussian(seeds[16], (8, D), (NPARAM ** -0.5), 0.0034179688, ((1, 32),), jnp.float32)
    vectors_second = jnp.clip(jnp.exp(math.log(1.264977299797465e-06) - 1.3862944 * jax.random.uniform(seeds[17], (8, D), jnp.float32) ** levels(seeds[17], (8, D), ((1, 32),), -0.2, 0.2)), 3.1624432494936627e-07, 1.264977299797465e-06)
    up_bias = gaussian(seeds[18], (FF,), 0.3, 1.75, ((0, 32),), jnp.float32)
    up_bias_first = gaussian(seeds[19], (FF,), (NPARAM ** -0.5), 0.0034179688, ((0, 32),), jnp.float32)
    up_bias_second = jnp.clip(jnp.exp(math.log(1.264977299797465e-06) - 1.3862944 * jax.random.uniform(seeds[20], (FF,), jnp.float32) ** levels(seeds[20], (FF,), ((0, 32),), -0.2, 0.2)), 3.1624432494936627e-07, 1.264977299797465e-06)
    memory_embed = gaussian(seeds[21], (MEM, D), 1.0, 6.0, ((1, 32),), jnp.float32)
    memory_first = gaussian(seeds[22], (MEM, D), (4.47213595 * NPARAM ** -0.5 * (MEM + SEQ) ** -0.5), 0.00061035156, ((1, 32),), jnp.float32)
    memory_second = jnp.clip(jnp.exp(math.log(4.755553817403779e-08) - 1.3862944 * jax.random.uniform(seeds[23], (MEM, D), jnp.float32) ** levels(seeds[23], (MEM, D), ((1, 32),), -0.2, 0.2)), 1.1888884543509448e-08, 4.755553817403779e-08)
    return dict(tokens=tokens, memory_state=memory_state, cotangent=cotangent, in_weight=in_weight, in_first=in_first, in_second=in_second, out_weight=out_weight, out_first=out_first, out_second=out_second, up_weight=up_weight, up_first=up_first, up_second=up_second, down_weight=down_weight, down_first=down_first, down_second=down_second, vectors=vectors, vectors_first=vectors_first, vectors_second=vectors_second, up_bias=up_bias, up_bias_first=up_bias_first, up_bias_second=up_bias_second, memory_embed=memory_embed, memory_first=memory_first, memory_second=memory_second)


@jax.custom_vjp
def low(v):
    return lax.optimization_barrier(v.astype(jnp.bfloat16)).astype(jnp.float32)

@jax.custom_vjp
def low_back(v):
    return v

def low_keep(v):
    return (low(v), None)

def low_pass(kept, grad):
    return (grad,)

def back_keep(v):
    return (v, None)

def back_low(kept, grad):
    return (low(grad),)
low.defvjp(low_keep, low_pass)
low_back.defvjp(back_keep, back_low)
norm_eps = 1e-05

def normalize(value, gain, shift):
    center = value - lax.optimization_barrier(jnp.mean(value, axis=-1, keepdims=True))
    rstd = lax.rsqrt(lax.optimization_barrier(jnp.mean(center * center, axis=-1, keepdims=True)) + norm_eps)
    return center * rstd * gain + shift

def layer(params, full, allowed):
    in_w, out_w, up_w, down_w, vecs, up_b = params
    highest = lax.Precision.HIGHEST
    count, length, width = full.shape
    heads = width // HDIM
    inputs = low(full)
    joint = jnp.einsum('csd,de->cse', inputs, in_w, precision=highest)
    query = low(low_back(joint[..., :width] + vecs[0])).reshape(count, length, heads, HDIM)
    keys = low(low_back(joint[..., width:2 * width])).reshape(count, length, heads, HDIM)
    values = low(low_back(joint[..., 2 * width:] + vecs[1])).reshape(count, length, heads, HDIM)
    scores = low_back(jnp.einsum('cqhe,ckhe->chqk', query, keys, precision=highest) * HDIM ** (-0.5))
    scores = jnp.where(allowed, scores, -1e+30)
    probs = low(jax.nn.softmax(scores, axis=-1))
    mixed = jnp.einsum('chqk,ckhe->cqhe', probs, values, precision=highest).reshape(count, length, width)
    mixed = low(low_back(mixed))
    attended = low_back(jnp.einsum('csd,de->cse', mixed, out_w, precision=highest) + vecs[2])
    first = normalize(full + attended, vecs[4], vecs[5])
    hidden_pre = low_back(jnp.einsum('csd,df->csf', low(first), up_w, precision=highest) + up_b)
    hidden = low(jax.nn.gelu(hidden_pre, approximate=True))
    branch = low_back(jnp.einsum('csf,fd->csd', hidden, down_w, precision=highest) + vecs[3])
    return normalize(first + branch, vecs[6], vecs[7])

def group_fn(lowered, pair, allowed):
    span_tokens, span_state = pair
    full = jnp.concatenate([lowered[6][None] + span_state, span_tokens], axis=1)
    return layer(lowered[:6], full, allowed)

def adam_step(weight, first, second, grad, rate, decay):
    first_new = 0.5 * first + 0.5 * grad
    second_new = 0.5 * second + 0.5 * grad * grad
    correction = 1.0 - 0.5 ** STEP
    weight_new = weight - rate * (first_new / correction / (jnp.sqrt(second_new / correction) + 1e-08) + decay * weight)
    return (weight_new, first_new, second_new)

def reference(tokens, memory_state, cotangent, in_weight, in_first, in_second, out_weight, out_first, out_second, up_weight, up_first, up_second, down_weight, down_first, down_second, vectors, vectors_first, vectors_second, up_bias, up_bias_first, up_bias_second, memory_embed, memory_first, memory_second):
    length = MEM + SEQ
    place = jnp.arange(length)
    allowed = (place[None, :] < MEM) | (place[:, None] < MEM) | (place[None, :] <= place[:, None])
    state = jnp.swapaxes(memory_state.astype(jnp.float32), 0, 1)
    masters = (in_weight, out_weight, up_weight, down_weight, vectors, up_bias, memory_embed)

    def model(token_values, *weights):
        lowered = tuple((low(w) for w in weights))
        checked = jax.checkpoint(group_fn)

        def one_group(pair):
            return checked(lowered, pair, allowed)
        result = lax.map(one_group, (jnp.swapaxes(token_values, 0, 1), state))
        return jnp.swapaxes(result, 0, 1)
    output, pull = jax.vjp(model, tokens.astype(jnp.float32), *masters)
    grads = pull(cotangent.astype(jnp.float32))
    input_grad = grads[0]
    weight_grads = grads[1:]
    total = jnp.float32(0.0)
    for grad in weight_grads:
        total = total + jnp.sum(grad * grad)
    grad_norm = jnp.sqrt(total)
    factor = 1.0 / jnp.maximum(grad_norm, 1.0)
    rates = (0.5 * D ** (-0.5), 0.5 * (D * 32 // (MEM + SEQ)) ** (-0.5), 0.5 * D ** (-0.5), 0.5 * FF ** (-0.5), 0.1, 0.1, 0.5)
    decays = (0.1, 0.1, 0.1, 0.1, 0.0, 0.0, 0.0)
    firsts = (in_first, out_first, up_first, down_first, vectors_first, up_bias_first, memory_first)
    seconds = (in_second, out_second, up_second, down_second, vectors_second, up_bias_second, memory_second)
    results = []
    for index in range(7):
        results.extend(adam_step(masters[index], firsts[index], seconds[index], weight_grads[index] * factor, rates[index], decays[index]))
    return (output.astype(jnp.bfloat16), input_grad, results[0], results[1], results[2], results[3], results[4], results[5], results[6], results[7], results[8], results[9], results[10], results[11], results[12], results[13], results[14], results[15], results[16], results[17], results[18], results[19], results[20], grad_norm)
```

```python
from functools import partial

import jax
import jax.numpy as jnp
from jax import lax
from jax.experimental import pallas as pl
from jax.experimental.pallas import tpu as pltpu
from jax.sharding import PartitionSpec as P

STEP = 7
HDIM = 64
PAD = 32
HALF = 256
FCHUNK = 256
ROWS = 32
BF = jnp.bfloat16
FL = jnp.float32
AXES = ("dp", "fsdp")
NEG = -1e30
EPS = 1e-05
SCALE = HDIM ** (-0.5)


def dot(a, b, ca, cb):
    return lax.dot_general(a, b, (((ca,), (cb,)), ((), ())), preferred_element_type=FL)


def head_mask(rows, width):
    row = lax.broadcasted_iota(jnp.int32, (rows, width), 0) // PAD
    col = lax.broadcasted_iota(jnp.int32, (rows, width), 1) // HDIM
    return row == col


def spread(x, heads):
    tiled = jnp.concatenate([x.astype(FL)] * heads, axis=0)
    return jnp.where(head_mask(*tiled.shape), tiled, 0.0).astype(BF)


def fold(y, heads):
    own = jnp.where(head_mask(*y.shape), y, 0.0)
    return sum(own[h * PAD : (h + 1) * PAD] for h in range(heads))


def pair_masks(width):
    col = lax.broadcasted_iota(jnp.int32, (1, width), 1)
    low = jnp.where(col < HDIM, 1.0, 0.0)
    return low.astype(BF), (1.0 - low).astype(BF)


def attend_kernel(
    extra,
    tok_ref,
    state_ref,
    memb_ref,
    vec_ref,
    inw_ref,
    qkv_ref,
    pt_ref,
    ptk_ref,
    ptq_ref,
    mixed_ref,
    vt_ref,
    sk_ref,
    ot_ref,
):
    length, width = tok_ref.shape[1:]
    heads = width // HDIM
    rows = length + PAD
    memory = (state_ref[0].astype(FL) + memb_ref[...]).astype(BF)
    inputs = jnp.concatenate([tok_ref[0], memory], axis=0)
    qkv_ref[0, :, :width] = ((dot(inputs, inw_ref[:, :width], 1, 0) + vec_ref[0:1, :]) * SCALE).astype(BF)
    qkv_ref[0, :, width : 2 * width] = dot(inputs, inw_ref[:, width : 2 * width], 1, 0).astype(BF)
    qkv_ref[0, :, 2 * width :] = (dot(inputs, inw_ref[:, 2 * width :], 1, 0) + vec_ref[1:2, :]).astype(BF)
    vt_ref[...] = qkv_ref[0, :length, 2 * width :].T

    key_place = lax.broadcasted_iota(jnp.int32, (heads * PAD, 1), 0) % PAD
    k_mem = spread(qkv_ref[0, length:, width : 2 * width], heads)
    sk_ref[...] = jnp.where(key_place < extra, dot(k_mem, qkv_ref[0, :length, :width], 1, 1), NEG)

    q_mem = spread(qkv_ref[0, length:, :width], heads)
    sq = dot(qkv_ref[0, :, width : 2 * width], q_mem, 1, 1)
    place = lax.broadcasted_iota(jnp.int32, (rows, 1), 0)
    sq = jnp.where(place < length + extra, sq, NEG)
    eq = jnp.exp(sq - jnp.max(sq, axis=0, keepdims=True))
    ptq_ref[0] = (eq * (1.0 / jnp.sum(eq, axis=0, keepdims=True))).astype(BF)
    om = dot(ptq_ref[0], qkv_ref[0, :, 2 * width :], 0, 0)
    mixed_ref[0, length:, :] = fold(om, heads).astype(BF)

    diag = lax.broadcasted_iota(jnp.int32, (HALF, HALF), 0) <= lax.broadcasted_iota(
        jnp.int32, (HALF, HALF), 1
    )
    masks = pair_masks(2 * HDIM)

    def pair(p, carry):
        lanes = pl.ds(pl.multiple_of(p * 2 * HDIM, 2 * HDIM), 2 * HDIM)
        key_lanes = pl.ds(pl.multiple_of(width + p * 2 * HDIM, 2 * HDIM), 2 * HDIM)
        kp = qkv_ref[0, :length, key_lanes]
        for side in range(2):
            h = 2 * p + side
            km = kp * masks[side]
            own = pl.ds(pl.multiple_of(h * PAD, PAD), PAD)
            feat = pl.ds(pl.multiple_of(h * HDIM, HDIM), HDIM)
            for part in range(length // HALF):
                cols = pl.ds(part * HALF, HALF)
                below = part * HALF
                upto = below + HALF
                qp = qkv_ref[0, cols, lanes]
                s_diag = jnp.where(diag, dot(km[below:upto], qp, 1, 1), NEG)
                s_mem = sk_ref[own, cols]
                top = jnp.maximum(
                    jnp.max(s_diag, axis=0, keepdims=True), jnp.max(s_mem, axis=0, keepdims=True)
                )
                if part:
                    s_low = dot(km[:below], qp, 1, 1)
                    top = jnp.maximum(top, jnp.max(s_low, axis=0, keepdims=True))
                e_diag = jnp.exp(s_diag - top)
                e_mem = jnp.exp(s_mem - top)
                total = jnp.sum(e_diag, axis=0, keepdims=True) + jnp.sum(e_mem, axis=0, keepdims=True)
                if part:
                    e_low = jnp.exp(s_low - top)
                    total = total + jnp.sum(e_low, axis=0, keepdims=True)
                share = 1.0 / total
                base = part * (part + 1) // 2 * HALF
                if part:
                    pt_ref[0, h, base : base + below, :] = (e_low * share).astype(BF)
                pt_ref[0, h, base + below : base + upto, :] = (e_diag * share).astype(BF)
                ptk_ref[0, own, cols] = (e_mem * share).astype(BF)
                ot_ref[feat, cols] = dot(vt_ref[feat, :upto], pt_ref[0, h, base : base + upto, :], 1, 0)
        return carry

    lax.fori_loop(0, heads // 2, pair, 0)
    v_mem = spread(qkv_ref[0, length:, 2 * width :], heads)
    om_t = ot_ref[...] + dot(v_mem, ptk_ref[0], 0, 0)
    mixed_ref[0, :length, :] = om_t.astype(BF).T


def attend(extra, tok, state, memb, vecs, in_w):
    count, length, width = tok.shape
    heads = width // HDIM
    rows = length + PAD
    parts = length // HALF
    ptrows = parts * (parts + 1) // 2 * HALF
    one = lambda *dims: pl.BlockSpec((1,) + dims, lambda b: (b,) + (0,) * len(dims))
    whole = lambda *dims: pl.BlockSpec(dims, lambda b: (0,) * len(dims))
    return pl.pallas_call(
        partial(attend_kernel, extra),
        grid=(count,),
        in_specs=[
            one(length, width),
            one(PAD, width),
            whole(PAD, width),
            whole(8, width),
            whole(width, 3 * width),
        ],
        out_specs=[
            one(rows, 3 * width),
            one(heads, ptrows, HALF),
            one(heads * PAD, length),
            one(rows, heads * PAD),
            one(rows, width),
        ],
        out_shape=[
            jax.ShapeDtypeStruct((count, rows, 3 * width), BF),
            jax.ShapeDtypeStruct((count, heads, ptrows, HALF), BF),
            jax.ShapeDtypeStruct((count, heads * PAD, length), BF),
            jax.ShapeDtypeStruct((count, rows, heads * PAD), BF),
            jax.ShapeDtypeStruct((count, rows, width), BF),
        ],
        scratch_shapes=[
            pltpu.VMEM((width, length), BF),
            pltpu.VMEM((heads * PAD, length), FL),
            pltpu.VMEM((width, length), FL),
        ],
        compiler_params=pltpu.CompilerParams(vmem_limit_bytes=56 << 20),
        name="attend",
    )(tok, state, memb, vecs, in_w)


def norm_rows(x):
    center = x - jnp.mean(x, axis=-1, keepdims=True)
    rstd = lax.rsqrt(jnp.mean(center * center, axis=-1, keepdims=True) + EPS)
    return center * rstd, rstd


def norm_back(grad, normed, rstd, gain):
    scaled = grad * gain
    return rstd * (
        scaled
        - jnp.mean(scaled, axis=-1, keepdims=True)
        - normed * jnp.mean(scaled * normed, axis=-1, keepdims=True)
    )


def by_eight(x):
    return jnp.sum(x.reshape(x.shape[0] // 8, 8, x.shape[1]), axis=0)


def feed_kernel(
    tok_ref,
    state_ref,
    memb_ref,
    vec_ref,
    upb_ref,
    wide_ref,
    mixed_ref,
    cot_ref,
    out_ref,
    one_ref,
    gm_ref,
    gwide_ref,
    gvec_ref,
    gupb_ref,
    acc_ref,
    sums_ref,
    upb_sum_ref,
    att_ref,
    n1_ref,
    r1_ref,
    low_ref,
    g2_ref,
    gb_ref,
    hidden_ref,
    slope_ref,
    gpre_ref,
    ga_ref,
    m_low_ref,
    m_gb_ref,
    m_ga_ref,
    m_mixed_ref,
    m_hidden_ref,
    m_gpre_ref,
):
    step = pl.program_id(0)
    last = pl.num_programs(0) - 1
    length, width = tok_ref.shape[1:]
    hid = upb_ref.shape[1]
    rows = length + PAD
    up = slice(0, hid)
    down = slice(hid, 2 * hid)
    outw = slice(2 * hid, 2 * hid + width)

    @pl.when(step == 0)
    def _():
        acc_ref[...] = jnp.zeros_like(acc_ref)
        sums_ref[...] = jnp.zeros_like(sums_ref)
        upb_sum_ref[...] = jnp.zeros_like(upb_sum_ref)

    att_ref[...] = dot(mixed_ref[0], wide_ref[:, outw], 1, 1)
    att_ref[:length] += tok_ref[0].astype(FL)
    att_ref[length:] += state_ref[0].astype(FL) + memb_ref[...]
    bias_att, bias_ffn = vec_ref[2:3, :], vec_ref[3:4, :]
    gain_one, shift_one, gain_two, shift_two = (vec_ref[i : i + 1, :] for i in range(4, 8))

    def norm_one(i, carry):
        r = pl.ds(pl.multiple_of(i * ROWS, ROWS), ROWS)
        normed, rstd = norm_rows(att_ref[r, :] + bias_att)
        n1_ref[r, :] = normed
        r1_ref[r, :] = rstd
        low_ref[r, :] = (normed * gain_one + shift_one).astype(BF)
        return carry

    lax.fori_loop(0, rows // ROWS, norm_one, 0, unroll=True)

    root = 0.7978845608
    for j in range(0, hid, FCHUNK):
        c = slice(j, j + FCHUNK)
        v = dot(low_ref[...], wide_ref[:, c], 1, 0) + upb_ref[:, c]
        square = v * v
        half = 0.5 + 0.5 * jnp.tanh(v * (root + (root * 0.044715) * square))
        act = v * half
        hidden_ref[:, c] = act.astype(BF)
        slope_ref[:, c] = half + (act * (1.0 - half)) * (2 * root + (6 * root * 0.044715) * square)

    att_ref[...] = dot(hidden_ref[...], wide_ref[:, down], 1, 1)

    def norm_two(i, carry):
        r = pl.ds(pl.multiple_of(i * ROWS, ROWS), ROWS)
        first = n1_ref[r, :] * gain_one + shift_one
        normed, rstd = norm_rows(first + (att_ref[r, :] + bias_ffn))
        out_ref[0, r, :] = (normed * gain_two + shift_two).astype(BF)
        cot = cot_ref[0, r, :].astype(FL)
        sums_ref[48:56] += by_eight(cot * normed)
        sums_ref[56:64] += by_eight(cot)
        back = norm_back(cot, normed, rstd, gain_two)
        g2_ref[r, :] = back
        low = back.astype(BF)
        gb_ref[r, :] = low
        sums_ref[24:32] += by_eight(low.astype(FL))
        return carry

    lax.fori_loop(0, rows // ROWS, norm_two, 0, unroll=True)

    for j in range(0, hid, FCHUNK):
        c = slice(j, j + FCHUNK)
        d = slice(hid + j, hid + j + FCHUNK)
        gpre = (dot(gb_ref[...], wide_ref[:, d], 1, 0) * slope_ref[:, c]).astype(BF)
        gpre_ref[:, c] = gpre
        upb_sum_ref[:, c] += by_eight(gpre.astype(FL))
        acc_ref[:, d] += dot(gb_ref[:length], hidden_ref[:length, c], 0, 0)
        acc_ref[:, c] += dot(low_ref[:length], gpre_ref[:length, c], 0, 0)

    att_ref[...] = dot(gpre_ref[...], wide_ref[:, up], 1, 1)

    def norm_last(i, carry):
        r = pl.ds(pl.multiple_of(i * ROWS, ROWS), ROWS)
        g1 = g2_ref[r, :] + att_ref[r, :]
        normed = n1_ref[r, :]
        sums_ref[32:40] += by_eight(g1 * normed)
        sums_ref[40:48] += by_eight(g1)
        back = norm_back(g1, normed, r1_ref[r, :], gain_one)
        one_ref[0, r, :] = back
        low = back.astype(BF)
        ga_ref[r, :] = low
        sums_ref[16:24] += by_eight(low.astype(FL))
        return carry

    lax.fori_loop(0, rows // ROWS, norm_last, 0, unroll=True)

    gm_ref[0] = dot(ga_ref[...], wide_ref[:, outw], 1, 0).astype(BF)
    acc_ref[:, outw] += dot(ga_ref[:length], mixed_ref[0, :length], 0, 0)

    mem = pl.ds(pl.multiple_of(step * PAD, PAD), PAD)
    m_low_ref[mem, :] = low_ref[length:, :]
    m_gb_ref[mem, :] = gb_ref[length:, :]
    m_ga_ref[mem, :] = ga_ref[length:, :]
    m_mixed_ref[mem, :] = mixed_ref[0, length:, :]
    m_hidden_ref[mem, :] = hidden_ref[length:, :]
    m_gpre_ref[mem, :] = gpre_ref[length:, :]

    @pl.when(step == last)
    def _():
        for j in range(0, hid, FCHUNK):
            c = slice(j, j + FCHUNK)
            d = slice(hid + j, hid + j + FCHUNK)
            gwide_ref[:, c] = (acc_ref[:, c] + dot(m_low_ref[...], m_gpre_ref[:, c], 0, 0)).astype(BF)
            gwide_ref[:, d] = (acc_ref[:, d] + dot(m_gb_ref[...], m_hidden_ref[:, c], 0, 0)).astype(BF)
        gwide_ref[:, outw] = (acc_ref[:, outw] + dot(m_ga_ref[...], m_mixed_ref[...], 0, 0)).astype(BF)
        for i in range(8):
            gvec_ref[i : i + 1, :] = jnp.sum(sums_ref[8 * i : 8 * i + 8], axis=0, keepdims=True)
        gupb_ref[...] = jnp.sum(upb_sum_ref[...], axis=0, keepdims=True)


def feed(tok, state, memb, vecs, upb, wide, mixed, cot):
    count, length, width = tok.shape
    rows = length + PAD
    hid = upb.shape[1]
    cols = wide.shape[1]
    one = lambda *dims: pl.BlockSpec((1,) + dims, lambda b: (b,) + (0,) * len(dims))
    whole = lambda *dims: pl.BlockSpec(dims, lambda b: (0,) * len(dims), pipeline_mode=pl.Buffered(1))
    final = lambda *dims: pl.BlockSpec(dims, lambda b: (0,) * len(dims))
    vm = pltpu.VMEM
    return pl.pallas_call(
        feed_kernel,
        grid=(count,),
        in_specs=[
            one(length, width),
            one(PAD, width),
            whole(PAD, width),
            whole(8, width),
            whole(1, hid),
            whole(width, cols),
            one(rows, width),
            one(rows, width),
        ],
        out_specs=[
            one(rows, width),
            one(rows, width),
            one(rows, width),
            final(width, cols),
            final(8, width),
            final(1, hid),
        ],
        out_shape=[
            jax.ShapeDtypeStruct((count, rows, width), BF),
            jax.ShapeDtypeStruct((count, rows, width), FL),
            jax.ShapeDtypeStruct((count, rows, width), BF),
            jax.ShapeDtypeStruct((width, cols), BF),
            jax.ShapeDtypeStruct((8, width), FL),
            jax.ShapeDtypeStruct((1, hid), FL),
        ],
        scratch_shapes=[
            vm((width, cols), FL),
            vm((64, width), FL),
            vm((8, hid), FL),
            vm((rows, width), FL),
            vm((rows, width), FL),
            vm((rows, 1), FL),
            vm((rows, width), BF),
            vm((rows, width), FL),
            vm((rows, width), BF),
            vm((rows, hid), BF),
            vm((rows, hid), FL),
            vm((rows, hid), BF),
            vm((rows, width), BF),
            vm((count * PAD, width), BF),
            vm((count * PAD, width), BF),
            vm((count * PAD, width), BF),
            vm((count * PAD, width), BF),
            vm((count * PAD, hid), BF),
            vm((count * PAD, hid), BF),
        ],
        compiler_params=pltpu.CompilerParams(vmem_limit_bytes=60 << 20),
        name="feed",
    )(tok, state, memb, vecs, upb, wide, mixed, cot)


def return_kernel(
    tok_ref,
    state_ref,
    memb_ref,
    inw_ref,
    qkv_ref,
    pt_ref,
    ptk_ref,
    ptq_ref,
    gm_ref,
    one_ref,
    grad_ref,
    gin_ref,
    acc_ref,
    sums_ref,
    kt_ref,
    dpk_ref,
    dsk_ref,
    dqt_ref,
    dk_ref,
    dv_ref,
    dj_ref,
    m_in_ref,
    m_dj_ref,
    side_ref,
):
    step = pl.program_id(0)
    last = pl.num_programs(0) - 1
    length, width = tok_ref.shape[1:]
    heads = width // HDIM

    @pl.when(step == 0)
    def _():
        acc_ref[...] = jnp.zeros_like(acc_ref)
        sums_ref[...] = jnp.zeros_like(sums_ref)
        side_ref[...] = jnp.zeros_like(side_ref)

    kt_ref[...] = qkv_ref[0, :length, width : 2 * width].T
    q_mem = spread(qkv_ref[0, length:, :width], heads)
    k_mem = spread(qkv_ref[0, length:, width : 2 * width], heads)
    v_mem = spread(qkv_ref[0, length:, 2 * width :], heads)
    do_mem = spread(gm_ref[0, length:, :], heads)

    dpk_ref[...] = dot(v_mem, gm_ref[0, :length, :], 1, 1)
    dpq = dot(qkv_ref[0, :, 2 * width :], do_mem, 1, 1)
    pq = ptq_ref[0].astype(FL)
    tq = pq * dpq
    dsq = (tq - pq * jnp.sum(tq, axis=0, keepdims=True)).astype(BF)
    dv_ref[...] = dot(ptq_ref[0], do_mem, 1, 0)
    dk_ref[...] = dot(dsq, q_mem, 1, 0)
    dj_ref[length:, :width] = (fold(dot(dsq, qkv_ref[0, :, width : 2 * width], 0, 0), heads) * SCALE).astype(BF)

    masks = pair_masks(2 * HDIM)

    def pair(p, carry):
        lanes = pl.ds(pl.multiple_of(p * 2 * HDIM, 2 * HDIM), 2 * HDIM)
        key_lanes = pl.ds(pl.multiple_of(width + p * 2 * HDIM, 2 * HDIM), 2 * HDIM)
        val_lanes = pl.ds(pl.multiple_of(2 * width + p * 2 * HDIM, 2 * HDIM), 2 * HDIM)
        vp = qkv_ref[0, :length, val_lanes]
        dop = gm_ref[0, :length, lanes]
        qp = qkv_ref[0, :length, lanes]
        for side in range(2):
            h = 2 * p + side
            own = pl.ds(pl.multiple_of(h * PAD, PAD), PAD)
            feat = pl.ds(pl.multiple_of(h * HDIM, HDIM), HDIM)
            vm = vp * masks[side]
            dom = dop * masks[side]
            qm = qp * masks[side]
            for part in range(length // HALF):
                cols = slice(part * HALF, (part + 1) * HALF)
                upto = (part + 1) * HALF
                base = part * (part + 1) // 2 * HALF
                block = slice(base, base + upto)
                dp = dot(vm[:upto], dop[cols], 1, 1)
                prob = pt_ref[0, h, block, :]
                pf = prob.astype(FL)
                t = pf * dp
                pm = ptk_ref[0, own, cols].astype(FL)
                tm = pm * dpk_ref[own, cols]
                delta = jnp.sum(t, axis=0, keepdims=True) + jnp.sum(tm, axis=0, keepdims=True)
                ds = (t - pf * delta).astype(BF)
                dsk_ref[own, cols] = (tm - pm * delta).astype(BF)
                dv_ref[:upto, lanes] += dot(prob, dom[cols], 1, 0)
                dk_ref[:upto, lanes] += dot(ds, qm[cols], 1, 0)
                dqt_ref[feat, cols] = dot(kt_ref[feat, :upto], ds, 1, 0)
        return carry

    lax.fori_loop(0, heads // 2, pair, 0)

    dq_t = dqt_ref[...] + dot(k_mem, dsk_ref[...], 0, 0)
    dj_ref[:length, :width] = (dq_t * SCALE).astype(BF).T
    dv_ref[length:, :] += fold(dot(ptk_ref[0], gm_ref[0, :length, :], 1, 0), heads)
    dk_ref[length:, :] += fold(dot(dsk_ref[...], qkv_ref[0, :length, :width], 1, 0), heads)
    dj_ref[:, width : 2 * width] = dk_ref[...].astype(BF)
    dj_ref[:, 2 * width :] = dv_ref[...].astype(BF)
    sums_ref[0:8] += by_eight(dj_ref[:, :width].astype(FL))
    sums_ref[8:16] += by_eight(dj_ref[:, 2 * width :].astype(FL))

    mem = pl.ds(pl.multiple_of(step * PAD, PAD), PAD)
    m_in_ref[mem, :] = (state_ref[0].astype(FL) + memb_ref[...]).astype(BF)
    m_dj_ref[mem, :] = dj_ref[length:, :]
    for j in range(3):
        c = slice(j * width, (j + 1) * width)
        acc_ref[:, c] += dot(tok_ref[0], dj_ref[:length, c], 0, 0)
    grad_ref[0] = one_ref[0, :length, :] + dot(dj_ref[:length, :], inw_ref[...], 1, 1)
    side_ref[0:PAD, :] += one_ref[0, length:, :] + dot(dj_ref[length:, :], inw_ref[...], 1, 1)

    @pl.when(step == last)
    def _():
        for j in range(3):
            c = slice(j * width, (j + 1) * width)
            gin_ref[:, c] = (acc_ref[:, c] + dot(m_in_ref[...], m_dj_ref[:, c], 0, 0)).astype(BF)
        side_ref[PAD : PAD + 1, :] = jnp.sum(sums_ref[0:8], axis=0, keepdims=True)
        side_ref[PAD + 1 : PAD + 2, :] = jnp.sum(sums_ref[8:16], axis=0, keepdims=True)
        gin_ref[:, 3 * width :] = side_ref[...].T.astype(BF)


def go_back(tok, state, memb, in_w, qkv, pt, ptk, ptq, gm, one_grad):
    count, length, width = tok.shape
    rows = length + PAD
    heads = width // HDIM
    one = lambda *dims: pl.BlockSpec((1,) + dims, lambda b: (b,) + (0,) * len(dims))
    whole = lambda *dims: pl.BlockSpec(dims, lambda b: (0,) * len(dims), pipeline_mode=pl.Buffered(1))
    final = lambda *dims: pl.BlockSpec(dims, lambda b: (0,) * len(dims))
    vm = pltpu.VMEM
    return pl.pallas_call(
        return_kernel,
        grid=(count,),
        in_specs=[
            one(length, width),
            one(PAD, width),
            whole(PAD, width),
            whole(width, 3 * width),
            one(rows, 3 * width),
            one(*pt.shape[1:]),
            one(heads * PAD, length),
            one(rows, heads * PAD),
            one(rows, width),
            one(rows, width),
        ],
        out_specs=[one(length, width), final(width, 3 * width + 128)],
        out_shape=[
            jax.ShapeDtypeStruct((count, length, width), FL),
            jax.ShapeDtypeStruct((width, 3 * width + 128), BF),
        ],
        scratch_shapes=[
            vm((width, 3 * width), FL),
            vm((16, width), FL),
            vm((width, length), BF),
            vm((heads * PAD, length), FL),
            vm((heads * PAD, length), BF),
            vm((width, length), FL),
            vm((rows, width), FL),
            vm((rows, width), FL),
            vm((rows, 3 * width), BF),
            vm((count * PAD, width), BF),
            vm((count * PAD, 3 * width), BF),
            vm((128, width), FL),
        ],
        compiler_params=pltpu.CompilerParams(vmem_limit_bytes=60 << 20),
        name="go_back",
    )(tok, state, memb, in_w, qkv, pt, ptk, ptq, gm, one_grad)


def gather(x, devices, index):
    rows, cols = x.shape
    held = x[None]
    bit = devices // 2
    while bit:
        got = lax.ppermute(held, AXES, [(i, i ^ bit) for i in range(devices)])
        upper = (index & bit) != 0
        held = jnp.stack([jnp.where(upper, got, held), jnp.where(upper, held, got)], axis=1)
        held = held.reshape(-1, rows, cols)
        bit //= 2
    return held.reshape(devices * rows, cols)


def scatter_sum(x, devices, index):
    total, cols = x.shape
    rows = total // devices
    held = x
    bit = 1
    while bit < devices:
        held = held.reshape(-1, 2, rows, cols)
        upper = (index & bit) != 0
        keep = jnp.where(upper, held[:, 1], held[:, 0]).astype(FL)
        send = jnp.where(upper, held[:, 0], held[:, 1]).astype(BF)
        held = keep + lax.ppermute(send, AXES, [(i, i ^ bit) for i in range(devices)]).astype(FL)
        bit *= 2
    return held.reshape(rows, cols)


def butterfly(x, devices):
    bit = 1
    while bit < devices:
        x = x + lax.ppermute(x, AXES, [(i, i ^ bit) for i in range(devices)])
        bit *= 2
    return x


def adam_step(weight, first, second, grad, rate, decay):
    first_new = 0.5 * first + 0.5 * grad
    second_new = 0.5 * second + 0.5 * grad * grad
    correction = 1.0 - 0.5**STEP
    weight_new = weight - rate * (
        first_new / correction / (jnp.sqrt(second_new / correction) + 1e-08) + decay * weight
    )
    return (weight_new, first_new, second_new)


def per_device(
    devices,
    tokens,
    memory_state,
    cotangent,
    in_weight,
    in_first,
    in_second,
    out_weight,
    out_first,
    out_second,
    up_weight,
    up_first,
    up_second,
    down_weight,
    down_first,
    down_second,
    vectors,
    vectors_first,
    vectors_second,
    up_bias,
    up_bias_first,
    up_bias_second,
    memory_embed,
    memory_first,
    memory_second,
):
    index = lax.axis_index(AXES)
    micro, local, length, width = tokens.shape
    count = micro * local
    extra = memory_state.shape[2]
    shard = in_weight.shape[0]
    hid = up_weight.shape[1]
    per_bias = up_bias.shape[0] // shard

    small = jnp.concatenate(
        [
            memory_embed.T,
            jnp.zeros((shard, PAD - extra), FL),
            vectors.T,
            up_bias.reshape(per_bias, shard).T,
            jnp.zeros((shard, 128 - PAD - 8 - per_bias), FL),
        ],
        axis=1,
    )
    near = jnp.concatenate([in_weight, small], axis=1).astype(BF)
    far = jnp.concatenate([up_weight, down_weight.T, out_weight.T], axis=1).astype(BF)
    near = gather(near, devices, index)
    wide = gather(far, devices, index)
    side = near[:, 3 * width :].astype(FL).T
    memb = side[:PAD]
    vecs = side[PAD : PAD + 8]
    upb = side[PAD + 8 : PAD + 8 + per_bias].reshape(per_bias, devices, shard)
    upb = upb.transpose(1, 0, 2).reshape(1, hid)
    in_w = near[:, : 3 * width]

    tok = tokens.reshape(count, length, width)
    state = jnp.pad(memory_state.reshape(count, extra, width), ((0, 0), (0, PAD - extra), (0, 0)))
    cot = cotangent.reshape(count, extra + length, width)
    cot = jnp.concatenate(
        [cot[:, extra:], cot[:, :extra], jnp.zeros((count, PAD - extra, width), BF)], axis=1
    )

    qkv, pt, ptk, ptq, mixed = attend(extra, tok, state, memb, vecs, in_w)
    out, one_grad, gm, gwide, gvec, gupb = feed(tok, state, memb, vecs, upb, wide, mixed, cot)
    gupb = gupb.reshape(devices, per_bias, shard).transpose(1, 0, 2).reshape(per_bias, width)
    gside = jnp.concatenate(
        [jnp.zeros((PAD, width), FL), gvec, gupb, jnp.zeros((128 - PAD - 8 - per_bias, width), FL)]
    ).T.astype(BF)
    gfar = scatter_sum(jnp.concatenate([gwide, gside], axis=1), devices, index)
    input_grad, gnear = go_back(tok, state, memb, in_w, qkv, pt, ptk, ptq, gm, one_grad)
    gnear = scatter_sum(gnear, devices, index)

    output = jnp.concatenate([out[:, length : length + extra], out[:, :length]], axis=1)
    output = output.reshape(micro, local, extra + length, width)
    input_grad = input_grad.reshape(micro, local, length, width)

    gsmall = (gnear[:, 3 * width :] + gfar[:, 2 * hid + width :]).T
    grads = (
        gnear[:, : 3 * width],
        gfar[:, 2 * hid : 2 * hid + width],
        gfar[:, :hid],
        gfar[:, hid : 2 * hid],
        gsmall[PAD : PAD + 8],
        gsmall[PAD + 8 : PAD + 8 + per_bias].reshape(up_bias.shape),
        gsmall[:extra],
    )
    squares = sum(jnp.sum(grad * grad) for grad in grads)
    grad_norm = jnp.sqrt(butterfly(squares.reshape(1, 1), devices)[0, 0])
    factor = 1.0 / jnp.maximum(grad_norm, 1.0)
    total_rows = extra + length
    rates = (
        0.5 * width ** (-0.5),
        0.5 * (width * 32 // total_rows) ** (-0.5),
        0.5 * width ** (-0.5),
        0.5 * hid ** (-0.5),
        0.1,
        0.1,
        0.5,
    )
    decays = (0.1, 0.1, 0.1, 0.1, 0.0, 0.0, 0.0)
    states = (
        (in_weight, in_first, in_second),
        (out_weight.T, out_first.T, out_second.T),
        (up_weight, up_first, up_second),
        (down_weight.T, down_first.T, down_second.T),
        (vectors, vectors_first, vectors_second),
        (up_bias, up_bias_first, up_bias_second),
        (memory_embed, memory_first, memory_second),
    )
    results = []
    for i, (weight, first, second) in enumerate(states):
        new = adam_step(weight, first, second, grads[i] * factor, rates[i], decays[i])
        results.extend(value.T if i in (1, 3) else value for value in new)
    return (output, input_grad, *results, grad_norm)


def solution(mesh):
    blocks = P(None, AXES, None, None)
    lead = P(AXES, None)
    trail = P(None, AXES)
    flat = P(AXES)
    weights = (lead,) * 3 + (trail,) * 3 + (lead,) * 3 + (trail,) * 6 + (flat,) * 3 + (trail,) * 3
    devices = mesh.shape["dp"] * mesh.shape["fsdp"]
    return jax.shard_map(
        partial(per_device, devices),
        mesh=mesh,
        in_specs=(blocks,) * 3 + weights,
        out_specs=(blocks,) * 2 + weights + (P(),),
        check_vma=False,
    )
```

```python
from functools import partial

import jax
import jax.numpy as jnp
from jax import lax
from jax.experimental import pallas as pl
from jax.experimental.pallas import tpu as pltpu
from jax.sharding import PartitionSpec as P

STEP = 7
HDIM = 64
PAD = 32
HALF = 256
FCHUNK = 256
ROWS = 32
BF = jnp.bfloat16
FL = jnp.float32
AXES = ("dp", "fsdp")
NEG = -1e30
EPS = 1e-05
SCALE = HDIM ** (-0.5)
LANES = 128
BIAS = 64
BACK = (1, 3, 2, 1, 1)


def dot(a, b, ca, cb):
    return lax.dot_general(a, b, (((ca,), (cb,)), ((), ())), preferred_element_type=FL)


def head_mask(rows, width):
    row = lax.broadcasted_iota(jnp.int32, (rows, width), 0) // PAD
    col = lax.broadcasted_iota(jnp.int32, (rows, width), 1) // HDIM
    return row == col


def spread(x, heads):
    tiled = jnp.concatenate([x.astype(FL)] * heads, axis=0)
    return jnp.where(head_mask(*tiled.shape), tiled, 0.0).astype(BF)


def fold(y, heads):
    own = jnp.where(head_mask(*y.shape), y, 0.0)
    return sum(own[h * PAD : (h + 1) * PAD] for h in range(heads))


def pair_masks(width):
    col = lax.broadcasted_iota(jnp.int32, (1, width), 1)
    low = jnp.where(col < HDIM, 1.0, 0.0)
    return low.astype(BF), (1.0 - low).astype(BF)


def attend_kernel(
    extra,
    tok_ref,
    state_ref,
    inw_ref,
    qkv_ref,
    pt_ref,
    ptk_ref,
    ptq_ref,
    mixed_ref,
    vt_ref,
    sk_ref,
    ot_ref,
    side_ref,
):
    length, width = tok_ref.shape[1:]
    heads = width // HDIM
    rows = length + PAD

    @pl.when(pl.program_id(0) == 0)
    def _():
        side_ref[...] = inw_ref[:, 3 * width :].astype(FL).T

    memory = (state_ref[0].astype(FL) + side_ref[:PAD]).astype(BF)
    inputs = jnp.concatenate([tok_ref[0], memory], axis=0)
    qkv_ref[0, :, :width] = ((dot(inputs, inw_ref[:, :width], 1, 0) + side_ref[PAD : PAD + 1]) * SCALE).astype(BF)
    qkv_ref[0, :, width : 2 * width] = dot(inputs, inw_ref[:, width : 2 * width], 1, 0).astype(BF)
    qkv_ref[0, :, 2 * width :] = (dot(inputs, inw_ref[:, 2 * width : 3 * width], 1, 0) + side_ref[PAD + 1 : PAD + 2]).astype(BF)
    vt_ref[...] = qkv_ref[0, :length, 2 * width :].T

    key_place = lax.broadcasted_iota(jnp.int32, (heads * PAD, 1), 0) % PAD
    k_mem = spread(qkv_ref[0, length:, width : 2 * width], heads)
    sk_ref[...] = jnp.where(key_place < extra, dot(k_mem, qkv_ref[0, :length, :width], 1, 1), NEG)

    q_mem = spread(qkv_ref[0, length:, :width], heads)
    sq = dot(qkv_ref[0, :, width : 2 * width], q_mem, 1, 1)
    place = lax.broadcasted_iota(jnp.int32, (rows, 1), 0)
    sq = jnp.where(place < length + extra, sq, NEG)
    eq = jnp.exp(sq - jnp.max(sq, axis=0, keepdims=True))
    ptq_ref[0] = (eq * (1.0 / jnp.sum(eq, axis=0, keepdims=True))).astype(BF)
    om = dot(ptq_ref[0], qkv_ref[0, :, 2 * width :], 0, 0)
    mixed_ref[0, length:, :] = fold(om, heads).astype(BF)

    diag = lax.broadcasted_iota(jnp.int32, (HALF, HALF), 0) <= lax.broadcasted_iota(
        jnp.int32, (HALF, HALF), 1
    )
    masks = pair_masks(2 * HDIM)

    def pair(p, carry):
        lanes = pl.ds(pl.multiple_of(p * 2 * HDIM, 2 * HDIM), 2 * HDIM)
        key_lanes = pl.ds(pl.multiple_of(width + p * 2 * HDIM, 2 * HDIM), 2 * HDIM)
        kp = qkv_ref[0, :length, key_lanes]
        for side in range(2):
            h = 2 * p + side
            km = kp * masks[side]
            own = pl.ds(pl.multiple_of(h * PAD, PAD), PAD)
            feat = pl.ds(pl.multiple_of(h * HDIM, HDIM), HDIM)
            for part in range(length // HALF):
                cols = pl.ds(part * HALF, HALF)
                below = part * HALF
                upto = below + HALF
                qp = qkv_ref[0, cols, lanes]
                s_diag = jnp.where(diag, dot(km[below:upto], qp, 1, 1), NEG)
                s_mem = sk_ref[own, cols]
                top = jnp.maximum(
                    jnp.max(s_diag, axis=0, keepdims=True), jnp.max(s_mem, axis=0, keepdims=True)
                )
                if part:
                    s_low = dot(km[:below], qp, 1, 1)
                    top = jnp.maximum(top, jnp.max(s_low, axis=0, keepdims=True))
                e_diag = jnp.exp(s_diag - top)
                e_mem = jnp.exp(s_mem - top)
                total = jnp.sum(e_diag, axis=0, keepdims=True) + jnp.sum(e_mem, axis=0, keepdims=True)
                if part:
                    e_low = jnp.exp(s_low - top)
                    total = total + jnp.sum(e_low, axis=0, keepdims=True)
                share = 1.0 / total
                base = part * (part + 1) // 2 * HALF
                if part:
                    pt_ref[0, h, base : base + below, :] = (e_low * share).astype(BF)
                pt_ref[0, h, base + below : base + upto, :] = (e_diag * share).astype(BF)
                ptk_ref[0, own, cols] = (e_mem * share).astype(BF)
                ot_ref[feat, cols] = dot(vt_ref[feat, :upto], pt_ref[0, h, base : base + upto, :], 1, 0)
        return carry

    lax.fori_loop(0, heads // 2, pair, 0)
    v_mem = spread(qkv_ref[0, length:, 2 * width :], heads)
    om_t = ot_ref[...] + dot(v_mem, ptk_ref[0], 0, 0)
    mixed_ref[0, :length, :] = om_t.astype(BF).T


def attend(extra, tok, state, near):
    count, length, width = tok.shape
    heads = width // HDIM
    rows = length + PAD
    parts = length // HALF
    ptrows = parts * (parts + 1) // 2 * HALF
    one = lambda *dims: pl.BlockSpec((1,) + dims, lambda b: (b,) + (0,) * len(dims))
    whole = lambda *dims: pl.BlockSpec(dims, lambda b: (0,) * len(dims))
    return pl.pallas_call(
        partial(attend_kernel, extra),
        grid=(count,),
        in_specs=[
            one(length, width),
            one(PAD, width),
            whole(width, 3 * width + LANES),
        ],
        out_specs=[
            one(rows, 3 * width),
            one(heads, ptrows, HALF),
            one(heads * PAD, length),
            one(rows, heads * PAD),
            one(rows, width),
        ],
        out_shape=[
            jax.ShapeDtypeStruct((count, rows, 3 * width), BF),
            jax.ShapeDtypeStruct((count, heads, ptrows, HALF), BF),
            jax.ShapeDtypeStruct((count, heads * PAD, length), BF),
            jax.ShapeDtypeStruct((count, rows, heads * PAD), BF),
            jax.ShapeDtypeStruct((count, rows, width), BF),
        ],
        scratch_shapes=[
            pltpu.VMEM((width, length), BF),
            pltpu.VMEM((heads * PAD, length), FL),
            pltpu.VMEM((width, length), FL),
            pltpu.VMEM((LANES, width), FL),
        ],
        compiler_params=pltpu.CompilerParams(vmem_limit_bytes=56 << 20),
        name="attend",
    )(tok, state, near)


def norm_rows(x):
    center = x - jnp.mean(x, axis=-1, keepdims=True)
    rstd = lax.rsqrt(jnp.mean(center * center, axis=-1, keepdims=True) + EPS)
    return center * rstd, rstd


def norm_back(grad, normed, rstd, gain):
    scaled = grad * gain
    return rstd * (
        scaled
        - jnp.mean(scaled, axis=-1, keepdims=True)
        - normed * jnp.mean(scaled * normed, axis=-1, keepdims=True)
    )


def by_eight(x):
    return jnp.sum(x.reshape(x.shape[0] // 8, 8, x.shape[1]), axis=0)


def feed_kernel(
    devices,
    tok_ref,
    state_ref,
    small_ref,
    upb_ref,
    wide_ref,
    mixed_ref,
    cot_ref,
    out_ref,
    one_ref,
    gm_ref,
    gwide_ref,
    side_ref,
    gside_ref,
    acc_ref,
    sums_ref,
    upb_sum_ref,
    att_ref,
    n1_ref,
    r1_ref,
    low_ref,
    g2_ref,
    gb_ref,
    hidden_ref,
    slope_ref,
    gpre_ref,
    ga_ref,
    m_low_ref,
    m_gb_ref,
    m_ga_ref,
    m_mixed_ref,
    m_hidden_ref,
    m_gpre_ref,
):
    step = pl.program_id(0)
    last = pl.num_programs(0) - 1
    length, width = tok_ref.shape[1:]
    hid = upb_ref.shape[1]
    rows = length + PAD
    shard, per = width // devices, hid // devices
    up = slice(0, hid)
    down = slice(hid, 2 * hid)
    outw = slice(2 * hid, 2 * hid + width)

    @pl.when(step == 0)
    def _():
        acc_ref[...] = jnp.zeros_like(acc_ref)
        sums_ref[...] = jnp.zeros_like(sums_ref)
        upb_sum_ref[...] = jnp.zeros_like(upb_sum_ref)
        side_ref[...] = small_ref[...].astype(FL).T

    att_ref[...] = dot(mixed_ref[0], wide_ref[:, outw], 1, 1)
    att_ref[:length] += tok_ref[0].astype(FL)
    att_ref[length:] += state_ref[0].astype(FL) + side_ref[:PAD]
    bias_att, bias_ffn = side_ref[PAD + 2 : PAD + 3], side_ref[PAD + 3 : PAD + 4]
    gain_one, shift_one, gain_two, shift_two = (side_ref[PAD + i : PAD + i + 1] for i in range(4, 8))

    def norm_one(i, carry):
        r = pl.ds(pl.multiple_of(i * ROWS, ROWS), ROWS)
        normed, rstd = norm_rows(att_ref[r, :] + bias_att)
        n1_ref[r, :] = normed
        r1_ref[r, :] = rstd
        low_ref[r, :] = (normed * gain_one + shift_one).astype(BF)
        return carry

    lax.fori_loop(0, rows // ROWS, norm_one, 0, unroll=True)

    root = 0.7978845608
    for j in range(0, hid, FCHUNK):
        c = slice(j, j + FCHUNK)
        v = dot(low_ref[...], wide_ref[:, c], 1, 0) + upb_ref[:, c]
        square = v * v
        half = 0.5 + 0.5 * jnp.tanh(v * (root + (root * 0.044715) * square))
        act = v * half
        hidden_ref[:, c] = act.astype(BF)
        slope_ref[:, c] = half + (act * (1.0 - half)) * (2 * root + (6 * root * 0.044715) * square)

    att_ref[...] = dot(hidden_ref[...], wide_ref[:, down], 1, 1)

    def norm_two(i, carry):
        r = pl.ds(pl.multiple_of(i * ROWS, ROWS), ROWS)
        first = n1_ref[r, :] * gain_one + shift_one
        normed, rstd = norm_rows(first + (att_ref[r, :] + bias_ffn))
        out_ref[0, r, :] = (normed * gain_two + shift_two).astype(BF)
        cot = cot_ref[0, r, :].astype(FL)
        sums_ref[48:56] += by_eight(cot * normed)
        sums_ref[56:64] += by_eight(cot)
        back = norm_back(cot, normed, rstd, gain_two)
        g2_ref[r, :] = back
        low = back.astype(BF)
        gb_ref[r, :] = low
        sums_ref[24:32] += by_eight(low.astype(FL))
        return carry

    lax.fori_loop(0, rows // ROWS, norm_two, 0, unroll=True)

    for j in range(0, hid, FCHUNK):
        c = slice(j, j + FCHUNK)
        d = slice(hid + j, hid + j + FCHUNK)
        gpre = (dot(gb_ref[...], wide_ref[:, d], 1, 0) * slope_ref[:, c]).astype(BF)
        gpre_ref[:, c] = gpre
        upb_sum_ref[:, c] += by_eight(gpre.astype(FL))
        acc_ref[:, d] += dot(gb_ref[:length], hidden_ref[:length, c], 0, 0)
        acc_ref[:, c] += dot(low_ref[:length], gpre_ref[:length, c], 0, 0)

    att_ref[...] = dot(gpre_ref[...], wide_ref[:, up], 1, 1)

    def norm_last(i, carry):
        r = pl.ds(pl.multiple_of(i * ROWS, ROWS), ROWS)
        g1 = g2_ref[r, :] + att_ref[r, :]
        normed = n1_ref[r, :]
        sums_ref[32:40] += by_eight(g1 * normed)
        sums_ref[40:48] += by_eight(g1)
        back = norm_back(g1, normed, r1_ref[r, :], gain_one)
        one_ref[0, r, :] = back
        low = back.astype(BF)
        ga_ref[r, :] = low
        sums_ref[16:24] += by_eight(low.astype(FL))
        return carry

    lax.fori_loop(0, rows // ROWS, norm_last, 0, unroll=True)

    gm_ref[0] = dot(ga_ref[...], wide_ref[:, outw], 1, 0).astype(BF)
    acc_ref[:, outw] += dot(ga_ref[:length], mixed_ref[0, :length], 0, 0)

    mem = pl.ds(pl.multiple_of(step * PAD, PAD), PAD)
    m_low_ref[mem, :] = low_ref[length:, :]
    m_gb_ref[mem, :] = gb_ref[length:, :]
    m_ga_ref[mem, :] = ga_ref[length:, :]
    m_mixed_ref[mem, :] = mixed_ref[0, length:, :]
    m_hidden_ref[mem, :] = hidden_ref[length:, :]
    m_gpre_ref[mem, :] = gpre_ref[length:, :]

    @pl.when(step == last)
    def _():
        for j in range(0, hid, FCHUNK):
            c = slice(j, j + FCHUNK)
            d = slice(hid + j, hid + j + FCHUNK)
            gwide_ref[:, c] = (acc_ref[:, c] + dot(m_low_ref[...], m_gpre_ref[:, c], 0, 0)).astype(BF)
            gwide_ref[:, d] = (acc_ref[:, d] + dot(m_gb_ref[...], m_hidden_ref[:, c], 0, 0)).astype(BF)
        gwide_ref[:, outw] = (acc_ref[:, outw] + dot(m_ga_ref[...], m_mixed_ref[...], 0, 0)).astype(BF)
        side_ref[...] = jnp.zeros_like(side_ref)
        for i in range(8):
            side_ref[PAD + i : PAD + i + 1] = jnp.sum(sums_ref[8 * i : 8 * i + 8], axis=0, keepdims=True)
        gside_ref[...] = side_ref[...].T
        bias = jnp.sum(upb_sum_ref[...], axis=0, keepdims=True)
        for i in range(devices):
            piece = bias[:, i * per : (i + 1) * per]
            gside_ref[i * shard : i * shard + 1, BIAS : BIAS + per] = piece
        gwide_ref[:, 2 * hid + width :] = gside_ref[...].astype(BF)


def feed(devices, tok, state, small, upb, wide, mixed, cot):
    count, length, width = tok.shape
    rows = length + PAD
    hid = upb.shape[1]
    cols = wide.shape[1]
    one = lambda *dims: pl.BlockSpec((1,) + dims, lambda b: (b,) + (0,) * len(dims))
    whole = lambda *dims: pl.BlockSpec(dims, lambda b: (0,) * len(dims), pipeline_mode=pl.Buffered(1))
    final = lambda *dims: pl.BlockSpec(dims, lambda b: (0,) * len(dims))
    vm = pltpu.VMEM
    return pl.pallas_call(
        partial(feed_kernel, devices),
        grid=(count,),
        in_specs=[
            one(length, width),
            one(PAD, width),
            whole(width, LANES),
            whole(1, hid),
            whole(width, cols),
            one(rows, width),
            one(rows, width),
        ],
        out_specs=[
            one(rows, width),
            one(rows, width),
            one(rows, width),
            final(width, cols + LANES),
        ],
        out_shape=[
            jax.ShapeDtypeStruct((count, rows, width), BF),
            jax.ShapeDtypeStruct((count, rows, width), FL),
            jax.ShapeDtypeStruct((count, rows, width), BF),
            jax.ShapeDtypeStruct((width, cols + LANES), BF),
        ],
        scratch_shapes=[
            vm((LANES, width), FL),
            vm((width, LANES), FL),
            vm((width, cols), FL),
            vm((64, width), FL),
            vm((8, hid), FL),
            vm((rows, width), FL),
            vm((rows, width), FL),
            vm((rows, 1), FL),
            vm((rows, width), BF),
            vm((rows, width), FL),
            vm((rows, width), BF),
            vm((rows, hid), BF),
            vm((rows, hid), FL),
            vm((rows, hid), BF),
            vm((rows, width), BF),
            vm((count * PAD, width), BF),
            vm((count * PAD, width), BF),
            vm((count * PAD, width), BF),
            vm((count * PAD, width), BF),
            vm((count * PAD, hid), BF),
            vm((count * PAD, hid), BF),
        ],
        compiler_params=pltpu.CompilerParams(vmem_limit_bytes=60 << 20),
        name="feed",
    )(tok, state, small, upb, wide, mixed, cot)


def return_kernel(
    qkv_ref,
    pt_ref,
    ptk_ref,
    ptq_ref,
    gm_ref,
    dj_ref,
    kt_ref,
    dpk_ref,
    dsk_ref,
    dqt_ref,
    dk_ref,
    dv_ref,
):
    width = gm_ref.shape[2]
    length = gm_ref.shape[1] - PAD
    heads = width // HDIM

    kt_ref[...] = qkv_ref[0, :length, width : 2 * width].T
    q_mem = spread(qkv_ref[0, length:, :width], heads)
    k_mem = spread(qkv_ref[0, length:, width : 2 * width], heads)
    v_mem = spread(qkv_ref[0, length:, 2 * width :], heads)
    do_mem = spread(gm_ref[0, length:, :], heads)

    dpk_ref[...] = dot(v_mem, gm_ref[0, :length, :], 1, 1)
    dpq = dot(qkv_ref[0, :, 2 * width :], do_mem, 1, 1)
    pq = ptq_ref[0].astype(FL)
    tq = pq * dpq
    dsq = (tq - pq * jnp.sum(tq, axis=0, keepdims=True)).astype(BF)
    dv_ref[...] = dot(ptq_ref[0], do_mem, 1, 0)
    dk_ref[...] = dot(dsq, q_mem, 1, 0)
    dq_mem = fold(dot(dsq, qkv_ref[0, :, width : 2 * width], 0, 0), heads)
    dj_ref[0, length:, :width] = (dq_mem * SCALE).astype(BF)

    masks = pair_masks(2 * HDIM)

    def pair(p, carry):
        lanes = pl.ds(pl.multiple_of(p * 2 * HDIM, 2 * HDIM), 2 * HDIM)
        val_lanes = pl.ds(pl.multiple_of(2 * width + p * 2 * HDIM, 2 * HDIM), 2 * HDIM)
        vp = qkv_ref[0, :length, val_lanes]
        dop = gm_ref[0, :length, lanes]
        qp = qkv_ref[0, :length, lanes]
        for side in range(2):
            h = 2 * p + side
            own = pl.ds(pl.multiple_of(h * PAD, PAD), PAD)
            feat = pl.ds(pl.multiple_of(h * HDIM, HDIM), HDIM)
            vm = vp * masks[side]
            dom = dop * masks[side]
            qm = qp * masks[side]
            for part in range(length // HALF):
                cols = slice(part * HALF, (part + 1) * HALF)
                upto = (part + 1) * HALF
                base = part * (part + 1) // 2 * HALF
                block = slice(base, base + upto)
                dp = dot(vm[:upto], dop[cols], 1, 1)
                prob = pt_ref[0, h, block, :]
                pf = prob.astype(FL)
                t = pf * dp
                pm = ptk_ref[0, own, cols].astype(FL)
                tm = pm * dpk_ref[own, cols]
                delta = jnp.sum(t, axis=0, keepdims=True) + jnp.sum(tm, axis=0, keepdims=True)
                ds = (t - pf * delta).astype(BF)
                dsk_ref[own, cols] = (tm - pm * delta).astype(BF)
                dv_ref[:upto, lanes] += dot(prob, dom[cols], 1, 0)
                dk_ref[:upto, lanes] += dot(ds, qm[cols], 1, 0)
                dqt_ref[feat, cols] = dot(kt_ref[feat, :upto], ds, 1, 0)
        return carry

    lax.fori_loop(0, heads // 2, pair, 0)

    dq_t = dqt_ref[...] + dot(k_mem, dsk_ref[...], 0, 0)
    dj_ref[0, :length, :width] = (dq_t * SCALE).astype(BF).T
    dv_ref[length:, :] += fold(dot(ptk_ref[0], gm_ref[0, :length, :], 1, 0), heads)
    dk_ref[length:, :] += fold(dot(dsk_ref[...], qkv_ref[0, :length, :width], 1, 0), heads)
    dj_ref[0, :, width : 2 * width] = dk_ref[...].astype(BF)
    dj_ref[0, :, 2 * width :] = dv_ref[...].astype(BF)


def go_back(begin, count, qkv, pt, ptk, ptq, gm):
    rows, width = gm.shape[1:]
    length = rows - PAD
    heads = width // HDIM
    one = lambda *dims: pl.BlockSpec((1,) + dims, lambda b: (b + begin,) + (0,) * len(dims))
    vm = pltpu.VMEM
    return pl.pallas_call(
        return_kernel,
        grid=(count,),
        in_specs=[
            one(rows, 3 * width),
            one(*pt.shape[1:]),
            one(heads * PAD, length),
            one(rows, heads * PAD),
            one(rows, width),
        ],
        out_specs=pl.BlockSpec((1, rows, 3 * width), lambda b: (b, 0, 0)),
        out_shape=jax.ShapeDtypeStruct((count, rows, 3 * width), BF),
        scratch_shapes=[
            vm((width, length), BF),
            vm((heads * PAD, length), FL),
            vm((heads * PAD, length), BF),
            vm((width, length), FL),
            vm((rows, width), FL),
            vm((rows, width), FL),
        ],
        compiler_params=pltpu.CompilerParams(vmem_limit_bytes=48 << 20),
        cost_estimate=pl.CostEstimate(flops=count * 10**10, bytes_accessed=count * 10**7, transcendentals=0),
        name="go_back",
    )(qkv, pt, ptk, ptq, gm)


def weigh_kernel(
    begins,
    tok_ref,
    state_ref,
    one_ref,
    inw_ref,
    *refs,
):
    dj_refs, refs = refs[: len(begins)], refs[len(begins) :]
    gin_ref, acc_ref, sums_ref, m_in_ref, m_dj_ref, side_ref, memb_ref = refs
    step = pl.program_id(0)
    last = pl.num_programs(0) - 1
    length, width = tok_ref.shape[1:]
    ends = begins[1:] + [last + 1]

    @pl.when(step == 0)
    def _():
        acc_ref[...] = jnp.zeros_like(acc_ref)
        sums_ref[...] = jnp.zeros_like(sums_ref)
        side_ref[...] = jnp.zeros_like(side_ref)
        memb_ref[...] = inw_ref[:, 3 * width :].astype(FL).T

    mem = pl.ds(pl.multiple_of(step * PAD, PAD), PAD)
    m_in_ref[mem, :] = (state_ref[0].astype(FL) + memb_ref[:PAD]).astype(BF)
    side_ref[0:PAD, :] += one_ref[0]
    for g, dj_ref in enumerate(dj_refs):

        @pl.when((step >= begins[g]) & (step < ends[g]))
        def _(dj_ref=dj_ref):
            m_dj_ref[mem, :] = dj_ref[0, length:, :]
            sums_ref[0:8] += by_eight(dj_ref[0, :, :width].astype(FL))
            sums_ref[8:16] += by_eight(dj_ref[0, :, 2 * width :].astype(FL))
            for j in range(3):
                c = slice(j * width, (j + 1) * width)
                acc_ref[:, c] += dot(tok_ref[0], dj_ref[0, :length, c], 0, 0)

    @pl.when(step == last)
    def _():
        for j in range(3):
            c = slice(j * width, (j + 1) * width)
            gin_ref[:, c] = (acc_ref[:, c] + dot(m_in_ref[...], m_dj_ref[:, c], 0, 0)).astype(BF)
        back = dot(m_dj_ref[...], inw_ref[:, : 3 * width], 1, 1)
        side_ref[0:PAD, :] += jnp.sum(back.reshape(last + 1, PAD, width), axis=0)
        side_ref[PAD : PAD + 1, :] = jnp.sum(sums_ref[0:8], axis=0, keepdims=True)
        side_ref[PAD + 1 : PAD + 2, :] = jnp.sum(sums_ref[8:16], axis=0, keepdims=True)
        gin_ref[:, 3 * width :] = side_ref[...].T.astype(BF)


def weigh(tok, state, near, one_grad, djs, begins):
    count, length, width = tok.shape
    rows = length + PAD
    one = lambda *dims: pl.BlockSpec((1,) + dims, lambda b: (b,) + (0,) * len(dims))
    whole = lambda *dims: pl.BlockSpec(dims, lambda b: (0,) * len(dims), pipeline_mode=pl.Buffered(1))
    final = lambda *dims: pl.BlockSpec(dims, lambda b: (0,) * len(dims))
    part = lambda g: pl.BlockSpec(
        (1, rows, 3 * width), lambda b: (jnp.clip(b - begins[g], 0, djs[g].shape[0] - 1), 0, 0)
    )
    vm = pltpu.VMEM
    return pl.pallas_call(
        partial(weigh_kernel, begins),
        grid=(count,),
        in_specs=[
            one(length, width),
            one(PAD, width),
            pl.BlockSpec((1, PAD, width), lambda b: (b, length // PAD, 0)),
            whole(width, 3 * width + LANES),
        ]
        + [part(g) for g in range(len(djs))],
        out_specs=final(width, 3 * width + LANES),
        out_shape=jax.ShapeDtypeStruct((width, 3 * width + LANES), BF),
        scratch_shapes=[
            vm((width, 3 * width), FL),
            vm((16, width), FL),
            vm((count * PAD, width), BF),
            vm((count * PAD, 3 * width), BF),
            vm((LANES, width), FL),
            vm((LANES, width), FL),
        ],
        compiler_params=pltpu.CompilerParams(vmem_limit_bytes=48 << 20),
        cost_estimate=pl.CostEstimate(flops=count * 10**9, bytes_accessed=count * 3 * 10**6, transcendentals=0),
        name="weigh",
    )(tok, state, one_grad, near, *djs)


def descend_kernel(one_ref, dj_ref, inw_ref, grad_ref):
    width = one_ref.shape[2]
    grad_ref[0] = one_ref[0] + dot(dj_ref[0], inw_ref[:, : 3 * width], 1, 1)


def descend(total, begin, one_grad, dj, near, into):
    count, rows, wide = dj.shape
    width = one_grad.shape[2]
    length = rows - PAD
    shift = lambda *dims: pl.BlockSpec((1,) + dims, lambda b: (b + begin, 0, 0))
    kept = () if into is None else (into,)

    def kernel(one_ref, dj_ref, inw_ref, *rest):
        descend_kernel(one_ref, dj_ref, inw_ref, rest[-1])

    return pl.pallas_call(
        kernel,
        grid=(count,),
        in_specs=[
            shift(length, width),
            pl.BlockSpec((1, length, wide), lambda b: (b, 0, 0)),
            pl.BlockSpec((width, wide + LANES), lambda b: (0, 0), pipeline_mode=pl.Buffered(1)),
        ]
        + [pl.BlockSpec(memory_space=pl.ANY)] * len(kept),
        out_specs=shift(length, width),
        out_shape=jax.ShapeDtypeStruct((total, length, width), FL),
        input_output_aliases={3: 0} if kept else {},
        compiler_params=pltpu.CompilerParams(vmem_limit_bytes=32 << 20),
        cost_estimate=pl.CostEstimate(flops=count * 10**9, bytes_accessed=count * 4 * 10**6, transcendentals=0),
        name="descend",
    )(one_grad, dj, near, *kept)


def pack_kernel(in_ref, up_ref, down_ref, out_ref, vec_ref, bias_ref, mem_ref, near_ref, far_ref, flip_ref):
    shard, cols = in_ref.shape
    hid, width = up_ref.shape[1], out_ref.shape[1]
    flip_ref[...] = jnp.zeros_like(flip_ref)
    flip_ref[PAD : PAD + 8, :shard] = vec_ref[...]
    flip_ref[...] = flip_ref[...].T
    flip_ref[:shard, : mem_ref.shape[1]] = mem_ref[...]
    flip_ref[0:1, BIAS : BIAS + bias_ref.shape[1]] = bias_ref[...]
    near_ref[:, :cols] = in_ref[...].astype(BF)
    near_ref[:, cols:] = flip_ref[:shard].astype(BF)
    far_ref[:, :hid] = up_ref[...].astype(BF)
    far_ref[:, hid : 2 * hid] = down_ref[...].astype(BF)
    far_ref[:, 2 * hid :] = out_ref[...].astype(BF)


def pack(in_w, up_w, down_t, out_t, vectors, bias, mem_t):
    shard, cols = in_w.shape
    wide = 2 * up_w.shape[1] + out_t.shape[1]
    return pl.pallas_call(
        pack_kernel,
        out_shape=[
            jax.ShapeDtypeStruct((shard, cols + LANES), BF),
            jax.ShapeDtypeStruct((shard, wide), BF),
        ],
        scratch_shapes=[pltpu.VMEM((LANES, LANES), FL)],
        name="pack",
    )(in_w, up_w, down_t, out_t, vectors, bias, mem_t)


def square_kernel(cols, near_ref, far_ref, sum_ref):
    wide = far_ref.shape[1] - LANES
    near, far = near_ref[:, :cols], far_ref[:, :wide]
    side = near_ref[:, cols:] + far_ref[:, wide:]
    total = jnp.sum(near * near) + jnp.sum(far * far) + jnp.sum(side * side)
    sum_ref[...] = jnp.full(sum_ref.shape, total, FL)


def adam_kernel(sizes, rates, decays, near_ref, far_ref, total_ref, *refs):
    cols, hid, width = sizes
    state_refs, new_refs, norm_ref, flip_ref = refs[:21], refs[21:42], refs[42], refs[43]
    shard = near_ref.shape[0]
    norm = jnp.sqrt(total_ref[...])
    norm_ref[...] = norm
    factor = (1.0 / jnp.maximum(norm, 1.0))[0:1, 0:1]
    side = near_ref[:, cols:] + far_ref[:, 2 * hid + width :]
    flip_ref[...] = jnp.zeros_like(flip_ref)
    flip_ref[:shard] = side
    turned = flip_ref[...].T
    bias = pltpu.roll(side, LANES - BIAS, 1)
    grads = (
        near_ref[:, :cols],
        far_ref[:, 2 * hid : 2 * hid + width],
        far_ref[:, :hid],
        far_ref[:, hid : 2 * hid],
        turned[PAD : PAD + 8, :shard],
        bias[0:1, : state_refs[15].shape[1]],
        side[:, : state_refs[18].shape[1]],
    )
    correction = 1.0 - 0.5**STEP
    for i in range(7):
        weight, first, second = (state_refs[3 * i + k][...] for k in range(3))
        grad = grads[i] * factor
        first_new = 0.5 * first + 0.5 * grad
        second_new = 0.5 * second + 0.5 * grad * grad
        step = first_new / correction / (jnp.sqrt(second_new / correction) + 1e-08)
        new_refs[3 * i][...] = weight - rates[i] * (step + decays[i] * weight)
        new_refs[3 * i + 1][...] = first_new
        new_refs[3 * i + 2][...] = second_new


def exchange(x, bit, devices):
    return lax.ppermute(x, AXES, [(i, i ^ bit) for i in range(devices)])


def beside(got, sent, work):
    if work is None:
        return got, None
    made = work(lambda value: lax.optimization_barrier((value, sent))[0])
    return lax.optimization_barrier((got, made))


def gather(x, devices, index, works):
    rows, cols = x.shape
    held = x[None]
    bit = devices // 2
    results = []
    while bit:
        got = exchange(held, bit, devices)
        got, made = beside(got, held, works.get(bit))
        results.append(made)
        upper = (index & bit) != 0
        held = jnp.stack([jnp.where(upper, got, held), jnp.where(upper, held, got)], axis=1)
        held = held.reshape(-1, rows, cols)
        bit //= 2
    return held.reshape(devices * rows, cols), [made for made in results if made is not None]


def halve(held, got, upper):
    total = held if got is None else held.astype(FL) + got.astype(FL)
    keep = jnp.where(upper, total[:, 1], total[:, 0])
    send = jnp.where(upper, total[:, 0], total[:, 1]).astype(BF)
    return keep, send


def scatter_sum(x, devices, index, works):
    total, cols = x.shape
    rows = total // devices
    held, got = x.reshape(-1, 2, rows, cols), None
    bit = 1
    results = []
    for step in range(devices.bit_length() - 1):
        keep, send = halve(held, got, (index & bit) != 0)
        got = exchange(send, bit, devices)
        got, made = beside(got, send, works[step] if step < len(works) else None)
        results.append(made)
        bit *= 2
        if bit < devices:
            held, got = keep.reshape(-1, 2, rows, cols), got.reshape(-1, 2, rows, cols)
    return (keep.astype(FL) + got.astype(FL)).reshape(rows, cols), results


def butterfly(x, devices):
    bit = 1
    while bit < devices:
        x = x + exchange(x, bit, devices)
        bit *= 2
    return x


def per_device(
    devices,
    tokens,
    memory_state,
    cotangent,
    in_weight,
    in_first,
    in_second,
    out_weight,
    out_first,
    out_second,
    up_weight,
    up_first,
    up_second,
    down_weight,
    down_first,
    down_second,
    vectors,
    vectors_first,
    vectors_second,
    up_bias,
    up_bias_first,
    up_bias_second,
    memory_embed,
    memory_first,
    memory_second,
):
    index = lax.axis_index(AXES)
    micro, local, length, width = tokens.shape
    count = micro * local
    extra = memory_state.shape[2]
    shard = in_weight.shape[0]
    hid = up_weight.shape[1]
    per_bias = up_bias.shape[0] // shard

    near, far = pack(
        in_weight,
        up_weight,
        down_weight.T,
        out_weight.T,
        vectors,
        up_bias.reshape(1, -1),
        memory_embed.T,
    )
    wide = lax.all_gather(far, AXES, axis=0, tiled=True)

    def align(tie):
        cot = tie(cotangent).reshape(count, extra + length, width)
        return jnp.concatenate(
            [cot[:, extra:], cot[:, :extra], jnp.zeros((count, PAD - extra, width), BF)], axis=1
        )

    near, (cot,) = gather(near, devices, index, {2: align})
    small = near[:, 3 * width :]
    upb = small.reshape(devices, shard, LANES)[:, 0, BIAS : BIAS + up_bias.shape[0]].astype(FL)
    upb = upb.reshape(1, hid)

    tok = tokens.reshape(count, length, width)
    state = jnp.pad(memory_state.reshape(count, extra, width), ((0, 0), (0, PAD - extra), (0, 0)))

    qkv, pt, ptk, ptq, mixed = attend(extra, tok, state, near)
    out, one_grad, gm, gwide = feed(devices, tok, state, small, upb, wide, mixed, cot)

    def split(sizes):
        begins = [0]
        for size in sizes:
            begins.append(begins[-1] + size)
        return list(zip(begins, sizes))

    def back(begin, size):
        return lambda tie: go_back(begin, size, tie(qkv), pt, ptk, ptq, gm)

    runs = split(BACK) if sum(BACK) == count else split([count])
    gfar, djs = scatter_sum(gwide, devices, index, [back(*run) for run in runs])
    djs = djs[: len(runs)]
    gin = weigh(tok, state, near, one_grad, djs, [begin for begin, _ in runs])
    grads = []

    def down(picked):
        def work(tie):
            for i in picked:
                into = grads[-1] if grads else None
                grads.append(descend(count, runs[i][0], one_grad, tie(djs[i]), near, into))
            return grads[-1]

        return work

    def order(tie):
        rows = tie(out)
        rows = jnp.concatenate([rows[:, length : length + extra], rows[:, :length]], axis=1)
        return rows.reshape(micro, local, extra + length, width).transpose(0, 2, 1, 3)

    cut = len(runs) // 2
    works = [down(range(cut)), down(range(cut, len(runs))), order]
    gnear, (_, input_grad, output, *_) = scatter_sum(gin, devices, index, works)
    output = output.transpose(0, 2, 1, 3)
    input_grad = input_grad.reshape(micro, local, length, width)

    squares = pl.pallas_call(
        partial(square_kernel, 3 * width),
        out_shape=jax.ShapeDtypeStruct((8, LANES), FL),
        name="squares",
    )(gnear, gfar)
    squares = butterfly(squares, devices)
    total_rows = extra + length
    rates = (
        0.5 * width ** (-0.5),
        0.5 * (width * 32 // total_rows) ** (-0.5),
        0.5 * width ** (-0.5),
        0.5 * hid ** (-0.5),
        0.1,
        0.1,
        0.5,
    )
    decays = (0.1, 0.1, 0.1, 0.1, 0.0, 0.0, 0.0)
    same = lambda value: value
    turn = lambda value: value.T
    flat = lambda value: value.reshape(1, -1)
    views = (same, turn, same, turn, same, flat, turn)
    states = (
        (in_weight, in_first, in_second),
        (out_weight, out_first, out_second),
        (up_weight, up_first, up_second),
        (down_weight, down_first, down_second),
        (vectors, vectors_first, vectors_second),
        (up_bias, up_bias_first, up_bias_second),
        (memory_embed, memory_first, memory_second),
    )
    held = [view(value) for view, group in zip(views, states) for value in group]
    *new, norm = pl.pallas_call(
        partial(adam_kernel, (3 * width, hid, width), rates, decays),
        out_shape=[jax.ShapeDtypeStruct(value.shape, FL) for value in held]
        + [jax.ShapeDtypeStruct((8, LANES), FL)],
        scratch_shapes=[pltpu.VMEM((LANES, LANES), FL)],
        name="adam",
    )(gnear, gfar, squares, *held)
    back_views = (same, turn, same, turn, same, lambda value: value.reshape(-1), turn)
    results = [back_views[i // 3](value) for i, value in enumerate(new)]
    return (output, input_grad, *results, norm[0, 0])


def solution(mesh):
    blocks = P(None, AXES, None, None)
    lead = P(AXES, None)
    trail = P(None, AXES)
    flat = P(AXES)
    weights = (lead,) * 3 + (trail,) * 3 + (lead,) * 3 + (trail,) * 6 + (flat,) * 3 + (trail,) * 3
    devices = mesh.shape["dp"] * mesh.shape["fsdp"]
    return jax.shard_map(
        partial(per_device, devices),
        mesh=mesh,
        in_specs=(blocks,) * 3 + weights,
        out_specs=(blocks,) * 2 + weights + (P(),),
        check_vma=False,
    )
```

```python
from functools import partial

import jax
import jax.numpy as jnp
from jax import lax
from jax.experimental import pallas as pl
from jax.experimental.pallas import tpu as pltpu
from jax.sharding import PartitionSpec as P

STEP = 7
HDIM = 64
PAD = 32
HALF = 256
FCHUNK = 256
ROWS = 32
BF = jnp.bfloat16
FL = jnp.float32
AXES = ("dp", "fsdp")
NEG = -1e30
EPS = 1e-05
SCALE = HDIM ** (-0.5)
LANES = 128
BIAS = 64
SLOTS = 4
CUT = 3
ONES = 16
BACK = (1, 3, 2, 2)


def dot(a, b, ca, cb):
    return lax.dot_general(a, b, (((ca,), (cb,)), ((), ())), preferred_element_type=FL)


def head_mask(rows, width):
    row = lax.broadcasted_iota(jnp.int32, (rows, width), 0) // PAD
    col = lax.broadcasted_iota(jnp.int32, (rows, width), 1) // HDIM
    return row == col


def spread(x, heads):
    tiled = jnp.concatenate([x.astype(FL)] * heads, axis=0)
    return jnp.where(head_mask(*tiled.shape), tiled, 0.0).astype(BF)


def fold(y, heads):
    own = jnp.where(head_mask(*y.shape), y, 0.0)
    return sum(own[h * PAD : (h + 1) * PAD] for h in range(heads))


def pair_masks(width):
    col = lax.broadcasted_iota(jnp.int32, (1, width), 1)
    low = jnp.where(col < HDIM, 1.0, 0.0)
    return low.astype(BF), (1.0 - low).astype(BF)


def attend_kernel(
    extra,
    tok_ref,
    state_ref,
    inw_ref,
    qkv_ref,
    pt_ref,
    ptk_ref,
    ptq_ref,
    mixed_ref,
    vt_ref,
    sk_ref,
    ot_ref,
    side_ref,
    inp_ref,
    s_ref,
):
    length, width = tok_ref.shape[1:]
    rows = length + PAD
    group = HALF // HDIM
    parts = length // HALF
    gpad = group * PAD

    @pl.when(pl.program_id(0) == 0)
    def _():
        side_ref[...] = inw_ref[:, 3 * width :].astype(FL).T

    inp_ref[:length] = tok_ref[0]
    inp_ref[length:] = (state_ref[0].astype(FL) + side_ref[:PAD]).astype(BF)
    diag = lax.broadcasted_iota(jnp.int32, (LANES, LANES), 0) <= lax.broadcasted_iota(
        jnp.int32, (LANES, LANES), 1
    )
    key_live = lax.broadcasted_iota(jnp.int32, (gpad, 1), 0) % PAD < extra
    place_live = lax.broadcasted_iota(jnp.int32, (rows, 1), 0) < length + extra
    masks = pair_masks(2 * HDIM)

    def project(g, which):
        at = which * width + g * HALF
        c = slice(at, at + HALF)
        made = dot(inp_ref[...], inw_ref[:, c], 1, 0)
        if which == 0:
            made = (made + side_ref[PAD : PAD + 1, g * HALF : (g + 1) * HALF]) * SCALE
        if which == 2:
            made = made + side_ref[PAD + 1 : PAD + 2, g * HALF : (g + 1) * HALF]
        qkv_ref[0, :, c] = made.astype(BF)
        if which == 2:
            vt_ref[g * HALF : (g + 1) * HALF, :] = qkv_ref[0, :length, c].T

    def columns(g, which):
        return slice(which * width + g * HALF, which * width + (g + 1) * HALF)

    def memory_keys(g):
        k_mem = spread(qkv_ref[0, length:, columns(g, 1)], group)
        made = dot(k_mem, qkv_ref[0, :length, columns(g, 0)], 1, 1)
        sk_ref[g * gpad : (g + 1) * gpad, :] = jnp.where(key_live, made, NEG)

    def memory_queries(g):
        q_mem = spread(qkv_ref[0, length:, columns(g, 0)], group)
        sq = jnp.where(place_live, dot(qkv_ref[0, :, columns(g, 1)], q_mem, 1, 1), NEG)
        eq = jnp.exp(sq - jnp.max(sq, axis=0, keepdims=True))
        probs = (eq * (1.0 / jnp.sum(eq, axis=0, keepdims=True))).astype(BF)
        ptq_ref[0, :, g * gpad : (g + 1) * gpad] = probs
        om = dot(probs, qkv_ref[0, :, columns(g, 2)], 0, 0)
        mixed_ref[0, length:, g * HALF : (g + 1) * HALF] = fold(om, group).astype(BF)

    def score(h, part, slot):
        at = (h // 2) * 2 * HDIM
        low, upto = part * HALF, (part + 1) * HALF
        qp = qkv_ref[0, low:upto, at : at + 2 * HDIM]
        km = qkv_ref[0, :upto, width + at : width + at + 2 * HDIM] * masks[h % 2]
        s = dot(km, qp, 1, 1)
        tops = []
        for c in range(0, HALF, LANES):
            lanes = slice(c, c + LANES)
            edge = jnp.where(diag, s[low + c : low + c + LANES, lanes], NEG)
            s_ref[slot, low + c : low + c + LANES, lanes] = edge
            top = jnp.maximum(
                jnp.max(edge, axis=0, keepdims=True),
                jnp.max(sk_ref[h * PAD : (h + 1) * PAD, low + c : low + c + LANES], axis=0, keepdims=True),
            )
            if low + c:
                s_ref[slot, : low + c, lanes] = s[: low + c, lanes]
                top = jnp.maximum(top, jnp.max(s[: low + c, lanes], axis=0, keepdims=True))
            tops.append(top)
        return tops

    def soften(h, part, slot, tops):
        low, upto = part * HALF, (part + 1) * HALF
        own = slice(h * PAD, (h + 1) * PAD)
        base = part * (part + 1) // 2 * HALF
        for c, top in zip(range(0, HALF, LANES), tops):
            lanes = slice(c, c + LANES)
            live = low + c + LANES
            cols = slice(low + c, live)
            e = jnp.exp(s_ref[slot, :live, lanes] - top)
            e_mem = jnp.exp(sk_ref[own, cols] - top)
            total = jnp.sum(e, axis=0, keepdims=True) + jnp.sum(e_mem, axis=0, keepdims=True)
            share = 1.0 / total
            pt_ref[0, h, base : base + live, lanes] = (e * share).astype(BF)
            if live < upto:
                pt_ref[0, h, base + live : base + upto, lanes] = jnp.zeros((upto - live, LANES), BF)
            ptk_ref[0, own, cols] = (e_mem * share).astype(BF)

    def mix(h, part):
        upto = (part + 1) * HALF
        base = part * (part + 1) // 2 * HALF
        feat = slice(h * HDIM, (h + 1) * HDIM)
        ot_ref[feat, part * HALF : upto] = dot(
            vt_ref[feat, :upto], pt_ref[0, h, base : base + upto, :], 1, 0
        )

    def finish(g):
        v_mem = spread(qkv_ref[0, length:, columns(g, 2)], group)
        feat = slice(g * HALF, (g + 1) * HALF)
        om_t = ot_ref[feat, :] + dot(v_mem, ptk_ref[0, g * gpad : (g + 1) * gpad, :], 0, 0)
        mixed_ref[0, :length, feat] = om_t.astype(BF).T

    groups = width // HALF
    units = [(g * group + i, part) for g in range(groups) for i in range(group) for part in range(parts)]
    per_group = group * parts
    for which in range(3):
        project(0, which)
    memory_keys(0)
    tops = {}
    for u in range(len(units) + 3):
        if u < len(units):
            g, at = u // per_group, u % per_group
            tops[u] = score(*units[u], u % SLOTS)
        if 2 <= u <= len(units) + 1:
            soften(*units[u - 2], (u - 2) % SLOTS, tops.pop(u - 2))
        if u >= 3:
            mix(*units[u - 3])
        if u < len(units):
            if g + 1 < groups and at in (2, 4, 6):
                project(g + 1, at // 2 - 1)
            if g + 1 < groups and at == 7:
                memory_keys(g + 1)
            if at == 1:
                memory_queries(g)
            if g and at == 3:
                finish(g - 1)
    finish(groups - 1)


def attend(extra, tok, state, near):
    count, length, width = tok.shape
    heads = width // HDIM
    rows = length + PAD
    parts = length // HALF
    ptrows = parts * (parts + 1) // 2 * HALF
    one = lambda *dims: pl.BlockSpec((1,) + dims, lambda b: (b,) + (0,) * len(dims))
    whole = lambda *dims: pl.BlockSpec(dims, lambda b: (0,) * len(dims))
    return pl.pallas_call(
        partial(attend_kernel, extra),
        grid=(count,),
        in_specs=[
            one(length, width),
            one(PAD, width),
            whole(width, 3 * width + LANES),
        ],
        out_specs=[
            one(rows, 3 * width),
            one(heads, ptrows, HALF),
            one(heads * PAD, length),
            one(rows, heads * PAD),
            one(rows, width),
        ],
        out_shape=[
            jax.ShapeDtypeStruct((count, rows, 3 * width), BF),
            jax.ShapeDtypeStruct((count, heads, ptrows, HALF), BF),
            jax.ShapeDtypeStruct((count, heads * PAD, length), BF),
            jax.ShapeDtypeStruct((count, rows, heads * PAD), BF),
            jax.ShapeDtypeStruct((count, rows, width), BF),
        ],
        scratch_shapes=[
            pltpu.VMEM((width, length), BF),
            pltpu.VMEM((heads * PAD, length), FL),
            pltpu.VMEM((width, length), FL),
            pltpu.VMEM((LANES, width), FL),
            pltpu.VMEM((rows, width), BF),
            pltpu.VMEM((SLOTS, length, HALF), FL),
        ],
        compiler_params=pltpu.CompilerParams(vmem_limit_bytes=56 << 20),
        name="attend",
    )(tok, state, near)


def norm_rows(x):
    center = x - jnp.mean(x, axis=-1, keepdims=True)
    rstd = lax.rsqrt(jnp.mean(center * center, axis=-1, keepdims=True) + EPS)
    return center * rstd, rstd


def norm_back(grad, normed, rstd, gain):
    scaled = grad * gain
    return rstd * (
        scaled
        - jnp.mean(scaled, axis=-1, keepdims=True)
        - normed * jnp.mean(scaled * normed, axis=-1, keepdims=True)
    )


def by_eight(x):
    return jnp.sum(x.reshape(x.shape[0] // 8, 8, x.shape[1]), axis=0)


def feed_kernel(
    devices,
    tok_ref,
    state_ref,
    small_ref,
    upb_ref,
    wide_ref,
    mixed_ref,
    cot_ref,
    out_ref,
    one_ref,
    gm_ref,
    gwide_ref,
    side_ref,
    gside_ref,
    acc_ref,
    sums_ref,
    upb_sum_ref,
    att_ref,
    n1_ref,
    r1_ref,
    low_ref,
    g2_ref,
    gb_ref,
    hidden_ref,
    slope_ref,
    gpre_ref,
    ga_ref,
    m_low_ref,
    m_gb_ref,
    m_ga_ref,
    m_mixed_ref,
    m_hidden_ref,
    m_gpre_ref,
    low_t_ref,
    gb_t_ref,
):
    step = pl.program_id(0)
    last = pl.num_programs(0) - 1
    length, width = tok_ref.shape[1:]
    hid = upb_ref.shape[1]
    rows = length + PAD
    shard, per = width // devices, hid // devices
    up = slice(0, hid)
    down = slice(hid, 2 * hid)
    outw = slice(2 * hid, 2 * hid + width)

    @pl.when(step == 0)
    def _():
        acc_ref[...] = jnp.zeros_like(acc_ref)
        sums_ref[...] = jnp.zeros_like(sums_ref)
        upb_sum_ref[...] = jnp.zeros_like(upb_sum_ref)
        gpre_ref[...] = jnp.zeros_like(gpre_ref)
        low_t_ref[...] = jnp.zeros_like(low_t_ref)
        side_ref[...] = small_ref[...].astype(FL).T

    def up_piece(j):
        c = slice(j, j + FCHUNK)
        acc_ref[:, c] += dot(low_t_ref[...], gpre_ref[:length, c], 1, 0)

    def down_piece(j):
        c = slice(j, j + FCHUNK)
        d = slice(hid + j, hid + j + FCHUNK)
        acc_ref[:, d] += dot(gb_t_ref[...], hidden_ref[:length, c], 1, 0)

    pieces = range(0, hid, FCHUNK)
    chunks = range(0, rows, ROWS)
    fills = [(up_piece, j) for j in pieces]

    def weave(stage, sums, works):
        totals = None
        done = 0
        for i, at in enumerate(chunks):
            made = stage(slice(at, at + ROWS))
            totals = made if totals is None else [x + y for x, y in zip(totals, made)]
            while done < len(works) and done * len(chunks) < (i + 1) * len(works):
                work, arg = works[done]
                work(arg)
                done += 1
        for at, total in zip(sums, totals or ()):
            sums_ref[8 * at : 8 * at + 8] += total

    att_ref[...] = dot(mixed_ref[0], wide_ref[:, outw], 1, 1)
    bias_att, bias_ffn = side_ref[PAD + 2 : PAD + 3], side_ref[PAD + 3 : PAD + 4]
    gain_one, shift_one, gain_two, shift_two = (side_ref[PAD + i : PAD + i + 1] for i in range(4, 8))

    def norm_one(r):
        if r.start < length:
            full = tok_ref[0, r, :].astype(FL)
        else:
            full = state_ref[0].astype(FL) + side_ref[:PAD]
        normed, rstd = norm_rows(full + (att_ref[r, :] + bias_att))
        n1_ref[r, :] = normed
        r1_ref[r, :] = rstd
        low_ref[r, :] = (normed * gain_one + shift_one).astype(BF)
        return []

    weave(norm_one, (), fills[:CUT])

    root = 0.7978845608
    for j in pieces:
        c = slice(j, j + FCHUNK)
        v = dot(low_ref[...], wide_ref[:, c], 1, 0) + upb_ref[:, c]
        square = v * v
        half = 0.5 + 0.5 * jnp.tanh(v * (root + (root * 0.044715) * square))
        act = v * half
        hidden_ref[:, c] = act.astype(BF)
        slope_ref[:, c] = half + (act * (1.0 - half)) * (2 * root + (6 * root * 0.044715) * square)

    att_ref[...] = dot(hidden_ref[...], wide_ref[:, down], 1, 1)

    def norm_two(r):
        first = n1_ref[r, :] * gain_one + shift_one
        normed, rstd = norm_rows(first + (att_ref[r, :] + bias_ffn))
        out_ref[0, r, :] = (normed * gain_two + shift_two).astype(BF)
        cot = cot_ref[0, r, :].astype(FL)
        back = norm_back(cot, normed, rstd, gain_two)
        g2_ref[r, :] = back
        low = back.astype(BF)
        gb_ref[r, :] = low
        return [by_eight(low.astype(FL)), by_eight(cot * normed), by_eight(cot)]

    weave(norm_two, (3, 6, 7), fills[CUT:])
    gb_t_ref[...] = gb_ref[:length].T
    low_t_ref[...] = low_ref[:length].T

    for j in pieces:
        c = slice(j, j + FCHUNK)
        d = slice(hid + j, hid + j + FCHUNK)
        gpre = (dot(gb_ref[...], wide_ref[:, d], 1, 0) * slope_ref[:, c]).astype(BF)
        gpre_ref[:, c] = gpre
        upb_sum_ref[:, c] += by_eight(gpre.astype(FL))

    att_ref[...] = dot(gpre_ref[...], wide_ref[:, up], 1, 1)

    def norm_last(r):
        g1 = g2_ref[r, :] + att_ref[r, :]
        normed = n1_ref[r, :]
        back = norm_back(g1, normed, r1_ref[r, :], gain_one)
        one_ref[0, r, :] = back
        low = back.astype(BF)
        ga_ref[r, :] = low
        return [by_eight(low.astype(FL)), by_eight(g1 * normed), by_eight(g1)]

    weave(norm_last, (2, 4, 5), [(down_piece, j) for j in pieces])

    gm_ref[0] = dot(ga_ref[...], wide_ref[:, outw], 1, 0).astype(BF)
    acc_ref[:, outw] += dot(ga_ref[:length], mixed_ref[0, :length], 0, 0)

    mem = pl.ds(pl.multiple_of(step * PAD, PAD), PAD)
    m_low_ref[mem, :] = low_ref[length:, :]
    m_gb_ref[mem, :] = gb_ref[length:, :]
    m_ga_ref[mem, :] = ga_ref[length:, :]
    m_mixed_ref[mem, :] = mixed_ref[0, length:, :]
    m_hidden_ref[mem, :] = hidden_ref[length:, :]
    m_gpre_ref[mem, :] = gpre_ref[length:, :]

    @pl.when(step == last)
    def _():
        left_low = jnp.concatenate([low_t_ref[...], m_low_ref[...].T], axis=1)
        left_gb = m_gb_ref[...].T
        for j in pieces:
            c = slice(j, j + FCHUNK)
            d = slice(hid + j, hid + j + FCHUNK)
            right = jnp.concatenate([gpre_ref[:length, c], m_gpre_ref[:, c]], axis=0)
            gwide_ref[:, c] = (acc_ref[:, c] + dot(left_low, right, 1, 0)).astype(BF)
            gwide_ref[:, d] = (acc_ref[:, d] + dot(left_gb, m_hidden_ref[:, c], 1, 0)).astype(BF)
        gwide_ref[:, outw] = (acc_ref[:, outw] + dot(m_ga_ref[...], m_mixed_ref[...], 0, 0)).astype(BF)
        side_ref[...] = jnp.zeros_like(side_ref)
        for i in range(8):
            side_ref[PAD + i : PAD + i + 1] = jnp.sum(sums_ref[8 * i : 8 * i + 8], axis=0, keepdims=True)
        gside_ref[...] = side_ref[...].T
        bias = jnp.sum(upb_sum_ref[...], axis=0, keepdims=True)
        for i in range(devices):
            piece = bias[:, i * per : (i + 1) * per]
            gside_ref[i * shard : i * shard + 1, BIAS : BIAS + per] = piece
        gwide_ref[:, 2 * hid + width :] = gside_ref[...].astype(BF)


def feed(devices, tok, state, small, upb, wide, mixed, cot):
    count, length, width = tok.shape
    rows = length + PAD
    hid = upb.shape[1]
    cols = wide.shape[1]
    one = lambda *dims: pl.BlockSpec((1,) + dims, lambda b: (b,) + (0,) * len(dims))
    whole = lambda *dims: pl.BlockSpec(dims, lambda b: (0,) * len(dims), pipeline_mode=pl.Buffered(1))
    final = lambda *dims: pl.BlockSpec(dims, lambda b: (0,) * len(dims))
    vm = pltpu.VMEM
    return pl.pallas_call(
        partial(feed_kernel, devices),
        grid=(count,),
        in_specs=[
            one(length, width),
            one(PAD, width),
            whole(width, LANES),
            whole(1, hid),
            whole(width, cols),
            one(rows, width),
            one(rows, width),
        ],
        out_specs=[
            one(rows, width),
            one(rows, width),
            one(rows, width),
            final(width, cols + LANES),
        ],
        out_shape=[
            jax.ShapeDtypeStruct((count, rows, width), BF),
            jax.ShapeDtypeStruct((count, rows, width), FL),
            jax.ShapeDtypeStruct((count, rows, width), BF),
            jax.ShapeDtypeStruct((width, cols + LANES), BF),
        ],
        scratch_shapes=[
            vm((LANES, width), FL),
            vm((width, LANES), FL),
            vm((width, cols), FL),
            vm((64, width), FL),
            vm((8, hid), FL),
            vm((rows, width), FL),
            vm((rows, width), FL),
            vm((rows, 1), FL),
            vm((rows, width), BF),
            vm((rows, width), FL),
            vm((rows, width), BF),
            vm((rows, hid), BF),
            vm((rows, hid), FL),
            vm((rows, hid), BF),
            vm((rows, width), BF),
            vm((count * PAD, width), BF),
            vm((count * PAD, width), BF),
            vm((count * PAD, width), BF),
            vm((count * PAD, width), BF),
            vm((count * PAD, hid), BF),
            vm((count * PAD, hid), BF),
            vm((width, length), BF),
            vm((width, length), BF),
        ],
        compiler_params=pltpu.CompilerParams(vmem_limit_bytes=60 << 20),
        name="feed",
    )(tok, state, small, upb, wide, mixed, cot)


def return_kernel(
    qkv_ref,
    pt_ref,
    ptk_ref,
    ptq_ref,
    gm_ref,
    dj_ref,
    kt_ref,
    dpk_ref,
    dsk_ref,
    dqt_ref,
    dk_ref,
    dv_ref,
    s_ref,
    ds_ref,
):
    width = gm_ref.shape[2]
    length = gm_ref.shape[1] - PAD
    group = HALF // HDIM
    parts = length // HALF
    gpad = group * PAD
    pairs = width // (2 * HDIM)
    masks = pair_masks(2 * HDIM)

    def columns(g, which):
        return slice(which * width + g * HALF, which * width + (g + 1) * HALF)

    def features(g):
        return slice(g * HALF, (g + 1) * HALF)

    def memory_keys(g):
        v_mem = spread(qkv_ref[0, length:, columns(g, 2)], group)
        dpk_ref[g * gpad : (g + 1) * gpad, :] = dot(v_mem, gm_ref[0, :length, features(g)], 1, 1)
        kt_ref[features(g), :] = qkv_ref[0, :length, columns(g, 1)].T

    def memory_queries(g):
        do_mem = spread(gm_ref[0, length:, features(g)], group)
        q_mem = spread(qkv_ref[0, length:, columns(g, 0)], group)
        prob = ptq_ref[0, :, g * gpad : (g + 1) * gpad]
        pf = prob.astype(FL)
        t = pf * dot(qkv_ref[0, :, columns(g, 2)], do_mem, 1, 1)
        ds = (t - pf * jnp.sum(t, axis=0, keepdims=True)).astype(BF)
        dv_ref[:, features(g)] = dot(prob, do_mem, 1, 0)
        dk_ref[:, features(g)] = dot(ds, q_mem, 1, 0)
        dq = fold(dot(ds, qkv_ref[0, :, columns(g, 1)], 0, 0), group)
        dj_ref[0, length:, features(g)] = (dq * SCALE).astype(BF)

    def rise(h, part, slot):
        at = (h // 2) * 2 * HDIM
        low, upto = part * HALF, (part + 1) * HALF
        base = part * (part + 1) // 2 * HALF
        own = slice(h * PAD, (h + 1) * PAD)
        vm = qkv_ref[0, :upto, 2 * width + at : 2 * width + at + 2 * HDIM] * masks[h % 2]
        dp = dot(vm, gm_ref[0, low:upto, at : at + 2 * HDIM], 1, 1)
        deltas = []
        for c in range(0, HALF, LANES):
            lanes = slice(c, c + LANES)
            live = low + c + LANES
            t = pt_ref[0, h, base : base + live, lanes].astype(FL) * dp[:live, lanes]
            tm = ptk_ref[0, own, low + c : live].astype(FL) * dpk_ref[own, low + c : live]
            s_ref[slot, :live, lanes] = t
            deltas.append(jnp.sum(t, axis=0, keepdims=True) + jnp.sum(tm, axis=0, keepdims=True))
        return deltas

    def settle(h, part, slot, deltas):
        low, upto = part * HALF, (part + 1) * HALF
        base = part * (part + 1) // 2 * HALF
        own = slice(h * PAD, (h + 1) * PAD)
        keep = (h // 2) % 2
        for c, delta in zip(range(0, HALF, LANES), deltas):
            lanes = slice(c, c + LANES)
            live = low + c + LANES
            pf = pt_ref[0, h, base : base + live, lanes].astype(FL)
            ds_ref[keep, h % 2, base : base + live, lanes] = (s_ref[slot, :live, lanes] - pf * delta).astype(BF)
            if live < upto:
                ds_ref[keep, h % 2, base + live : base + upto, lanes] = jnp.zeros((upto - live, LANES), BF)
            pm = ptk_ref[0, own, low + c : live].astype(FL)
            dsk_ref[own, low + c : live] = (pm * (dpk_ref[own, low + c : live] - delta)).astype(BF)

    def gather_rows(p, source, other, into):
        lanes = slice(p * 2 * HDIM, (p + 1) * 2 * HDIM)
        rows = [other * masks[side] for side in range(2)]
        for tile in range(parts):
            left, right = [], []
            for side in range(2):
                for part in range(tile, parts):
                    base = part * (part + 1) // 2 * HALF + tile * HALF
                    left.append(source(side, slice(base, base + HALF)))
                    right.append(rows[side][part * HALF : (part + 1) * HALF])
            into[tile * HALF : (tile + 1) * HALF, lanes] += dot(
                jnp.concatenate(left, axis=1), jnp.concatenate(right, axis=0), 1, 0
            )

    def values_back(p):
        lanes = slice(p * 2 * HDIM, (p + 1) * 2 * HDIM)
        gather_rows(p, lambda side, r: pt_ref[0, 2 * p + side, r, :], gm_ref[0, :length, lanes], dv_ref)

    def keys_back(p):
        lanes = slice(p * 2 * HDIM, (p + 1) * 2 * HDIM)
        gather_rows(p, lambda side, r: ds_ref[p % 2, side, r, :], qkv_ref[0, :length, lanes], dk_ref)

    def queries_back(h):
        feat = slice(h * HDIM, (h + 1) * HDIM)
        for part in range(parts):
            low, upto = part * HALF, (part + 1) * HALF
            base = part * (part + 1) // 2 * HALF
            ds = ds_ref[(h // 2) % 2, h % 2, base : base + upto, :]
            dqt_ref[feat, low:upto] = dot(kt_ref[feat, :upto], ds, 1, 0)

    def finish(g):
        own = slice(g * gpad, (g + 1) * gpad)
        k_mem = spread(qkv_ref[0, length:, columns(g, 1)], group)
        dq_t = dqt_ref[features(g), :] + dot(k_mem, dsk_ref[own, :], 0, 0)
        dj_ref[0, :length, features(g)] = (dq_t * SCALE).astype(BF).T
        dv_mem = fold(dot(ptk_ref[0, own, :], gm_ref[0, :length, features(g)], 1, 0), group)
        dk_mem = fold(dot(dsk_ref[own, :], qkv_ref[0, :length, columns(g, 0)], 1, 0), group)
        dj_ref[0, :length, columns(g, 1)] = dk_ref[:length, features(g)].astype(BF)
        dj_ref[0, :length, columns(g, 2)] = dv_ref[:length, features(g)].astype(BF)
        dj_ref[0, length:, columns(g, 1)] = (dk_ref[length:, features(g)] + dk_mem).astype(BF)
        dj_ref[0, length:, columns(g, 2)] = (dv_ref[length:, features(g)] + dv_mem).astype(BF)

    groups = width // HALF
    memory_keys(0)
    units = [(2 * p + side, part) for p in range(pairs) for side in range(2) for part in range(parts)]
    per_pair = 2 * parts
    deltas = {}
    later = []
    for u in range(len(units) + 1):
        if u < len(units):
            deltas[u] = rise(*units[u], u % SLOTS)
        if u >= 1:
            settle(*units[u - 1], (u - 1) % SLOTS, deltas.pop(u - 1))
            if u % per_pair == 0:
                p = u // per_pair - 1
                later += [(queries_back, 2 * p), (queries_back, 2 * p + 1), (keys_back, p)]
                if p % 2 == 1:
                    later.append((finish, p // 2))
        if u < len(units):
            p, at = u // per_pair, u % per_pair
            if at == 0 and p % 2 == 0:
                memory_queries(p // 2)
            if at == 1:
                values_back(p)
            if at == 2 and p % 2 == 1 and p // 2 + 1 < groups:
                memory_keys(p // 2 + 1)
        if later:
            work, arg = later.pop(0)
            work(arg)
    for work, arg in later:
        work(arg)


def go_back(begin, count, qkv, pt, ptk, ptq, gm):
    rows, width = gm.shape[1:]
    length = rows - PAD
    heads = width // HDIM
    one = lambda *dims: pl.BlockSpec((1,) + dims, lambda b: (b + begin,) + (0,) * len(dims))
    vm = pltpu.VMEM
    return pl.pallas_call(
        return_kernel,
        grid=(count,),
        in_specs=[
            one(rows, 3 * width),
            one(*pt.shape[1:]),
            one(heads * PAD, length),
            one(rows, heads * PAD),
            one(rows, width),
        ],
        out_specs=pl.BlockSpec((1, rows, 3 * width), lambda b: (b, 0, 0)),
        out_shape=jax.ShapeDtypeStruct((count, rows, 3 * width), BF),
        scratch_shapes=[
            vm((width, length), BF),
            vm((heads * PAD, length), FL),
            vm((heads * PAD, length), BF),
            vm((width, length), FL),
            vm((rows, width), FL),
            vm((rows, width), FL),
            vm((SLOTS, length, HALF), FL),
            vm((2, 2, pt.shape[2], HALF), BF),
        ],
        compiler_params=pltpu.CompilerParams(vmem_limit_bytes=48 << 20),
        cost_estimate=pl.CostEstimate(flops=count * 10**10, bytes_accessed=count * 10**7, transcendentals=0),
        name="go_back",
    )(qkv, pt, ptk, ptq, gm)


def weigh_kernel(
    begins,
    tok_ref,
    state_ref,
    one_ref,
    inw_ref,
    *refs,
):
    dj_refs, refs = refs[: len(begins)], refs[len(begins) :]
    gin_ref, acc_ref, left_ref, m_in_ref, m_dj_ref, side_ref, memb_ref = refs
    step = pl.program_id(0)
    last = pl.num_programs(0) - 1
    length, width = tok_ref.shape[1:]
    ends = begins[1:] + [last + 1]

    @pl.when(step == 0)
    def _():
        acc_ref[...] = jnp.zeros_like(acc_ref)
        side_ref[...] = jnp.zeros_like(side_ref)
        memb_ref[...] = inw_ref[:, 3 * width :].astype(FL).T
        left_ref[width:, :] = jnp.ones((ONES, length), BF)

    mem = pl.ds(pl.multiple_of(step * PAD, PAD), PAD)
    m_in_ref[mem, :] = (state_ref[0].astype(FL) + memb_ref[:PAD]).astype(BF)
    side_ref[0:PAD, :] += one_ref[0]
    left_ref[:width, :] = tok_ref[0].T
    for g, dj_ref in enumerate(dj_refs):

        @pl.when((step >= begins[g]) & (step < ends[g]))
        def _(dj_ref=dj_ref):
            m_dj_ref[mem, :] = dj_ref[0, length:, :]
            for j in range(0, 3 * width, FCHUNK):
                c = slice(j, j + FCHUNK)
                acc_ref[:, c] += dot(left_ref[...], dj_ref[0, :length, c], 1, 0)

    @pl.when(step == last)
    def _():
        more = jnp.concatenate([m_in_ref[...].T, jnp.ones((ONES, m_in_ref.shape[0]), BF)], axis=0)
        for j in range(0, 3 * width, FCHUNK):
            c = slice(j, j + FCHUNK)
            acc_ref[:, c] += dot(more, m_dj_ref[:, c], 1, 0)
        gin_ref[:, : 3 * width] = acc_ref[:width].astype(BF)
        back = dot(m_dj_ref[...], inw_ref[:, : 3 * width], 1, 1)
        side_ref[0:PAD, :] += jnp.sum(back.reshape(last + 1, PAD, width), axis=0)
        side_ref[PAD : PAD + 1, :] = acc_ref[width : width + 1, :width]
        side_ref[PAD + 1 : PAD + 2, :] = acc_ref[width : width + 1, 2 * width :]
        gin_ref[:, 3 * width :] = side_ref[...].T.astype(BF)


def weigh(tok, state, near, one_grad, djs, begins):
    count, length, width = tok.shape
    rows = length + PAD
    one = lambda *dims: pl.BlockSpec((1,) + dims, lambda b: (b,) + (0,) * len(dims))
    whole = lambda *dims: pl.BlockSpec(dims, lambda b: (0,) * len(dims), pipeline_mode=pl.Buffered(1))
    final = lambda *dims: pl.BlockSpec(dims, lambda b: (0,) * len(dims))
    part = lambda g: pl.BlockSpec(
        (1, rows, 3 * width), lambda b: (jnp.clip(b - begins[g], 0, djs[g].shape[0] - 1), 0, 0)
    )
    vm = pltpu.VMEM
    return pl.pallas_call(
        partial(weigh_kernel, begins),
        grid=(count,),
        in_specs=[
            one(length, width),
            one(PAD, width),
            pl.BlockSpec((1, PAD, width), lambda b: (b, length // PAD, 0)),
            whole(width, 3 * width + LANES),
        ]
        + [part(g) for g in range(len(djs))],
        out_specs=final(width, 3 * width + LANES),
        out_shape=jax.ShapeDtypeStruct((width, 3 * width + LANES), BF),
        scratch_shapes=[
            vm((width + ONES, 3 * width), FL),
            vm((width + ONES, length), BF),
            vm((count * PAD, width), BF),
            vm((count * PAD, 3 * width), BF),
            vm((LANES, width), FL),
            vm((LANES, width), FL),
        ],
        compiler_params=pltpu.CompilerParams(vmem_limit_bytes=48 << 20),
        cost_estimate=pl.CostEstimate(flops=count * 10**9, bytes_accessed=count * 3 * 10**6, transcendentals=0),
        name="weigh",
    )(tok, state, one_grad, near, *djs)


def descend_kernel(one_ref, dj_ref, inw_ref, grad_ref):
    width = one_ref.shape[2]
    grad_ref[0] = one_ref[0] + dot(dj_ref[0], inw_ref[:, : 3 * width], 1, 1)


def descend(total, begin, one_grad, dj, near, into):
    count, rows, wide = dj.shape
    width = one_grad.shape[2]
    length = rows - PAD
    shift = lambda *dims: pl.BlockSpec((1,) + dims, lambda b: (b + begin, 0, 0))
    kept = () if into is None else (into,)

    def kernel(one_ref, dj_ref, inw_ref, *rest):
        descend_kernel(one_ref, dj_ref, inw_ref, rest[-1])

    return pl.pallas_call(
        kernel,
        grid=(count,),
        in_specs=[
            shift(length, width),
            pl.BlockSpec((1, length, wide), lambda b: (b, 0, 0)),
            pl.BlockSpec((width, wide + LANES), lambda b: (0, 0), pipeline_mode=pl.Buffered(1)),
        ]
        + [pl.BlockSpec(memory_space=pl.ANY)] * len(kept),
        out_specs=shift(length, width),
        out_shape=jax.ShapeDtypeStruct((total, length, width), FL),
        input_output_aliases={3: 0} if kept else {},
        compiler_params=pltpu.CompilerParams(vmem_limit_bytes=32 << 20),
        cost_estimate=pl.CostEstimate(flops=count * 10**9, bytes_accessed=count * 4 * 10**6, transcendentals=0),
        name="descend",
    )(one_grad, dj, near, *kept)


def pack_kernel(in_ref, up_ref, down_ref, out_ref, vec_ref, bias_ref, mem_ref, near_ref, far_ref, flip_ref):
    shard, cols = in_ref.shape
    hid, width = up_ref.shape[1], out_ref.shape[1]
    flip_ref[...] = jnp.zeros_like(flip_ref)
    flip_ref[PAD : PAD + 8, :shard] = vec_ref[...]
    flip_ref[...] = flip_ref[...].T
    flip_ref[:shard, : mem_ref.shape[1]] = mem_ref[...]
    flip_ref[0:1, BIAS : BIAS + bias_ref.shape[1]] = bias_ref[...]
    near_ref[:, :cols] = in_ref[...].astype(BF)
    near_ref[:, cols:] = flip_ref[:shard].astype(BF)
    far_ref[:, :hid] = up_ref[...].astype(BF)
    far_ref[:, hid : 2 * hid] = down_ref[...].astype(BF)
    far_ref[:, 2 * hid :] = out_ref[...].astype(BF)


def pack(in_w, up_w, down_t, out_t, vectors, bias, mem_t):
    shard, cols = in_w.shape
    wide = 2 * up_w.shape[1] + out_t.shape[1]
    return pl.pallas_call(
        pack_kernel,
        out_shape=[
            jax.ShapeDtypeStruct((shard, cols + LANES), BF),
            jax.ShapeDtypeStruct((shard, wide), BF),
        ],
        scratch_shapes=[pltpu.VMEM((LANES, LANES), FL)],
        name="pack",
    )(in_w, up_w, down_t, out_t, vectors, bias, mem_t)


def square_kernel(cols, near_ref, far_ref, sum_ref):
    wide = far_ref.shape[1] - LANES
    near, far = near_ref[:, :cols], far_ref[:, :wide]
    side = near_ref[:, cols:] + far_ref[:, wide:]
    total = jnp.sum(near * near) + jnp.sum(far * far) + jnp.sum(side * side)
    sum_ref[...] = jnp.full(sum_ref.shape, total, FL)


def adam_kernel(sizes, rates, decays, near_ref, far_ref, total_ref, *refs):
    cols, hid, width = sizes
    state_refs, new_refs, norm_ref, flip_ref = refs[:21], refs[21:42], refs[42], refs[43]
    shard = near_ref.shape[0]
    norm = jnp.sqrt(total_ref[...])
    norm_ref[...] = norm
    factor = (1.0 / jnp.maximum(norm, 1.0))[0:1, 0:1]
    side = near_ref[:, cols:] + far_ref[:, 2 * hid + width :]
    flip_ref[...] = jnp.zeros_like(flip_ref)
    flip_ref[:shard] = side
    turned = flip_ref[...].T
    bias = pltpu.roll(side, LANES - BIAS, 1)
    grads = (
        near_ref[:, :cols],
        far_ref[:, 2 * hid : 2 * hid + width],
        far_ref[:, :hid],
        far_ref[:, hid : 2 * hid],
        turned[PAD : PAD + 8, :shard],
        bias[0:1, : state_refs[15].shape[1]],
        side[:, : state_refs[18].shape[1]],
    )
    correction = 1.0 - 0.5**STEP
    for i in range(7):
        weight, first, second = (state_refs[3 * i + k][...] for k in range(3))
        grad = grads[i] * factor
        first_new = 0.5 * first + 0.5 * grad
        second_new = 0.5 * second + 0.5 * grad * grad
        step = first_new / correction / (jnp.sqrt(second_new / correction) + 1e-08)
        new_refs[3 * i][...] = weight - rates[i] * (step + decays[i] * weight)
        new_refs[3 * i + 1][...] = first_new
        new_refs[3 * i + 2][...] = second_new


def exchange(x, bit, devices):
    return lax.ppermute(x, AXES, [(i, i ^ bit) for i in range(devices)])


def beside(got, sent, work):
    if work is None:
        return got, None
    made = work(lambda value: lax.optimization_barrier((value, sent))[0])
    return lax.optimization_barrier((got, made))


def gather(x, devices, index, works):
    rows, cols = x.shape
    held = x[None]
    bit = devices // 2
    results = []
    while bit:
        got = exchange(held, bit, devices)
        got, made = beside(got, held, works.get(bit))
        results.append(made)
        upper = (index & bit) != 0
        held = jnp.stack([jnp.where(upper, got, held), jnp.where(upper, held, got)], axis=1)
        held = held.reshape(-1, rows, cols)
        bit //= 2
    return held.reshape(devices * rows, cols), [made for made in results if made is not None]


def halve(held, got, place, upper):
    total = held if got is None else held.astype(FL) + got.astype(FL)
    low, high = (lax.index_in_dim(total, i, place, keepdims=False) for i in range(2))
    return jnp.where(upper, high, low), jnp.where(upper, low, high).astype(BF)


def scatter_sum(x, devices, index, works):
    total, cols = x.shape
    rows = total // devices
    bits = devices.bit_length() - 1
    cut = cols // (2 * LANES) * LANES
    orders = [list(range(bits)) for _ in range(2)]
    if bits > 2:
        orders[1][1:3] = [2, 1]
    held = [half.reshape((2,) * bits + (rows, -1)) for half in (x[:, :cut], x[:, cut:])]
    got = [None, None]
    results = []
    for step in range(bits):
        send = [None, None]
        for half, order in enumerate(orders):
            bit = order[step]
            place = sum(1 for other in order[step:] if other > bit)
            upper = (index & (1 << bit)) != 0
            held[half], send[half] = halve(held[half], got[half], place, upper)
        got = [exchange(value, 1 << order[step], devices) for value, order in zip(send, orders)]
        got, made = beside(got, send, works[step] if step < len(works) else None)
        results.append(made)
    whole = [(value.astype(FL) + extra.astype(FL)).reshape(rows, -1) for value, extra in zip(held, got)]
    return jnp.concatenate(whole, axis=1), results


def butterfly(x, devices):
    bit = 1
    while bit < devices:
        x = x + exchange(x, bit, devices)
        bit *= 2
    return x


def per_device(
    devices,
    tokens,
    memory_state,
    cotangent,
    in_weight,
    in_first,
    in_second,
    out_weight,
    out_first,
    out_second,
    up_weight,
    up_first,
    up_second,
    down_weight,
    down_first,
    down_second,
    vectors,
    vectors_first,
    vectors_second,
    up_bias,
    up_bias_first,
    up_bias_second,
    memory_embed,
    memory_first,
    memory_second,
):
    index = lax.axis_index(AXES)
    micro, local, length, width = tokens.shape
    count = micro * local
    extra = memory_state.shape[2]
    shard = in_weight.shape[0]
    hid = up_weight.shape[1]
    per_bias = up_bias.shape[0] // shard

    near, far = pack(
        in_weight,
        up_weight,
        down_weight.T,
        out_weight.T,
        vectors,
        up_bias.reshape(1, -1),
        memory_embed.T,
    )
    wide = lax.all_gather(far, AXES, axis=0, tiled=True)

    def align(tie):
        cot = tie(cotangent).reshape(count, extra + length, width)
        return jnp.concatenate(
            [cot[:, extra:], cot[:, :extra], jnp.zeros((count, PAD - extra, width), BF)], axis=1
        )

    near, (cot,) = gather(near, devices, index, {2: align})
    small = near[:, 3 * width :]
    upb = small.reshape(devices, shard, LANES)[:, 0, BIAS : BIAS + up_bias.shape[0]].astype(FL)
    upb = upb.reshape(1, hid)

    tok = tokens.reshape(count, length, width)
    state = jnp.pad(memory_state.reshape(count, extra, width), ((0, 0), (0, PAD - extra), (0, 0)))

    qkv, pt, ptk, ptq, mixed = attend(extra, tok, state, near)
    out, one_grad, gm, gwide = feed(devices, tok, state, small, upb, wide, mixed, cot)

    def split(sizes):
        begins = [0]
        for size in sizes:
            begins.append(begins[-1] + size)
        return list(zip(begins, sizes))

    def back(begin, size):
        return lambda tie: go_back(begin, size, tie(qkv), pt, ptk, ptq, gm)

    runs = split(BACK) if sum(BACK) == count else split([count])
    gfar, djs = scatter_sum(gwide, devices, index, [back(*run) for run in runs])
    djs = djs[: len(runs)]
    gin = weigh(tok, state, near, one_grad, djs, [begin for begin, _ in runs])
    grads = []

    def down(picked):
        def work(tie):
            for i in picked:
                into = grads[-1] if grads else None
                grads.append(descend(count, runs[i][0], one_grad, tie(djs[i]), near, into))
            return grads[-1]

        return work

    def order(tie):
        rows = tie(out)
        rows = jnp.concatenate([rows[:, length : length + extra], rows[:, :length]], axis=1)
        return rows.reshape(micro, local, extra + length, width).transpose(0, 2, 1, 3)

    cut = len(runs) // 2
    works = [down(range(cut)), down(range(cut, len(runs))), order]
    gnear, (_, input_grad, output, *_) = scatter_sum(gin, devices, index, works)
    output = output.transpose(0, 2, 1, 3)
    input_grad = input_grad.reshape(micro, local, length, width)

    squares = pl.pallas_call(
        partial(square_kernel, 3 * width),
        out_shape=jax.ShapeDtypeStruct((8, LANES), FL),
        name="squares",
    )(gnear, gfar)
    squares = butterfly(squares, devices)
    total_rows = extra + length
    rates = (
        0.5 * width ** (-0.5),
        0.5 * (width * 32 // total_rows) ** (-0.5),
        0.5 * width ** (-0.5),
        0.5 * hid ** (-0.5),
        0.1,
        0.1,
        0.5,
    )
    decays = (0.1, 0.1, 0.1, 0.1, 0.0, 0.0, 0.0)
    same = lambda value: value
    turn = lambda value: value.T
    flat = lambda value: value.reshape(1, -1)
    views = (same, turn, same, turn, same, flat, turn)
    states = (
        (in_weight, in_first, in_second),
        (out_weight, out_first, out_second),
        (up_weight, up_first, up_second),
        (down_weight, down_first, down_second),
        (vectors, vectors_first, vectors_second),
        (up_bias, up_bias_first, up_bias_second),
        (memory_embed, memory_first, memory_second),
    )
    held = [view(value) for view, group in zip(views, states) for value in group]
    *new, norm = pl.pallas_call(
        partial(adam_kernel, (3 * width, hid, width), rates, decays),
        out_shape=[jax.ShapeDtypeStruct(value.shape, FL) for value in held]
        + [jax.ShapeDtypeStruct((8, LANES), FL)],
        scratch_shapes=[pltpu.VMEM((LANES, LANES), FL)],
        name="adam",
    )(gnear, gfar, squares, *held)
    back_views = (same, turn, same, turn, same, lambda value: value.reshape(-1), turn)
    results = [back_views[i // 3](value) for i, value in enumerate(new)]
    return (output, input_grad, *results, norm[0, 0])


def solution(mesh):
    blocks = P(None, AXES, None, None)
    lead = P(AXES, None)
    trail = P(None, AXES)
    flat = P(AXES)
    weights = (lead,) * 3 + (trail,) * 3 + (lead,) * 3 + (trail,) * 6 + (flat,) * 3 + (trail,) * 3
    devices = mesh.shape["dp"] * mesh.shape["fsdp"]
    return jax.shard_map(
        partial(per_device, devices),
        mesh=mesh,
        in_specs=(blocks,) * 3 + weights,
        out_specs=(blocks,) * 2 + weights + (P(),),
        check_vma=False,
    )
```

```python
from functools import partial

import jax
import jax.numpy as jnp
from jax import lax
from jax.experimental import pallas as pl
from jax.experimental.pallas import tpu as pltpu
from jax.sharding import PartitionSpec as P

STEP = 7
HDIM = 64
PAD = 32
HALF = 256
FCHUNK = 256
ROWS = 32
BF = jnp.bfloat16
FL = jnp.float32
AXES = ("dp", "fsdp")
NEG = -1e30
EPS = 1e-05
SCALE = HDIM ** (-0.5)
LANES = 128
BIAS = 64
SLOTS = 4
PLAN_MORE = (0, 2, 4, 5)
PLAN_LAST = (2, 4, 7, 5)
CUT = 3
ONES = 16
BACK = (1, 3, 2, 2)


def dot(a, b, ca, cb):
    return lax.dot_general(a, b, (((ca,), (cb,)), ((), ())), preferred_element_type=FL)


def head_mask(rows, width):
    row = lax.broadcasted_iota(jnp.int32, (rows, width), 0) // PAD
    col = lax.broadcasted_iota(jnp.int32, (rows, width), 1) // HDIM
    return row == col


def spread(x, heads):
    tiled = jnp.concatenate([x.astype(FL)] * heads, axis=0)
    return jnp.where(head_mask(*tiled.shape), tiled, 0.0).astype(BF)


def fold(y, heads):
    own = jnp.where(head_mask(*y.shape), y, 0.0)
    return sum(own[h * PAD : (h + 1) * PAD] for h in range(heads))


def pair_masks(width):
    col = lax.broadcasted_iota(jnp.int32, (1, width), 1)
    low = jnp.where(col < HDIM, 1.0, 0.0)
    return low.astype(BF), (1.0 - low).astype(BF)


def attend_kernel(
    extra,
    tok_ref,
    state_ref,
    first_ref,
    first_state_ref,
    inw_ref,
    qkv_ref,
    pt_ref,
    ptk_ref,
    ptq_ref,
    mixed_ref,
    vt_ref,
    sk_ref,
    ot_ref,
    side_ref,
    inp_ref,
    s_ref,
    ahead_ref,
):
    length, width = tok_ref.shape[1:]
    rows = length + PAD
    group = HALF // HDIM
    parts = length // HALF
    gpad = group * PAD
    diag = lax.broadcasted_iota(jnp.int32, (LANES, LANES), 0) <= lax.broadcasted_iota(
        jnp.int32, (LANES, LANES), 1
    )
    key_live = lax.broadcasted_iota(jnp.int32, (gpad, 1), 0) % PAD < extra
    place_live = lax.broadcasted_iota(jnp.int32, (rows, 1), 0) < length + extra
    masks = pair_masks(2 * HDIM)

    def columns(g, which):
        return slice(which * width + g * HALF, which * width + (g + 1) * HALF)

    def ahead(which):
        return slice(which * HALF, (which + 1) * HALF)

    def take(source, source_state):
        inp_ref[:length] = source[0]
        inp_ref[length:] = (source_state[0].astype(FL) + side_ref[:PAD]).astype(BF)

    def project(g, which):
        feat = slice(g * HALF, (g + 1) * HALF)
        made = dot(inp_ref[...], inw_ref[:, columns(g, which)], 1, 0)
        if which == 0:
            made = (made + side_ref[PAD : PAD + 1, feat]) * SCALE
        if which == 2:
            made = made + side_ref[PAD + 1 : PAD + 2, feat]
        made = made.astype(BF)
        if g:
            qkv_ref[0, :, columns(g, which)] = made
        else:
            ahead_ref[:, ahead(which)] = made
        if which == 2:
            vt_ref[feat, :] = made[:length].T

    def memory_keys(g):
        if g:
            mem, query = qkv_ref[0, length:, columns(g, 1)], qkv_ref[0, :length, columns(g, 0)]
        else:
            mem, query = ahead_ref[length:, ahead(1)], ahead_ref[:length, ahead(0)]
        made = dot(spread(mem, group), query, 1, 1)
        sk_ref[g * gpad : (g + 1) * gpad, :] = jnp.where(key_live, made, NEG)

    def memory_queries(g):
        q_mem = spread(qkv_ref[0, length:, columns(g, 0)], group)
        sq = jnp.where(place_live, dot(qkv_ref[0, :, columns(g, 1)], q_mem, 1, 1), NEG)
        eq = jnp.exp(sq - jnp.max(sq, axis=0, keepdims=True))
        probs = (eq * (1.0 / jnp.sum(eq, axis=0, keepdims=True))).astype(BF)
        ptq_ref[0, :, g * gpad : (g + 1) * gpad] = probs
        om = dot(probs, qkv_ref[0, :, columns(g, 2)], 0, 0)
        mixed_ref[0, length:, g * HALF : (g + 1) * HALF] = fold(om, group).astype(BF)

    @pl.when(pl.program_id(0) == 0)
    def _():
        side_ref[...] = inw_ref[:, 3 * width :].astype(FL).T
        take(first_ref, first_state_ref)
        for which in range(3):
            project(0, which)
        memory_keys(0)

    def score(h, part, slot):
        at = (h // 2) * 2 * HDIM
        low, upto = part * HALF, (part + 1) * HALF
        qp = qkv_ref[0, low:upto, at : at + 2 * HDIM]
        km = qkv_ref[0, :upto, width + at : width + at + 2 * HDIM] * masks[h % 2]
        s = dot(km, qp, 1, 1)
        tops = []
        for c in range(0, HALF, LANES):
            lanes = slice(c, c + LANES)
            edge = jnp.where(diag, s[low + c : low + c + LANES, lanes], NEG)
            s_ref[slot, low + c : low + c + LANES, lanes] = edge
            top = jnp.maximum(
                jnp.max(edge, axis=0, keepdims=True),
                jnp.max(sk_ref[h * PAD : (h + 1) * PAD, low + c : low + c + LANES], axis=0, keepdims=True),
            )
            if low + c:
                s_ref[slot, : low + c, lanes] = s[: low + c, lanes]
                top = jnp.maximum(top, jnp.max(s[: low + c, lanes], axis=0, keepdims=True))
            tops.append(top)
        return tops

    def soften(h, part, slot, tops):
        low, upto = part * HALF, (part + 1) * HALF
        own = slice(h * PAD, (h + 1) * PAD)
        base = part * (part + 1) // 2 * HALF
        made, made_mem = [], []
        for c, top in zip(range(0, HALF, LANES), tops):
            lanes = slice(c, c + LANES)
            live = low + c + LANES
            e = jnp.exp(s_ref[slot, :live, lanes] - top)
            e_mem = jnp.exp(sk_ref[own, low + c : live] - top)
            total = jnp.sum(e, axis=0, keepdims=True) + jnp.sum(e_mem, axis=0, keepdims=True)
            share = 1.0 / total
            made.append(e * share)
            made_mem.append(e_mem * share)
            if live < upto:
                made[-1] = jnp.concatenate([made[-1], jnp.zeros((upto - live, LANES), FL)], axis=0)
        pt_ref[0, h, base : base + upto, :] = jnp.concatenate(made, axis=1).astype(BF)
        ptk_ref[0, own, low:upto] = jnp.concatenate(made_mem, axis=1).astype(BF)

    def mix(h, part):
        upto = (part + 1) * HALF
        base = part * (part + 1) // 2 * HALF
        feat = slice(h * HDIM, (h + 1) * HDIM)
        ot_ref[feat, part * HALF : upto] = dot(
            vt_ref[feat, :upto], pt_ref[0, h, base : base + upto, :], 1, 0
        )

    def finish(g):
        v_mem = spread(qkv_ref[0, length:, columns(g, 2)], group)
        feat = slice(g * HALF, (g + 1) * HALF)
        om_t = ot_ref[feat, :] + dot(v_mem, ptk_ref[0, g * gpad : (g + 1) * gpad, :], 0, 0)
        mixed_ref[0, :length, feat] = om_t.astype(BF).T

    groups = width // HALF
    units = [(g * group + i, part) for g in range(groups) for i in range(group) for part in range(parts)]
    per_group = group * parts
    for which in range(3):
        qkv_ref[0, :, columns(0, which)] = ahead_ref[:, ahead(which)]
    works = {}
    for g in range(groups):
        at = g * per_group
        more = g + 1 < groups
        plan = PLAN_MORE if more else PLAN_LAST
        works.setdefault(at + 1, []).append((memory_queries, g))
        if g:
            works.setdefault(at + 3, []).append((finish, g - 1))
        if not more:
            works.setdefault(at, []).append((take, tok_ref, state_ref))
        for which in range(3):
            works.setdefault(at + plan[which], []).append((project, g + 1 if more else 0, which))
        works.setdefault(at + plan[3], []).append((memory_keys, g + 1 if more else 0))
    tops = {}
    for u in range(len(units) + 3):
        if u < len(units):
            tops[u] = score(*units[u], u % SLOTS)
        if 2 <= u <= len(units) + 1:
            soften(*units[u - 2], (u - 2) % SLOTS, tops.pop(u - 2))
        if u >= 3:
            mix(*units[u - 3])
        for work, *given in works.get(u, ()):
            work(*given)
    finish(groups - 1)


def attend(extra, tok, state, near):
    count, length, width = tok.shape
    heads = width // HDIM
    rows = length + PAD
    parts = length // HALF
    ptrows = parts * (parts + 1) // 2 * HALF
    one = lambda *dims: pl.BlockSpec((1,) + dims, lambda b: (b,) + (0,) * len(dims))
    after = lambda *dims: pl.BlockSpec((1,) + dims, lambda b: (jnp.minimum(b + 1, count - 1), 0, 0))
    whole = lambda *dims: pl.BlockSpec(dims, lambda b: (0,) * len(dims), pipeline_mode=pl.Buffered(1))
    return pl.pallas_call(
        partial(attend_kernel, extra),
        grid=(count,),
        in_specs=[
            after(length, width),
            after(PAD, width),
            pl.BlockSpec((1, length, width), lambda b: (0, 0, 0), pipeline_mode=pl.Buffered(1)),
            pl.BlockSpec((1, PAD, width), lambda b: (0, 0, 0), pipeline_mode=pl.Buffered(1)),
            whole(width, 3 * width + LANES),
        ],
        out_specs=[
            one(rows, 3 * width),
            one(heads, ptrows, HALF),
            one(heads * PAD, length),
            one(rows, heads * PAD),
            one(rows, width),
        ],
        out_shape=[
            jax.ShapeDtypeStruct((count, rows, 3 * width), BF),
            jax.ShapeDtypeStruct((count, heads, ptrows, HALF), BF),
            jax.ShapeDtypeStruct((count, heads * PAD, length), BF),
            jax.ShapeDtypeStruct((count, rows, heads * PAD), BF),
            jax.ShapeDtypeStruct((count, rows, width), BF),
        ],
        scratch_shapes=[
            pltpu.VMEM((width, length), BF),
            pltpu.VMEM((heads * PAD, length), FL),
            pltpu.VMEM((width, length), FL),
            pltpu.VMEM((LANES, width), FL),
            pltpu.VMEM((rows, width), BF),
            pltpu.VMEM((SLOTS, length, HALF), FL),
            pltpu.VMEM((rows, 3 * HALF), BF),
        ],
        compiler_params=pltpu.CompilerParams(vmem_limit_bytes=56 << 20),
        name="attend",
    )(tok, state, tok, state, near)


def norm_rows(x):
    center = x - jnp.mean(x, axis=-1, keepdims=True)
    rstd = lax.rsqrt(jnp.mean(center * center, axis=-1, keepdims=True) + EPS)
    return center * rstd, rstd


def norm_back(grad, normed, rstd, gain):
    scaled = grad * gain
    return rstd * (
        scaled
        - jnp.mean(scaled, axis=-1, keepdims=True)
        - normed * jnp.mean(scaled * normed, axis=-1, keepdims=True)
    )


def by_eight(x):
    return jnp.sum(x.reshape(x.shape[0] // 8, 8, x.shape[1]), axis=0)


def feed_kernel(
    devices,
    tok_ref,
    state_ref,
    small_ref,
    wide_ref,
    mixed_ref,
    cot_ref,
    out_ref,
    one_ref,
    gm_ref,
    gone_ref,
    gtwo_ref,
    upb_ref,
    side_ref,
    gside_ref,
    acc_ref,
    sums_ref,
    upb_sum_ref,
    att_ref,
    n1_ref,
    r1_ref,
    low_ref,
    g2_ref,
    gb_ref,
    hidden_ref,
    slope_ref,
    gpre_ref,
    ga_ref,
    m_low_ref,
    m_gb_ref,
    m_ga_ref,
    m_mixed_ref,
    m_hidden_ref,
    m_gpre_ref,
    low_t_ref,
    gb_t_ref,
):
    step = pl.program_id(0)
    last = pl.num_programs(0) - 1
    length, width = tok_ref.shape[1:]
    hid = upb_ref.shape[1]
    rows = length + PAD
    shard, per = width // devices, hid // devices
    up = slice(0, hid)
    down = slice(hid, 2 * hid)
    outw = slice(2 * hid, 2 * hid + width)

    @pl.when(step == 0)
    def _():
        acc_ref[...] = jnp.zeros_like(acc_ref)
        sums_ref[...] = jnp.zeros_like(sums_ref)
        upb_sum_ref[...] = jnp.zeros_like(upb_sum_ref)
        gpre_ref[...] = jnp.zeros_like(gpre_ref)
        low_t_ref[:width] = jnp.zeros((width, length), BF)
        low_t_ref[width:] = jnp.ones((ONES, length), BF)
        gside_ref[...] = small_ref[...].astype(FL)
        side_ref[...] = gside_ref[...].T
        for i in range(devices):
            upb_ref[:, i * per : (i + 1) * per] = gside_ref[i * shard : i * shard + 1, BIAS : BIAS + per]

    def put(at, value):
        cut = gone_ref.shape[1]
        if at < cut:
            gone_ref[:, at : at + value.shape[1]] = value.astype(BF)
        else:
            gtwo_ref[:, at - cut : at - cut + value.shape[1]] = value.astype(BF)

    def up_piece(j):
        c = slice(j, j + FCHUNK)
        made = dot(low_t_ref[...], gpre_ref[:length, c], 1, 0)
        acc_ref[:, c] += made[:width]
        upb_sum_ref[:, c] += made[width : width + 8]

    def down_piece(j):
        c = slice(j, j + FCHUNK)
        d = slice(hid + j, hid + j + FCHUNK)
        acc_ref[:, d] += dot(gb_t_ref[...], hidden_ref[:length, c], 1, 0)

    pieces = range(0, hid, FCHUNK)
    chunks = range(0, rows, ROWS)
    fills = [(up_piece, j) for j in pieces]

    def weave(stage, sums, works):
        totals = None
        done = 0
        for i, at in enumerate(chunks):
            made = stage(slice(at, at + ROWS))
            totals = made if totals is None else [x + y for x, y in zip(totals, made)]
            while done < len(works) and done * len(chunks) < (i + 1) * len(works):
                work, arg = works[done]
                work(arg)
                done += 1
        for at, total in zip(sums, totals or ()):
            sums_ref[8 * at : 8 * at + 8] += total

    att_ref[...] = dot(mixed_ref[0], wide_ref[:, outw], 1, 1)
    bias_att, bias_ffn = side_ref[PAD + 2 : PAD + 3], side_ref[PAD + 3 : PAD + 4]
    gain_one, shift_one, gain_two, shift_two = (side_ref[PAD + i : PAD + i + 1] for i in range(4, 8))

    shift_ffn = shift_one + bias_ffn

    def norm_one(r):
        if r.start < length:
            full = tok_ref[0, r, :].astype(FL)
        else:
            full = state_ref[0].astype(FL) + side_ref[:PAD]
        normed, rstd = norm_rows(full + (att_ref[r, :] + bias_att))
        n1_ref[r, :] = normed
        r1_ref[r, :] = rstd
        low_ref[r, :] = (normed * gain_one + shift_one).astype(BF)
        return []

    weave(norm_one, (), fills[:CUT])

    root = 0.7978845608
    for j in pieces:
        c = slice(j, j + FCHUNK)
        v = dot(low_ref[...], wide_ref[:, c], 1, 0) + upb_ref[:, c]
        square = v * v
        half = 0.5 + 0.5 * jnp.tanh(v * (root + (root * 0.044715) * square))
        act = v * half
        hidden_ref[:, c] = act.astype(BF)
        slope_ref[:, c] = half + (act * (1.0 - half)) * (2 * root + (6 * root * 0.044715) * square)

    att_ref[...] = dot(hidden_ref[...], wide_ref[:, down], 1, 1)

    def norm_two(r):
        normed, rstd = norm_rows(n1_ref[r, :] * gain_one + (att_ref[r, :] + shift_ffn))
        out_ref[0, r, :] = (normed * gain_two + shift_two).astype(BF)
        cot = cot_ref[0, r, :].astype(FL)
        back = norm_back(cot, normed, rstd, gain_two)
        g2_ref[r, :] = back
        low = back.astype(BF)
        gb_ref[r, :] = low
        return [by_eight(low.astype(FL)), by_eight(cot * normed), by_eight(cot)]

    weave(norm_two, (3, 6, 7), fills[CUT:])
    gb_t_ref[...] = gb_ref[:length].T
    low_t_ref[:width] = low_ref[:length].T

    for j in pieces:
        c = slice(j, j + FCHUNK)
        d = slice(hid + j, hid + j + FCHUNK)
        gpre = (dot(gb_ref[...], wide_ref[:, d], 1, 0) * slope_ref[:, c]).astype(BF)
        gpre_ref[:, c] = gpre

    att_ref[...] = dot(gpre_ref[...], wide_ref[:, up], 1, 1)

    def norm_last(r):
        g1 = g2_ref[r, :] + att_ref[r, :]
        normed = n1_ref[r, :]
        back = norm_back(g1, normed, r1_ref[r, :], gain_one)
        one_ref[0, r, :] = back
        low = back.astype(BF)
        ga_ref[r, :] = low
        return [by_eight(low.astype(FL)), by_eight(g1 * normed), by_eight(g1)]

    weave(norm_last, (2, 4, 5), [(down_piece, j) for j in pieces])

    gm_ref[0] = dot(ga_ref[...], wide_ref[:, outw], 1, 0).astype(BF)
    acc_ref[:, outw] += dot(ga_ref[:length], mixed_ref[0, :length], 0, 0)

    mem = pl.ds(pl.multiple_of(step * PAD, PAD), PAD)
    m_low_ref[mem, :] = low_ref[length:, :]
    m_gb_ref[mem, :] = gb_ref[length:, :]
    m_ga_ref[mem, :] = ga_ref[length:, :]
    m_mixed_ref[mem, :] = mixed_ref[0, length:, :]
    m_hidden_ref[mem, :] = hidden_ref[length:, :]
    m_gpre_ref[mem, :] = gpre_ref[length:, :]

    @pl.when(step == last)
    def _():
        more = jnp.concatenate([m_low_ref[...].T, jnp.ones((ONES, m_low_ref.shape[0]), BF)], axis=0)
        left_low = jnp.concatenate([low_t_ref[...], more], axis=1)
        left_gb = m_gb_ref[...].T
        for j in pieces:
            c = slice(j, j + FCHUNK)
            d = slice(hid + j, hid + j + FCHUNK)
            right = jnp.concatenate([gpre_ref[:length, c], m_gpre_ref[:, c]], axis=0)
            made = dot(left_low, right, 1, 0)
            put(c.start, acc_ref[:, c] + made[:width])
            upb_sum_ref[:, c] += made[width : width + 8]
            put(d.start, acc_ref[:, d] + dot(left_gb, m_hidden_ref[:, c], 1, 0))
        put(2 * hid, acc_ref[:, outw] + dot(m_ga_ref[...], m_mixed_ref[...], 0, 0))
        side_ref[...] = jnp.zeros_like(side_ref)
        for i in range(8):
            side_ref[PAD + i : PAD + i + 1] = jnp.sum(sums_ref[8 * i : 8 * i + 8], axis=0, keepdims=True)
        gside_ref[...] = side_ref[...].T
        bias = upb_sum_ref[0:1]
        for i in range(devices):
            piece = bias[:, i * per : (i + 1) * per]
            gside_ref[i * shard : i * shard + 1, BIAS : BIAS + per] = piece
        put(2 * hid + width, gside_ref[...])


def halfway(cols):
    return cols // (2 * LANES) * LANES


def feed(devices, tok, state, near, wide, mixed, cot):
    count, length, width = tok.shape
    rows = length + PAD
    cols = wide.shape[1]
    hid = (cols - width) // 2
    cut = halfway(cols + LANES)
    one = lambda *dims: pl.BlockSpec((1,) + dims, lambda b: (b,) + (0,) * len(dims))
    whole = lambda *dims: pl.BlockSpec(dims, lambda b: (0,) * len(dims), pipeline_mode=pl.Buffered(1))
    final = lambda *dims: pl.BlockSpec(dims, lambda b: (0,) * len(dims))
    vm = pltpu.VMEM
    return pl.pallas_call(
        partial(feed_kernel, devices),
        grid=(count,),
        in_specs=[
            one(length, width),
            one(PAD, width),
            pl.BlockSpec(
                (width, LANES), lambda b: (0, 3 * width // LANES), pipeline_mode=pl.Buffered(1)
            ),
            whole(width, cols),
            one(rows, width),
            one(rows, width),
        ],
        out_specs=[
            one(rows, width),
            one(rows, width),
            one(rows, width),
            final(width, cut),
            final(width, cols + LANES - cut),
        ],
        out_shape=[
            jax.ShapeDtypeStruct((count, rows, width), BF),
            jax.ShapeDtypeStruct((count, rows, width), FL),
            jax.ShapeDtypeStruct((count, rows, width), BF),
            jax.ShapeDtypeStruct((width, cut), BF),
            jax.ShapeDtypeStruct((width, cols + LANES - cut), BF),
        ],
        scratch_shapes=[
            vm((1, hid), FL),
            vm((LANES, width), FL),
            vm((width, LANES), FL),
            vm((width, cols), FL),
            vm((64, width), FL),
            vm((8, hid), FL),
            vm((rows, width), FL),
            vm((rows, width), FL),
            vm((rows, 1), FL),
            vm((rows, width), BF),
            vm((rows, width), FL),
            vm((rows, width), BF),
            vm((rows, hid), BF),
            vm((rows, hid), FL),
            vm((rows, hid), BF),
            vm((rows, width), BF),
            vm((count * PAD, width), BF),
            vm((count * PAD, width), BF),
            vm((count * PAD, width), BF),
            vm((count * PAD, width), BF),
            vm((count * PAD, hid), BF),
            vm((count * PAD, hid), BF),
            vm((width + ONES, length), BF),
            vm((width, length), BF),
        ],
        compiler_params=pltpu.CompilerParams(vmem_limit_bytes=60 << 20),
        name="feed",
    )(tok, state, near, wide, mixed, cot)


def return_kernel(
    qkv_ref,
    pt_ref,
    ptk_ref,
    ptq_ref,
    gm_ref,
    dj_ref,
    kt_ref,
    dpk_ref,
    dsk_ref,
    dqt_ref,
    dk_ref,
    dv_ref,
    s_ref,
    ds_ref,
):
    width = gm_ref.shape[2]
    length = gm_ref.shape[1] - PAD
    group = HALF // HDIM
    parts = length // HALF
    gpad = group * PAD
    pairs = width // (2 * HDIM)
    masks = pair_masks(2 * HDIM)

    def columns(g, which):
        return slice(which * width + g * HALF, which * width + (g + 1) * HALF)

    def features(g):
        return slice(g * HALF, (g + 1) * HALF)

    def memory_keys(g):
        v_mem = spread(qkv_ref[0, length:, columns(g, 2)], group)
        dpk_ref[g * gpad : (g + 1) * gpad, :] = dot(v_mem, gm_ref[0, :length, features(g)], 1, 1)
        kt_ref[features(g), :] = qkv_ref[0, :length, columns(g, 1)].T

    def memory_queries(g):
        do_mem = spread(gm_ref[0, length:, features(g)], group)
        q_mem = spread(qkv_ref[0, length:, columns(g, 0)], group)
        prob = ptq_ref[0, :, g * gpad : (g + 1) * gpad]
        pf = prob.astype(FL)
        t = pf * dot(qkv_ref[0, :, columns(g, 2)], do_mem, 1, 1)
        ds = (t - pf * jnp.sum(t, axis=0, keepdims=True)).astype(BF)
        dv_ref[:, features(g)] = dot(prob, do_mem, 1, 0)
        dk_ref[:, features(g)] = dot(ds, q_mem, 1, 0)
        dq = fold(dot(ds, qkv_ref[0, :, columns(g, 1)], 0, 0), group)
        dj_ref[0, length:, features(g)] = (dq * SCALE).astype(BF)

    def rise(h, part, slot):
        at = (h // 2) * 2 * HDIM
        low, upto = part * HALF, (part + 1) * HALF
        base = part * (part + 1) // 2 * HALF
        own = slice(h * PAD, (h + 1) * PAD)
        vm = qkv_ref[0, :upto, 2 * width + at : 2 * width + at + 2 * HDIM] * masks[h % 2]
        dp = dot(vm, gm_ref[0, low:upto, at : at + 2 * HDIM], 1, 1)
        deltas = []
        for c in range(0, HALF, LANES):
            lanes = slice(c, c + LANES)
            live = low + c + LANES
            t = pt_ref[0, h, base : base + live, lanes].astype(FL) * dp[:live, lanes]
            tm = ptk_ref[0, own, low + c : live].astype(FL) * dpk_ref[own, low + c : live]
            s_ref[slot, :live, lanes] = t
            deltas.append(jnp.sum(t, axis=0, keepdims=True) + jnp.sum(tm, axis=0, keepdims=True))
        return deltas

    def settle(h, part, slot, deltas):
        low, upto = part * HALF, (part + 1) * HALF
        base = part * (part + 1) // 2 * HALF
        own = slice(h * PAD, (h + 1) * PAD)
        keep = (h // 2) % 2
        made, made_mem = [], []
        for c, delta in zip(range(0, HALF, LANES), deltas):
            lanes = slice(c, c + LANES)
            live = low + c + LANES
            pf = pt_ref[0, h, base : base + live, lanes].astype(FL)
            made.append(s_ref[slot, :live, lanes] - pf * delta)
            if live < upto:
                made[-1] = jnp.concatenate([made[-1], jnp.zeros((upto - live, LANES), FL)], axis=0)
            pm = ptk_ref[0, own, low + c : live].astype(FL)
            made_mem.append(pm * (dpk_ref[own, low + c : live] - delta))
        ds_ref[keep, h % 2, base : base + upto, :] = jnp.concatenate(made, axis=1).astype(BF)
        dsk_ref[own, low:upto] = jnp.concatenate(made_mem, axis=1).astype(BF)

    def gather_rows(p, source, other, into):
        lanes = slice(p * 2 * HDIM, (p + 1) * 2 * HDIM)
        rows = [other * masks[side] for side in range(2)]
        for tile in range(parts):
            left, right = [], []
            for side in range(2):
                for part in range(tile, parts):
                    base = part * (part + 1) // 2 * HALF + tile * HALF
                    left.append(source(side, slice(base, base + HALF)))
                    right.append(rows[side][part * HALF : (part + 1) * HALF])
            into[tile * HALF : (tile + 1) * HALF, lanes] += dot(
                jnp.concatenate(left, axis=1), jnp.concatenate(right, axis=0), 1, 0
            )

    def values_back(p):
        lanes = slice(p * 2 * HDIM, (p + 1) * 2 * HDIM)
        gather_rows(p, lambda side, r: pt_ref[0, 2 * p + side, r, :], gm_ref[0, :length, lanes], dv_ref)

    def keys_back(p):
        lanes = slice(p * 2 * HDIM, (p + 1) * 2 * HDIM)
        gather_rows(p, lambda side, r: ds_ref[p % 2, side, r, :], qkv_ref[0, :length, lanes], dk_ref)

    def queries_back(h):
        feat = slice(h * HDIM, (h + 1) * HDIM)
        for part in range(parts):
            low, upto = part * HALF, (part + 1) * HALF
            base = part * (part + 1) // 2 * HALF
            ds = ds_ref[(h // 2) % 2, h % 2, base : base + upto, :]
            dqt_ref[feat, low:upto] = dot(kt_ref[feat, :upto], ds, 1, 0)

    def finish(g):
        own = slice(g * gpad, (g + 1) * gpad)
        k_mem = spread(qkv_ref[0, length:, columns(g, 1)], group)
        dq_t = dqt_ref[features(g), :] + dot(k_mem, dsk_ref[own, :], 0, 0)
        dj_ref[0, :length, features(g)] = (dq_t * SCALE).astype(BF).T
        dv_mem = fold(dot(ptk_ref[0, own, :], gm_ref[0, :length, features(g)], 1, 0), group)
        dk_mem = fold(dot(dsk_ref[own, :], qkv_ref[0, :length, columns(g, 0)], 1, 0), group)
        dj_ref[0, :length, columns(g, 1)] = dk_ref[:length, features(g)].astype(BF)
        dj_ref[0, :length, columns(g, 2)] = dv_ref[:length, features(g)].astype(BF)
        dj_ref[0, length:, columns(g, 1)] = (dk_ref[length:, features(g)] + dk_mem).astype(BF)
        dj_ref[0, length:, columns(g, 2)] = (dv_ref[length:, features(g)] + dv_mem).astype(BF)

    groups = width // HALF
    memory_keys(0)
    units = [(2 * p + side, part) for p in range(pairs) for side in range(2) for part in range(parts)]
    per_pair = 2 * parts
    deltas = {}
    later = []
    for u in range(len(units) + 2):
        if u < len(units):
            deltas[u] = rise(*units[u], u % SLOTS)
        if u >= 2:
            settle(*units[u - 2], (u - 2) % SLOTS, deltas.pop(u - 2))
            if (u - 1) % per_pair == 0:
                p = (u - 1) // per_pair - 1
                later += [(queries_back, 2 * p), (queries_back, 2 * p + 1), (keys_back, p)]
                if p % 2 == 1:
                    later.append((finish, p // 2))
        if u < len(units):
            p, at = u // per_pair, u % per_pair
            if at == 0 and p % 2 == 0:
                memory_queries(p // 2)
            if at == 3:
                values_back(p)
            if at == 2 and p % 2 == 1 and p // 2 + 1 < groups:
                memory_keys(p // 2 + 1)
        if later:
            work, arg = later.pop(0)
            work(arg)
    for work, arg in later:
        work(arg)


def go_back(begin, count, qkv, pt, ptk, ptq, gm):
    rows, width = gm.shape[1:]
    length = rows - PAD
    heads = width // HDIM
    one = lambda *dims: pl.BlockSpec((1,) + dims, lambda b: (b + begin,) + (0,) * len(dims))
    vm = pltpu.VMEM
    return pl.pallas_call(
        return_kernel,
        grid=(count,),
        in_specs=[
            one(rows, 3 * width),
            one(*pt.shape[1:]),
            one(heads * PAD, length),
            one(rows, heads * PAD),
            one(rows, width),
        ],
        out_specs=pl.BlockSpec((1, rows, 3 * width), lambda b: (b, 0, 0)),
        out_shape=jax.ShapeDtypeStruct((count, rows, 3 * width), BF),
        scratch_shapes=[
            vm((width, length), BF),
            vm((heads * PAD, length), FL),
            vm((heads * PAD, length), BF),
            vm((width, length), FL),
            vm((rows, width), FL),
            vm((rows, width), FL),
            vm((SLOTS, length, HALF), FL),
            vm((2, 2, pt.shape[2], HALF), BF),
        ],
        compiler_params=pltpu.CompilerParams(vmem_limit_bytes=48 << 20),
        cost_estimate=pl.CostEstimate(flops=count * 10**10, bytes_accessed=count * 10**7, transcendentals=0),
        name="go_back",
    )(qkv, pt, ptk, ptq, gm)


def weigh_kernel(
    begins,
    tok_ref,
    state_ref,
    one_ref,
    inw_ref,
    *refs,
):
    dj_refs, refs = refs[: len(begins)], refs[len(begins) :]
    gone_ref, gtwo_ref, acc_ref, left_ref, m_in_ref, m_dj_ref, side_ref, memb_ref = refs
    cut = gone_ref.shape[1]
    step = pl.program_id(0)
    last = pl.num_programs(0) - 1
    length, width = tok_ref.shape[1:]
    ends = begins[1:] + [last + 1]

    @pl.when(step == 0)
    def _():
        acc_ref[...] = jnp.zeros_like(acc_ref)
        side_ref[...] = jnp.zeros_like(side_ref)
        memb_ref[...] = inw_ref[:, 3 * width :].astype(FL).T
        left_ref[width:, :] = jnp.ones((ONES, length), BF)

    mem = pl.ds(pl.multiple_of(step * PAD, PAD), PAD)
    m_in_ref[mem, :] = (state_ref[0].astype(FL) + memb_ref[:PAD]).astype(BF)
    side_ref[0:PAD, :] += one_ref[0]
    left_ref[:width, :] = tok_ref[0].T
    for g, dj_ref in enumerate(dj_refs):

        @pl.when((step >= begins[g]) & (step < ends[g]))
        def _(dj_ref=dj_ref):
            m_dj_ref[mem, :] = dj_ref[0, length:, :]
            for j in range(0, 3 * width, FCHUNK):
                c = slice(j, j + FCHUNK)
                acc_ref[:, c] += dot(left_ref[...], dj_ref[0, :length, c], 1, 0)

    @pl.when(step == last)
    def _():
        more = jnp.concatenate([m_in_ref[...].T, jnp.ones((ONES, m_in_ref.shape[0]), BF)], axis=0)
        for j in range(0, 3 * width, FCHUNK):
            c = slice(j, j + FCHUNK)
            acc_ref[:, c] += dot(more, m_dj_ref[:, c], 1, 0)
        gone_ref[...] = acc_ref[:width, :cut].astype(BF)
        gtwo_ref[:, : 3 * width - cut] = acc_ref[:width, cut:].astype(BF)
        back = dot(m_dj_ref[...], inw_ref[:, : 3 * width], 1, 1)
        side_ref[0:PAD, :] += jnp.sum(back.reshape(last + 1, PAD, width), axis=0)
        side_ref[PAD : PAD + 1, :] = acc_ref[width : width + 1, :width]
        side_ref[PAD + 1 : PAD + 2, :] = acc_ref[width : width + 1, 2 * width :]
        gtwo_ref[:, 3 * width - cut :] = side_ref[...].T.astype(BF)


def weigh(tok, state, near, one_grad, djs, begins):
    count, length, width = tok.shape
    rows = length + PAD
    cut = halfway(3 * width + LANES)
    one = lambda *dims: pl.BlockSpec((1,) + dims, lambda b: (b,) + (0,) * len(dims))
    whole = lambda *dims: pl.BlockSpec(dims, lambda b: (0,) * len(dims), pipeline_mode=pl.Buffered(1))
    final = lambda *dims: pl.BlockSpec(dims, lambda b: (0,) * len(dims))
    part = lambda g: pl.BlockSpec(
        (1, rows, 3 * width), lambda b: (jnp.clip(b - begins[g], 0, djs[g].shape[0] - 1), 0, 0)
    )
    vm = pltpu.VMEM
    return pl.pallas_call(
        partial(weigh_kernel, begins),
        grid=(count,),
        in_specs=[
            one(length, width),
            one(PAD, width),
            pl.BlockSpec((1, PAD, width), lambda b: (b, length // PAD, 0)),
            whole(width, 3 * width + LANES),
        ]
        + [part(g) for g in range(len(djs))],
        out_specs=[final(width, cut), final(width, 3 * width + LANES - cut)],
        out_shape=[
            jax.ShapeDtypeStruct((width, cut), BF),
            jax.ShapeDtypeStruct((width, 3 * width + LANES - cut), BF),
        ],
        scratch_shapes=[
            vm((width + ONES, 3 * width), FL),
            vm((width + ONES, length), BF),
            vm((count * PAD, width), BF),
            vm((count * PAD, 3 * width), BF),
            vm((LANES, width), FL),
            vm((LANES, width), FL),
        ],
        compiler_params=pltpu.CompilerParams(vmem_limit_bytes=48 << 20),
        cost_estimate=pl.CostEstimate(flops=count * 10**9, bytes_accessed=count * 3 * 10**6, transcendentals=0),
        name="weigh",
    )(tok, state, one_grad, near, *djs)


def descend_kernel(one_ref, dj_ref, inw_ref, grad_ref):
    width = one_ref.shape[2]
    grad_ref[0] = one_ref[0] + dot(dj_ref[0], inw_ref[:, : 3 * width], 1, 1)


def descend(total, begin, one_grad, dj, near, into):
    count, rows, wide = dj.shape
    width = one_grad.shape[2]
    length = rows - PAD
    shift = lambda *dims: pl.BlockSpec((1,) + dims, lambda b: (b + begin, 0, 0))
    kept = () if into is None else (into,)

    def kernel(one_ref, dj_ref, inw_ref, *rest):
        descend_kernel(one_ref, dj_ref, inw_ref, rest[-1])

    return pl.pallas_call(
        kernel,
        grid=(count,),
        in_specs=[
            shift(length, width),
            pl.BlockSpec((1, length, wide), lambda b: (b, 0, 0)),
            pl.BlockSpec((width, wide + LANES), lambda b: (0, 0), pipeline_mode=pl.Buffered(1)),
        ]
        + [pl.BlockSpec(memory_space=pl.ANY)] * len(kept),
        out_specs=shift(length, width),
        out_shape=jax.ShapeDtypeStruct((total, length, width), FL),
        input_output_aliases={3: 0} if kept else {},
        compiler_params=pltpu.CompilerParams(vmem_limit_bytes=32 << 20),
        cost_estimate=pl.CostEstimate(flops=count * 10**9, bytes_accessed=count * 4 * 10**6, transcendentals=0),
        name="descend",
    )(one_grad, dj, near, *kept)


def pack_kernel(in_ref, up_ref, down_ref, out_ref, vec_ref, bias_ref, mem_ref, near_ref, far_ref, flip_ref):
    shard, cols = in_ref.shape
    hid, width = up_ref.shape[1], out_ref.shape[1]
    flip_ref[...] = jnp.zeros_like(flip_ref)
    flip_ref[PAD : PAD + 8, :shard] = vec_ref[...]
    flip_ref[...] = flip_ref[...].T
    flip_ref[:shard, : mem_ref.shape[1]] = mem_ref[...]
    flip_ref[0:1, BIAS : BIAS + bias_ref.shape[1]] = bias_ref[...]
    near_ref[:, :cols] = in_ref[...].astype(BF)
    near_ref[:, cols:] = flip_ref[:shard].astype(BF)
    far_ref[:, :hid] = up_ref[...].astype(BF)
    far_ref[:, hid : 2 * hid] = down_ref[...].astype(BF)
    far_ref[:, 2 * hid :] = out_ref[...].astype(BF)


def pack(in_w, up_w, down_t, out_t, vectors, bias, mem_t):
    shard, cols = in_w.shape
    wide = 2 * up_w.shape[1] + out_t.shape[1]
    return pl.pallas_call(
        pack_kernel,
        out_shape=[
            jax.ShapeDtypeStruct((shard, cols + LANES), BF),
            jax.ShapeDtypeStruct((shard, wide), BF),
        ],
        scratch_shapes=[pltpu.VMEM((LANES, LANES), FL)],
        name="pack",
    )(in_w, up_w, down_t, out_t, vectors, bias, mem_t)


def square_kernel(cols, *refs):
    held_refs, got_refs, (far_ref, near_ref, sum_ref) = refs[:2], refs[2:4], refs[4:]
    at = 0
    for held_ref, got_ref in zip(held_refs, got_refs):
        size = held_ref.shape[1]
        near_ref[:, at : at + size] = held_ref[...] + got_ref[...].astype(FL)
        at += size
    wide = far_ref.shape[1] - LANES
    near, far = near_ref[:, :cols], far_ref[:, :wide]
    side = near_ref[:, cols:] + far_ref[:, wide:]
    total = jnp.sum(near * near) + jnp.sum(far * far) + jnp.sum(side * side)
    sum_ref[...] = jnp.full(sum_ref.shape, total, FL)


def adam_kernel(sizes, rates, decays, near_ref, far_ref, total_ref, *refs):
    cols, hid, width = sizes
    state_refs, new_refs, norm_ref, flip_ref = refs[:21], refs[21:42], refs[42], refs[43]
    shard = near_ref.shape[0]
    norm = jnp.sqrt(total_ref[...])
    norm_ref[...] = norm[0:1, 0:1]
    factor = (1.0 / jnp.maximum(norm, 1.0))[0:1, 0:1]
    side = near_ref[:, cols:] + far_ref[:, 2 * hid + width :]
    flip_ref[...] = jnp.zeros_like(flip_ref)
    flip_ref[:shard] = side
    turned = flip_ref[...].T
    bias = pltpu.roll(side, LANES - BIAS, 1)
    grads = (
        near_ref[:, :cols],
        far_ref[:, 2 * hid : 2 * hid + width],
        far_ref[:, :hid],
        far_ref[:, hid : 2 * hid],
        turned[PAD : PAD + 8, :shard],
        bias[0:1, : state_refs[15].shape[1]],
        side[:, : state_refs[18].shape[1]],
    )
    correction = 1.0 - 0.5**STEP
    for i in range(7):
        weight, first, second = (state_refs[3 * i + k][...] for k in range(3))
        grad = grads[i] * factor
        first_new = 0.5 * first + 0.5 * grad
        second_new = 0.5 * second + 0.5 * grad * grad
        step = first_new / correction / (jnp.sqrt(second_new / correction) + 1e-08)
        new_refs[3 * i][...] = weight - rates[i] * (step + decays[i] * weight)
        new_refs[3 * i + 1][...] = first_new
        new_refs[3 * i + 2][...] = second_new


def exchange(x, bit, devices):
    return lax.ppermute(x, AXES, [(i, i ^ bit) for i in range(devices)])


def beside(got, sent, work):
    if work is None:
        return got, None
    made = work(lambda value: lax.optimization_barrier((value, sent))[0])
    return lax.optimization_barrier((got, made))


def gather(x, devices, index, works):
    rows, cols = x.shape
    held = x[None]
    results = []
    bits = devices.bit_length() - 1
    for step in range(bits):
        bit = devices >> (step + 1)
        got = exchange(held, bit, devices)
        got, made = beside(got, held, works[step] if step < len(works) else None)
        results.append(made)
        upper = (index & bit) != 0
        held = jnp.stack([jnp.where(upper, got, held), jnp.where(upper, held, got)], axis=1)
        held = held.reshape(-1, rows, cols)
    return held.reshape(devices * rows, cols), [made for made in results if made is not None]


def halve(held, got, place, upper):
    total = held if got is None else held.astype(FL) + got.astype(FL)
    low, high = (lax.index_in_dim(total, i, place, keepdims=False) for i in range(2))
    return jnp.where(upper, high, low), jnp.where(upper, low, high).astype(BF)


def scatter_sum(halves, devices, index, works):
    rows = halves[0].shape[0] // devices
    bits = devices.bit_length() - 1
    orders = [list(range(bits)) for _ in range(2)]
    if bits > 2:
        orders[1][1:3] = [2, 1]
    held = [half.reshape((2,) * bits + (rows, -1)) for half in halves]
    got = [None, None]
    results = []
    for step in range(bits):
        send = [None, None]
        for half, order in enumerate(orders):
            bit = order[step]
            place = sum(1 for other in order[step:] if other > bit)
            upper = (index & (1 << bit)) != 0
            held[half], send[half] = halve(held[half], got[half], place, upper)
        if step < 3:
            got = [exchange(value, 1 << order[step], devices) for value, order in zip(send, orders)]
            got, made = beside(got, send, works[step] if step < len(works) else None)
        else:
            sent = jnp.concatenate(send, axis=-1)
            both, made = beside(exchange(sent, 1 << orders[0][step], devices), sent, works[step] if step < len(works) else None)
            cut = send[0].shape[-1]
            got = [both[..., :cut], both[..., cut:]]
        results.append(made)
    return [value.astype(FL).reshape(rows, -1) for value in held], [value.reshape(rows, -1) for value in got], results


def butterfly(x, devices):
    for step in range(devices.bit_length() - 1):
        x = x + exchange(x, 1 << step, devices)
    return x


def per_device(
    devices,
    tokens,
    memory_state,
    cotangent,
    in_weight,
    in_first,
    in_second,
    out_weight,
    out_first,
    out_second,
    up_weight,
    up_first,
    up_second,
    down_weight,
    down_first,
    down_second,
    vectors,
    vectors_first,
    vectors_second,
    up_bias,
    up_bias_first,
    up_bias_second,
    memory_embed,
    memory_first,
    memory_second,
):
    index = lax.axis_index(AXES)
    micro, local, length, width = tokens.shape
    count = micro * local
    extra = memory_state.shape[2]
    shard = in_weight.shape[0]
    hid = up_weight.shape[1]
    per_bias = up_bias.shape[0] // shard

    near, far = pack(
        in_weight,
        up_weight,
        down_weight.T,
        out_weight.T,
        vectors,
        up_bias.reshape(1, -1),
        memory_embed.T,
    )
    wide = lax.all_gather(far, AXES, axis=0, tiled=True)

    def pad_state(tie):
        rows = tie(memory_state).reshape(count, extra, width)
        return jnp.pad(rows, ((0, 0), (0, PAD - extra), (0, 0)))

    def align(tie):
        cot = tie(cotangent).reshape(count, extra + length, width)
        return jnp.concatenate(
            [cot[:, extra:], cot[:, :extra], jnp.zeros((count, PAD - extra, width), BF)], axis=1
        )

    near, (state, cot) = gather(near, devices, index, [pad_state, None, None, align])

    tok = tokens.reshape(count, length, width)

    qkv, pt, ptk, ptq, mixed = attend(extra, tok, state, near)
    out, one_grad, gm, *gwide = feed(devices, tok, state, near, wide, mixed, cot)

    def split(sizes):
        begins = [0]
        for size in sizes:
            begins.append(begins[-1] + size)
        return list(zip(begins, sizes))

    def back(begin, size):
        return lambda tie: go_back(begin, size, tie(qkv), pt, ptk, ptq, gm)

    runs = split(BACK) if sum(BACK) == count else split([count])
    held, got, djs = scatter_sum(gwide, devices, index, [back(*run) for run in runs])
    gfar = jnp.concatenate([mine + extra.astype(FL) for mine, extra in zip(held, got)], axis=1)
    djs = djs[: len(runs)]
    gin = weigh(tok, state, near, one_grad, djs, [begin for begin, _ in runs])
    grads = []

    def down(i):
        def work(tie):
            into = grads[-1] if grads else None
            grads.append(descend(count, runs[i][0], one_grad, tie(djs[i]), near, into))
            return grads[-1]

        return work

    def order(tie):
        rows = tie(out)
        rows = jnp.concatenate([rows[:, length : length + extra], rows[:, :length]], axis=1)
        return rows.reshape(micro, local, extra + length, width).transpose(0, 2, 1, 3)

    works = [down(i) for i in range(len(runs))] + [order]
    held, got, made = scatter_sum(gin, devices, index, works)
    input_grad = made[len(runs) - 1].reshape(micro, local, length, width)

    gnear, squares = pl.pallas_call(
        partial(square_kernel, 3 * width),
        out_shape=[
            jax.ShapeDtypeStruct((shard, 3 * width + LANES), FL),
            jax.ShapeDtypeStruct((8, LANES), FL),
        ],
        name="squares",
    )(*held, *got, gfar)
    squares = butterfly(squares, devices)
    output = made[len(runs)].transpose(0, 2, 1, 3)
    total_rows = extra + length
    rates = (
        0.5 * width ** (-0.5),
        0.5 * (width * 32 // total_rows) ** (-0.5),
        0.5 * width ** (-0.5),
        0.5 * hid ** (-0.5),
        0.1,
        0.1,
        0.5,
    )
    decays = (0.1, 0.1, 0.1, 0.1, 0.0, 0.0, 0.0)
    same = lambda value: value
    turn = lambda value: value.T
    flat = lambda value: value.reshape(1, -1)
    views = (same, turn, same, turn, same, flat, turn)
    states = (
        (in_weight, in_first, in_second),
        (out_weight, out_first, out_second),
        (up_weight, up_first, up_second),
        (down_weight, down_first, down_second),
        (vectors, vectors_first, vectors_second),
        (up_bias, up_bias_first, up_bias_second),
        (memory_embed, memory_first, memory_second),
    )
    held = [view(value) for view, group in zip(views, states) for value in group]
    *new, norm = pl.pallas_call(
        partial(adam_kernel, (3 * width, hid, width), rates, decays),
        out_shape=[jax.ShapeDtypeStruct(value.shape, FL) for value in held]
        + [jax.ShapeDtypeStruct((1, 1), FL)],
        scratch_shapes=[pltpu.VMEM((LANES, LANES), FL)],
        name="adam",
    )(gnear, gfar, squares, *held)
    back_views = (same, turn, same, turn, same, lambda value: value.reshape(-1), turn)
    results = [back_views[i // 3](value) for i, value in enumerate(new)]
    return (output, input_grad, *results, norm.reshape(()))


def solution(mesh):
    blocks = P(None, AXES, None, None)
    lead = P(AXES, None)
    trail = P(None, AXES)
    flat = P(AXES)
    weights = (lead,) * 3 + (trail,) * 3 + (lead,) * 3 + (trail,) * 6 + (flat,) * 3 + (trail,) * 3
    devices = mesh.shape["dp"] * mesh.shape["fsdp"]
    return jax.shard_map(
        partial(per_device, devices),
        mesh=mesh,
        in_specs=(blocks,) * 3 + weights,
        out_specs=(blocks,) * 2 + weights + (P(),),
        check_vma=False,
    )
```

```python
from functools import partial

import jax
import jax.numpy as jnp
from jax import lax
from jax.experimental import pallas as pl
from jax.experimental.pallas import tpu as pltpu
from jax.sharding import PartitionSpec as P

STEP = 7
HDIM = 64
PAD = 32
HALF = 256
FCHUNK = 256
ROWS = 32
BF = jnp.bfloat16
FL = jnp.float32
AXES = ("dp", "fsdp")
NEG = -1e30
EPS = 1e-05
SCALE = HDIM ** (-0.5)
LANES = 128
BIAS = 64
SLOTS = 4
PLAN_MORE = (0, 2, 4, 5)
PLAN_LAST = (2, 4, 7, 5)
CUT = 3
ONES = 16
BACK = (2, 4, 2)


def dot(a, b, ca, cb):
    return lax.dot_general(a, b, (((ca,), (cb,)), ((), ())), preferred_element_type=FL)


def head_mask(rows, width):
    row = lax.broadcasted_iota(jnp.int32, (rows, width), 0) // PAD
    col = lax.broadcasted_iota(jnp.int32, (rows, width), 1) // HDIM
    return row == col


def spread(x, heads):
    tiled = jnp.concatenate([x.astype(FL)] * heads, axis=0)
    return jnp.where(head_mask(*tiled.shape), tiled, 0.0).astype(BF)


def fold(y, heads):
    own = jnp.where(head_mask(*y.shape), y, 0.0)
    return sum(own[h * PAD : (h + 1) * PAD] for h in range(heads))


def pair_masks(width):
    col = lax.broadcasted_iota(jnp.int32, (1, width), 1)
    low = jnp.where(col < HDIM, 1.0, 0.0)
    return low.astype(BF), (1.0 - low).astype(BF)


def attend_kernel(
    extra,
    tok_ref,
    state_ref,
    first_ref,
    first_state_ref,
    inw_ref,
    qkv_ref,
    pt_ref,
    ptk_ref,
    ptq_ref,
    mixed_ref,
    vt_ref,
    sk_ref,
    ot_ref,
    side_ref,
    inp_ref,
    s_ref,
    ahead_ref,
):
    length, width = tok_ref.shape[1:]
    rows = length + PAD
    group = HALF // HDIM
    parts = length // HALF
    gpad = group * PAD
    diag = lax.broadcasted_iota(jnp.int32, (LANES, LANES), 0) <= lax.broadcasted_iota(
        jnp.int32, (LANES, LANES), 1
    )
    key_live = lax.broadcasted_iota(jnp.int32, (gpad, 1), 0) % PAD < extra
    place_live = lax.broadcasted_iota(jnp.int32, (rows, 1), 0) < length + extra
    masks = pair_masks(2 * HDIM)

    def columns(g, which):
        return slice(which * width + g * HALF, which * width + (g + 1) * HALF)

    def ahead(which):
        return slice(which * HALF, (which + 1) * HALF)

    def take(source, source_state):
        inp_ref[:length] = source[0]
        inp_ref[length:] = (source_state[0].astype(FL) + side_ref[:PAD]).astype(BF)

    def project(g, which):
        feat = slice(g * HALF, (g + 1) * HALF)
        made = dot(inp_ref[...], inw_ref[:, columns(g, which)], 1, 0)
        if which == 0:
            made = (made + side_ref[PAD : PAD + 1, feat]) * SCALE
        if which == 2:
            made = made + side_ref[PAD + 1 : PAD + 2, feat]
        made = made.astype(BF)
        if g:
            qkv_ref[0, :, columns(g, which)] = made
        else:
            ahead_ref[:, ahead(which)] = made
        if which == 2:
            vt_ref[feat, :] = made[:length].T

    def memory_keys(g):
        if g:
            mem, query = qkv_ref[0, length:, columns(g, 1)], qkv_ref[0, :length, columns(g, 0)]
        else:
            mem, query = ahead_ref[length:, ahead(1)], ahead_ref[:length, ahead(0)]
        made = dot(spread(mem, group), query, 1, 1)
        sk_ref[g * gpad : (g + 1) * gpad, :] = jnp.where(key_live, made, NEG)

    def memory_queries(g):
        q_mem = spread(qkv_ref[0, length:, columns(g, 0)], group)
        sq = jnp.where(place_live, dot(qkv_ref[0, :, columns(g, 1)], q_mem, 1, 1), NEG)
        eq = jnp.exp(sq - jnp.max(sq, axis=0, keepdims=True))
        probs = (eq * (1.0 / jnp.sum(eq, axis=0, keepdims=True))).astype(BF)
        ptq_ref[0, :, g * gpad : (g + 1) * gpad] = probs
        om = dot(probs, qkv_ref[0, :, columns(g, 2)], 0, 0)
        mixed_ref[0, length:, g * HALF : (g + 1) * HALF] = fold(om, group).astype(BF)

    @pl.when(pl.program_id(0) == 0)
    def _():
        side_ref[...] = inw_ref[:, 3 * width :].astype(FL).T
        take(first_ref, first_state_ref)
        for which in range(3):
            project(0, which)
        memory_keys(0)

    def score(h, part, slot):
        at = (h // 2) * 2 * HDIM
        low, upto = part * HALF, (part + 1) * HALF
        qp = qkv_ref[0, low:upto, at : at + 2 * HDIM]
        km = qkv_ref[0, :upto, width + at : width + at + 2 * HDIM] * masks[h % 2]
        s = dot(km, qp, 1, 1)
        tops = []
        for c in range(0, HALF, LANES):
            lanes = slice(c, c + LANES)
            edge = jnp.where(diag, s[low + c : low + c + LANES, lanes], NEG)
            s_ref[slot, low + c : low + c + LANES, lanes] = edge
            top = jnp.maximum(
                jnp.max(edge, axis=0, keepdims=True),
                jnp.max(sk_ref[h * PAD : (h + 1) * PAD, low + c : low + c + LANES], axis=0, keepdims=True),
            )
            if low + c:
                s_ref[slot, : low + c, lanes] = s[: low + c, lanes]
                top = jnp.maximum(top, jnp.max(s[: low + c, lanes], axis=0, keepdims=True))
            tops.append(top)
        return tops

    def soften(h, part, slot, tops):
        low, upto = part * HALF, (part + 1) * HALF
        own = slice(h * PAD, (h + 1) * PAD)
        base = part * (part + 1) // 2 * HALF
        made, made_mem = [], []
        for c, top in zip(range(0, HALF, LANES), tops):
            lanes = slice(c, c + LANES)
            live = low + c + LANES
            e = jnp.exp(s_ref[slot, :live, lanes] - top)
            e_mem = jnp.exp(sk_ref[own, low + c : live] - top)
            total = jnp.sum(e, axis=0, keepdims=True) + jnp.sum(e_mem, axis=0, keepdims=True)
            share = 1.0 / total
            made.append(e * share)
            made_mem.append(e_mem * share)
            if live < upto:
                made[-1] = jnp.concatenate([made[-1], jnp.zeros((upto - live, LANES), FL)], axis=0)
        pt_ref[0, h, base : base + upto, :] = jnp.concatenate(made, axis=1).astype(BF)
        ptk_ref[0, own, low:upto] = jnp.concatenate(made_mem, axis=1).astype(BF)

    def mix(h, part):
        upto = (part + 1) * HALF
        base = part * (part + 1) // 2 * HALF
        feat = slice(h * HDIM, (h + 1) * HDIM)
        ot_ref[feat, part * HALF : upto] = dot(
            vt_ref[feat, :upto], pt_ref[0, h, base : base + upto, :], 1, 0
        )

    def finish(g):
        v_mem = spread(qkv_ref[0, length:, columns(g, 2)], group)
        feat = slice(g * HALF, (g + 1) * HALF)
        om_t = ot_ref[feat, :] + dot(v_mem, ptk_ref[0, g * gpad : (g + 1) * gpad, :], 0, 0)
        mixed_ref[0, :length, feat] = om_t.astype(BF).T

    groups = width // HALF
    units = [(g * group + i, part) for g in range(groups) for i in range(group) for part in range(parts)]
    per_group = group * parts
    for which in range(3):
        qkv_ref[0, :, columns(0, which)] = ahead_ref[:, ahead(which)]
    works = {}
    for g in range(groups):
        at = g * per_group
        more = g + 1 < groups
        plan = PLAN_MORE if more else PLAN_LAST
        works.setdefault(at + 1, []).append((memory_queries, g))
        if g:
            works.setdefault(at + 3, []).append((finish, g - 1))
        if not more:
            works.setdefault(at, []).append((take, tok_ref, state_ref))
        for which in range(3):
            works.setdefault(at + plan[which], []).append((project, g + 1 if more else 0, which))
        works.setdefault(at + plan[3], []).append((memory_keys, g + 1 if more else 0))
    tops = {}
    for u in range(len(units) + 3):
        if u < len(units):
            tops[u] = score(*units[u], u % SLOTS)
        if 2 <= u <= len(units) + 1:
            soften(*units[u - 2], (u - 2) % SLOTS, tops.pop(u - 2))
        if u >= 3:
            mix(*units[u - 3])
        for work, *given in works.get(u, ()):
            work(*given)
    finish(groups - 1)


def attend(extra, tok, state, near):
    count, length, width = tok.shape
    heads = width // HDIM
    rows = length + PAD
    parts = length // HALF
    ptrows = parts * (parts + 1) // 2 * HALF
    one = lambda *dims: pl.BlockSpec((1,) + dims, lambda b: (b,) + (0,) * len(dims))
    after = lambda *dims: pl.BlockSpec((1,) + dims, lambda b: (jnp.minimum(b + 1, count - 1), 0, 0))
    whole = lambda *dims: pl.BlockSpec(dims, lambda b: (0,) * len(dims), pipeline_mode=pl.Buffered(1))
    return pl.pallas_call(
        partial(attend_kernel, extra),
        grid=(count,),
        in_specs=[
            after(length, width),
            after(PAD, width),
            pl.BlockSpec((1, length, width), lambda b: (0, 0, 0), pipeline_mode=pl.Buffered(1)),
            pl.BlockSpec((1, PAD, width), lambda b: (0, 0, 0), pipeline_mode=pl.Buffered(1)),
            whole(width, 3 * width + LANES),
        ],
        out_specs=[
            one(rows, 3 * width),
            one(heads, ptrows, HALF),
            one(heads * PAD, length),
            one(rows, heads * PAD),
            one(rows, width),
        ],
        out_shape=[
            jax.ShapeDtypeStruct((count, rows, 3 * width), BF),
            jax.ShapeDtypeStruct((count, heads, ptrows, HALF), BF),
            jax.ShapeDtypeStruct((count, heads * PAD, length), BF),
            jax.ShapeDtypeStruct((count, rows, heads * PAD), BF),
            jax.ShapeDtypeStruct((count, rows, width), BF),
        ],
        scratch_shapes=[
            pltpu.VMEM((width, length), BF),
            pltpu.VMEM((heads * PAD, length), FL),
            pltpu.VMEM((width, length), FL),
            pltpu.VMEM((LANES, width), FL),
            pltpu.VMEM((rows, width), BF),
            pltpu.VMEM((SLOTS, length, HALF), FL),
            pltpu.VMEM((rows, 3 * HALF), BF),
        ],
        compiler_params=pltpu.CompilerParams(vmem_limit_bytes=56 << 20),
        name="attend",
    )(tok, state, tok, state, near)


def norm_rows(x):
    center = x - jnp.mean(x, axis=-1, keepdims=True)
    rstd = lax.rsqrt(jnp.mean(center * center, axis=-1, keepdims=True) + EPS)
    return center * rstd, rstd


def norm_back(grad, normed, rstd, gain):
    scaled = grad * gain
    return rstd * (
        scaled
        - jnp.mean(scaled, axis=-1, keepdims=True)
        - normed * jnp.mean(scaled * normed, axis=-1, keepdims=True)
    )


def by_eight(x):
    return jnp.sum(x.reshape(x.shape[0] // 8, 8, x.shape[1]), axis=0)


def feed_kernel(
    devices,
    tok_ref,
    state_ref,
    small_ref,
    wide_ref,
    mixed_ref,
    cot_ref,
    out_ref,
    one_ref,
    gm_ref,
    gone_ref,
    gtwo_ref,
    upb_ref,
    side_ref,
    gside_ref,
    acc_ref,
    sums_ref,
    upb_sum_ref,
    att_ref,
    n1_ref,
    r1_ref,
    low_ref,
    g2_ref,
    gb_ref,
    hidden_ref,
    slope_ref,
    gpre_ref,
    ga_ref,
    m_low_ref,
    m_gb_ref,
    m_ga_ref,
    m_mixed_ref,
    m_hidden_ref,
    m_gpre_ref,
    low_t_ref,
    gb_t_ref,
):
    step = pl.program_id(0)
    last = pl.num_programs(0) - 1
    length, width = tok_ref.shape[1:]
    hid = upb_ref.shape[1]
    rows = length + PAD
    shard, per = width // devices, hid // devices
    up = slice(0, hid)
    down = slice(hid, 2 * hid)
    outw = slice(2 * hid, 2 * hid + width)

    @pl.when(step == 0)
    def _():
        acc_ref[...] = jnp.zeros_like(acc_ref)
        sums_ref[...] = jnp.zeros_like(sums_ref)
        upb_sum_ref[...] = jnp.zeros_like(upb_sum_ref)
        gpre_ref[...] = jnp.zeros_like(gpre_ref)
        low_t_ref[:width] = jnp.zeros((width, length), BF)
        low_t_ref[width:] = jnp.ones((ONES, length), BF)
        gside_ref[...] = small_ref[...].astype(FL)
        side_ref[...] = gside_ref[...].T
        for i in range(devices):
            upb_ref[:, i * per : (i + 1) * per] = gside_ref[i * shard : i * shard + 1, BIAS : BIAS + per]

    def put(at, value):
        cut = gone_ref.shape[1]
        if at < cut:
            gone_ref[:, at : at + value.shape[1]] = value.astype(BF)
        else:
            gtwo_ref[:, at - cut : at - cut + value.shape[1]] = value.astype(BF)

    def up_piece(j):
        c = slice(j, j + FCHUNK)
        made = dot(low_t_ref[...], gpre_ref[:length, c], 1, 0)
        acc_ref[:, c] += made[:width]
        upb_sum_ref[:, c] += made[width : width + 8]

    def down_piece(j):
        c = slice(j, j + FCHUNK)
        d = slice(hid + j, hid + j + FCHUNK)
        acc_ref[:, d] += dot(gb_t_ref[...], hidden_ref[:length, c], 1, 0)

    pieces = range(0, hid, FCHUNK)
    chunks = range(0, rows, ROWS)
    fills = [(up_piece, j) for j in pieces]

    def weave(stage, sums, works):
        totals = None
        done = 0
        for i, at in enumerate(chunks):
            made = stage(slice(at, at + ROWS))
            totals = made if totals is None else [x + y for x, y in zip(totals, made)]
            while done < len(works) and done * len(chunks) < (i + 1) * len(works):
                work, arg = works[done]
                work(arg)
                done += 1
        for at, total in zip(sums, totals or ()):
            sums_ref[8 * at : 8 * at + 8] += total

    att_ref[...] = dot(mixed_ref[0], wide_ref[:, outw], 1, 1)
    bias_att, bias_ffn = side_ref[PAD + 2 : PAD + 3], side_ref[PAD + 3 : PAD + 4]
    gain_one, shift_one, gain_two, shift_two = (side_ref[PAD + i : PAD + i + 1] for i in range(4, 8))

    shift_ffn = shift_one + bias_ffn

    def norm_one(r):
        if r.start < length:
            full = tok_ref[0, r, :].astype(FL)
        else:
            full = state_ref[0].astype(FL) + side_ref[:PAD]
        normed, rstd = norm_rows(full + (att_ref[r, :] + bias_att))
        n1_ref[r, :] = normed
        r1_ref[r, :] = rstd
        low_ref[r, :] = (normed * gain_one + shift_one).astype(BF)
        return []

    weave(norm_one, (), fills[:CUT])

    root = 0.7978845608
    for j in pieces:
        c = slice(j, j + FCHUNK)
        v = dot(low_ref[...], wide_ref[:, c], 1, 0) + upb_ref[:, c]
        square = v * v
        half = 0.5 + 0.5 * jnp.tanh(v * (root + (root * 0.044715) * square))
        act = v * half
        hidden_ref[:, c] = act.astype(BF)
        slope_ref[:, c] = half + (act * (1.0 - half)) * (2 * root + (6 * root * 0.044715) * square)

    att_ref[...] = dot(hidden_ref[...], wide_ref[:, down], 1, 1)

    def norm_two(r):
        normed, rstd = norm_rows(n1_ref[r, :] * gain_one + (att_ref[r, :] + shift_ffn))
        out_ref[0, r, :] = (normed * gain_two + shift_two).astype(BF)
        cot = cot_ref[0, r, :].astype(FL)
        back = norm_back(cot, normed, rstd, gain_two)
        g2_ref[r, :] = back
        low = back.astype(BF)
        gb_ref[r, :] = low
        return [by_eight(low.astype(FL)), by_eight(cot * normed), by_eight(cot)]

    weave(norm_two, (3, 6, 7), fills[CUT:])
    gb_t_ref[...] = gb_ref[:length].T
    low_t_ref[:width] = low_ref[:length].T

    for j in pieces:
        c = slice(j, j + FCHUNK)
        d = slice(hid + j, hid + j + FCHUNK)
        gpre = (dot(gb_ref[...], wide_ref[:, d], 1, 0) * slope_ref[:, c]).astype(BF)
        gpre_ref[:, c] = gpre

    att_ref[...] = dot(gpre_ref[...], wide_ref[:, up], 1, 1)

    def norm_last(r):
        g1 = g2_ref[r, :] + att_ref[r, :]
        normed = n1_ref[r, :]
        back = norm_back(g1, normed, r1_ref[r, :], gain_one)
        one_ref[0, r, :] = back
        low = back.astype(BF)
        ga_ref[r, :] = low
        return [by_eight(low.astype(FL)), by_eight(g1 * normed), by_eight(g1)]

    weave(norm_last, (2, 4, 5), [(down_piece, j) for j in pieces])

    gm_ref[0] = dot(ga_ref[...], wide_ref[:, outw], 1, 0).astype(BF)
    acc_ref[:, outw] += dot(ga_ref[:length], mixed_ref[0, :length], 0, 0)

    mem = pl.ds(pl.multiple_of(step * PAD, PAD), PAD)
    m_low_ref[mem, :] = low_ref[length:, :]
    m_gb_ref[mem, :] = gb_ref[length:, :]
    m_ga_ref[mem, :] = ga_ref[length:, :]
    m_mixed_ref[mem, :] = mixed_ref[0, length:, :]
    m_hidden_ref[mem, :] = hidden_ref[length:, :]
    m_gpre_ref[mem, :] = gpre_ref[length:, :]

    @pl.when(step == last)
    def _():
        more = jnp.concatenate([m_low_ref[...].T, jnp.ones((ONES, m_low_ref.shape[0]), BF)], axis=0)
        left_low = jnp.concatenate([low_t_ref[...], more], axis=1)
        left_gb = m_gb_ref[...].T
        for j in pieces:
            c = slice(j, j + FCHUNK)
            d = slice(hid + j, hid + j + FCHUNK)
            right = jnp.concatenate([gpre_ref[:length, c], m_gpre_ref[:, c]], axis=0)
            made = dot(left_low, right, 1, 0)
            put(c.start, acc_ref[:, c] + made[:width])
            upb_sum_ref[:, c] += made[width : width + 8]
            put(d.start, acc_ref[:, d] + dot(left_gb, m_hidden_ref[:, c], 1, 0))
        put(2 * hid, acc_ref[:, outw] + dot(m_ga_ref[...], m_mixed_ref[...], 0, 0))
        side_ref[...] = jnp.zeros_like(side_ref)
        for i in range(8):
            side_ref[PAD + i : PAD + i + 1] = jnp.sum(sums_ref[8 * i : 8 * i + 8], axis=0, keepdims=True)
        gside_ref[...] = side_ref[...].T
        bias = upb_sum_ref[0:1]
        for i in range(devices):
            piece = bias[:, i * per : (i + 1) * per]
            gside_ref[i * shard : i * shard + 1, BIAS : BIAS + per] = piece
        put(2 * hid + width, gside_ref[...])


def halfway(cols):
    return cols // (2 * LANES) * LANES


def feed(devices, tok, state, near, wide, mixed, cot):
    count, length, width = tok.shape
    rows = length + PAD
    cols = wide.shape[1]
    hid = (cols - width) // 2
    cut = halfway(cols + LANES)
    one = lambda *dims: pl.BlockSpec((1,) + dims, lambda b: (b,) + (0,) * len(dims))
    whole = lambda *dims: pl.BlockSpec(dims, lambda b: (0,) * len(dims), pipeline_mode=pl.Buffered(1))
    final = lambda *dims: pl.BlockSpec(dims, lambda b: (0,) * len(dims))
    vm = pltpu.VMEM
    return pl.pallas_call(
        partial(feed_kernel, devices),
        grid=(count,),
        in_specs=[
            one(length, width),
            one(PAD, width),
            pl.BlockSpec(
                (width, LANES), lambda b: (0, 3 * width // LANES), pipeline_mode=pl.Buffered(1)
            ),
            whole(width, cols),
            one(rows, width),
            one(rows, width),
        ],
        out_specs=[
            one(rows, width),
            one(rows, width),
            one(rows, width),
            final(width, cut),
            final(width, cols + LANES - cut),
        ],
        out_shape=[
            jax.ShapeDtypeStruct((count, rows, width), BF),
            jax.ShapeDtypeStruct((count, rows, width), FL),
            jax.ShapeDtypeStruct((count, rows, width), BF),
            jax.ShapeDtypeStruct((width, cut), BF),
            jax.ShapeDtypeStruct((width, cols + LANES - cut), BF),
        ],
        scratch_shapes=[
            vm((1, hid), FL),
            vm((LANES, width), FL),
            vm((width, LANES), FL),
            vm((width, cols), FL),
            vm((64, width), FL),
            vm((8, hid), FL),
            vm((rows, width), FL),
            vm((rows, width), FL),
            vm((rows, 1), FL),
            vm((rows, width), BF),
            vm((rows, width), FL),
            vm((rows, width), BF),
            vm((rows, hid), BF),
            vm((rows, hid), FL),
            vm((rows, hid), BF),
            vm((rows, width), BF),
            vm((count * PAD, width), BF),
            vm((count * PAD, width), BF),
            vm((count * PAD, width), BF),
            vm((count * PAD, width), BF),
            vm((count * PAD, hid), BF),
            vm((count * PAD, hid), BF),
            vm((width + ONES, length), BF),
            vm((width, length), BF),
        ],
        compiler_params=pltpu.CompilerParams(vmem_limit_bytes=60 << 20),
        name="feed",
    )(tok, state, near, wide, mixed, cot)


def return_kernel(
    qkv_ref,
    pt_ref,
    ptk_ref,
    ptq_ref,
    gm_ref,
    dj_ref,
    kt_ref,
    dpk_ref,
    dsk_ref,
    dqt_ref,
    dk_ref,
    dv_ref,
    s_ref,
    ds_ref,
):
    width = gm_ref.shape[2]
    length = gm_ref.shape[1] - PAD
    group = HALF // HDIM
    parts = length // HALF
    gpad = group * PAD
    pairs = width // (2 * HDIM)
    masks = pair_masks(2 * HDIM)

    def columns(g, which):
        return slice(which * width + g * HALF, which * width + (g + 1) * HALF)

    def features(g):
        return slice(g * HALF, (g + 1) * HALF)

    def memory_keys(g):
        v_mem = spread(qkv_ref[0, length:, columns(g, 2)], group)
        dpk_ref[g * gpad : (g + 1) * gpad, :] = dot(v_mem, gm_ref[0, :length, features(g)], 1, 1)
        kt_ref[features(g), :] = qkv_ref[0, :length, columns(g, 1)].T

    def memory_queries(g):
        do_mem = spread(gm_ref[0, length:, features(g)], group)
        q_mem = spread(qkv_ref[0, length:, columns(g, 0)], group)
        prob = ptq_ref[0, :, g * gpad : (g + 1) * gpad]
        pf = prob.astype(FL)
        t = pf * dot(qkv_ref[0, :, columns(g, 2)], do_mem, 1, 1)
        ds = (t - pf * jnp.sum(t, axis=0, keepdims=True)).astype(BF)
        dv_ref[:, features(g)] = dot(prob, do_mem, 1, 0)
        dk_ref[:, features(g)] = dot(ds, q_mem, 1, 0)
        dq = fold(dot(ds, qkv_ref[0, :, columns(g, 1)], 0, 0), group)
        dj_ref[0, length:, features(g)] = (dq * SCALE).astype(BF)

    def rise(h, part, slot):
        at = (h // 2) * 2 * HDIM
        low, upto = part * HALF, (part + 1) * HALF
        base = part * (part + 1) // 2 * HALF
        own = slice(h * PAD, (h + 1) * PAD)
        vm = qkv_ref[0, :upto, 2 * width + at : 2 * width + at + 2 * HDIM] * masks[h % 2]
        dp = dot(vm, gm_ref[0, low:upto, at : at + 2 * HDIM], 1, 1)
        deltas = []
        for c in range(0, HALF, LANES):
            lanes = slice(c, c + LANES)
            live = low + c + LANES
            t = pt_ref[0, h, base : base + live, lanes].astype(FL) * dp[:live, lanes]
            tm = ptk_ref[0, own, low + c : live].astype(FL) * dpk_ref[own, low + c : live]
            s_ref[slot, :live, lanes] = t
            deltas.append(jnp.sum(t, axis=0, keepdims=True) + jnp.sum(tm, axis=0, keepdims=True))
        return deltas

    def settle(h, part, slot, deltas):
        low, upto = part * HALF, (part + 1) * HALF
        base = part * (part + 1) // 2 * HALF
        own = slice(h * PAD, (h + 1) * PAD)
        keep = (h // 2) % 2
        made, made_mem = [], []
        for c, delta in zip(range(0, HALF, LANES), deltas):
            lanes = slice(c, c + LANES)
            live = low + c + LANES
            pf = pt_ref[0, h, base : base + live, lanes].astype(FL)
            made.append(s_ref[slot, :live, lanes] - pf * delta)
            if live < upto:
                made[-1] = jnp.concatenate([made[-1], jnp.zeros((upto - live, LANES), FL)], axis=0)
            pm = ptk_ref[0, own, low + c : live].astype(FL)
            made_mem.append(pm * (dpk_ref[own, low + c : live] - delta))
        ds_ref[keep, h % 2, base : base + upto, :] = jnp.concatenate(made, axis=1).astype(BF)
        dsk_ref[own, low:upto] = jnp.concatenate(made_mem, axis=1).astype(BF)

    def gather_rows(p, source, other, into):
        lanes = slice(p * 2 * HDIM, (p + 1) * 2 * HDIM)
        rows = [other * masks[side] for side in range(2)]
        for tile in range(parts):
            left, right = [], []
            for side in range(2):
                for part in range(tile, parts):
                    base = part * (part + 1) // 2 * HALF + tile * HALF
                    left.append(source(side, slice(base, base + HALF)))
                    right.append(rows[side][part * HALF : (part + 1) * HALF])
            into[tile * HALF : (tile + 1) * HALF, lanes] += dot(
                jnp.concatenate(left, axis=1), jnp.concatenate(right, axis=0), 1, 0
            )

    def values_back(p):
        lanes = slice(p * 2 * HDIM, (p + 1) * 2 * HDIM)
        gather_rows(p, lambda side, r: pt_ref[0, 2 * p + side, r, :], gm_ref[0, :length, lanes], dv_ref)

    def keys_back(p):
        lanes = slice(p * 2 * HDIM, (p + 1) * 2 * HDIM)
        gather_rows(p, lambda side, r: ds_ref[p % 2, side, r, :], qkv_ref[0, :length, lanes], dk_ref)

    def queries_back(h):
        feat = slice(h * HDIM, (h + 1) * HDIM)
        for part in range(parts):
            low, upto = part * HALF, (part + 1) * HALF
            base = part * (part + 1) // 2 * HALF
            ds = ds_ref[(h // 2) % 2, h % 2, base : base + upto, :]
            dqt_ref[feat, low:upto] = dot(kt_ref[feat, :upto], ds, 1, 0)

    def finish(g):
        own = slice(g * gpad, (g + 1) * gpad)
        k_mem = spread(qkv_ref[0, length:, columns(g, 1)], group)
        dq_t = dqt_ref[features(g), :] + dot(k_mem, dsk_ref[own, :], 0, 0)
        dj_ref[0, :length, features(g)] = (dq_t * SCALE).astype(BF).T
        dv_mem = fold(dot(ptk_ref[0, own, :], gm_ref[0, :length, features(g)], 1, 0), group)
        dk_mem = fold(dot(dsk_ref[own, :], qkv_ref[0, :length, columns(g, 0)], 1, 0), group)
        dj_ref[0, :length, columns(g, 1)] = dk_ref[:length, features(g)].astype(BF)
        dj_ref[0, :length, columns(g, 2)] = dv_ref[:length, features(g)].astype(BF)
        dj_ref[0, length:, columns(g, 1)] = (dk_ref[length:, features(g)] + dk_mem).astype(BF)
        dj_ref[0, length:, columns(g, 2)] = (dv_ref[length:, features(g)] + dv_mem).astype(BF)

    groups = width // HALF
    memory_keys(0)
    units = [(2 * p + side, part) for p in range(pairs) for side in range(2) for part in range(parts)]
    per_pair = 2 * parts
    deltas = {}
    later = []
    for u in range(len(units) + 2):
        if u < len(units):
            deltas[u] = rise(*units[u], u % SLOTS)
        if u >= 2:
            settle(*units[u - 2], (u - 2) % SLOTS, deltas.pop(u - 2))
            if (u - 1) % per_pair == 0:
                p = (u - 1) // per_pair - 1
                later += [(queries_back, 2 * p), (queries_back, 2 * p + 1), (keys_back, p)]
                if p % 2 == 1:
                    later.append((finish, p // 2))
        if u < len(units):
            p, at = u // per_pair, u % per_pair
            if at == 0 and p % 2 == 0:
                memory_queries(p // 2)
            if at == 3:
                values_back(p)
            if at == 2 and p % 2 == 1 and p // 2 + 1 < groups:
                memory_keys(p // 2 + 1)
        if later:
            work, arg = later.pop(0)
            work(arg)
    for work, arg in later:
        work(arg)


def go_back(begin, count, qkv, pt, ptk, ptq, gm):
    rows, width = gm.shape[1:]
    length = rows - PAD
    heads = width // HDIM
    one = lambda *dims: pl.BlockSpec((1,) + dims, lambda b: (b + begin,) + (0,) * len(dims))
    vm = pltpu.VMEM
    return pl.pallas_call(
        return_kernel,
        grid=(count,),
        in_specs=[
            one(rows, 3 * width),
            one(*pt.shape[1:]),
            one(heads * PAD, length),
            one(rows, heads * PAD),
            one(rows, width),
        ],
        out_specs=pl.BlockSpec((1, rows, 3 * width), lambda b: (b, 0, 0)),
        out_shape=jax.ShapeDtypeStruct((count, rows, 3 * width), BF),
        scratch_shapes=[
            vm((width, length), BF),
            vm((heads * PAD, length), FL),
            vm((heads * PAD, length), BF),
            vm((width, length), FL),
            vm((rows, width), FL),
            vm((rows, width), FL),
            vm((SLOTS, length, HALF), FL),
            vm((2, 2, pt.shape[2], HALF), BF),
        ],
        compiler_params=pltpu.CompilerParams(vmem_limit_bytes=48 << 20),
        cost_estimate=pl.CostEstimate(flops=count * 10**10, bytes_accessed=count * 10**7, transcendentals=0),
        name="go_back",
    )(qkv, pt, ptk, ptq, gm)


def weigh_kernel(
    begins,
    tok_ref,
    state_ref,
    one_ref,
    inw_ref,
    *refs,
):
    dj_refs, refs = refs[: len(begins)], refs[len(begins) :]
    gone_ref, gtwo_ref, acc_ref, left_ref, m_in_ref, m_dj_ref, side_ref, memb_ref = refs
    cut = gone_ref.shape[1]
    step = pl.program_id(0)
    last = pl.num_programs(0) - 1
    length, width = tok_ref.shape[1:]
    ends = begins[1:] + [last + 1]

    @pl.when(step == 0)
    def _():
        acc_ref[...] = jnp.zeros_like(acc_ref)
        side_ref[...] = jnp.zeros_like(side_ref)
        memb_ref[...] = inw_ref[:, 3 * width :].astype(FL).T
        left_ref[width:, :] = jnp.ones((ONES, length), BF)

    mem = pl.ds(pl.multiple_of(step * PAD, PAD), PAD)
    m_in_ref[mem, :] = (state_ref[0].astype(FL) + memb_ref[:PAD]).astype(BF)
    side_ref[0:PAD, :] += one_ref[0]
    left_ref[:width, :] = tok_ref[0].T
    for g, dj_ref in enumerate(dj_refs):

        @pl.when((step >= begins[g]) & (step < ends[g]))
        def _(dj_ref=dj_ref):
            m_dj_ref[mem, :] = dj_ref[0, length:, :]
            for j in range(0, 3 * width, FCHUNK):
                c = slice(j, j + FCHUNK)
                acc_ref[:, c] += dot(left_ref[...], dj_ref[0, :length, c], 1, 0)

    @pl.when(step == last)
    def _():
        more = jnp.concatenate([m_in_ref[...].T, jnp.ones((ONES, m_in_ref.shape[0]), BF)], axis=0)
        for j in range(0, 3 * width, FCHUNK):
            c = slice(j, j + FCHUNK)
            acc_ref[:, c] += dot(more, m_dj_ref[:, c], 1, 0)
        gone_ref[...] = acc_ref[:width, :cut].astype(BF)
        gtwo_ref[:, : 3 * width - cut] = acc_ref[:width, cut:].astype(BF)
        back = dot(m_dj_ref[...], inw_ref[:, : 3 * width], 1, 1)
        side_ref[0:PAD, :] += jnp.sum(back.reshape(last + 1, PAD, width), axis=0)
        side_ref[PAD : PAD + 1, :] = acc_ref[width : width + 1, :width]
        side_ref[PAD + 1 : PAD + 2, :] = acc_ref[width : width + 1, 2 * width :]
        gtwo_ref[:, 3 * width - cut :] = side_ref[...].T.astype(BF)


def weigh(tok, state, near, one_grad, djs, begins):
    count, length, width = tok.shape
    rows = length + PAD
    cut = halfway(3 * width + LANES)
    one = lambda *dims: pl.BlockSpec((1,) + dims, lambda b: (b,) + (0,) * len(dims))
    whole = lambda *dims: pl.BlockSpec(dims, lambda b: (0,) * len(dims), pipeline_mode=pl.Buffered(1))
    final = lambda *dims: pl.BlockSpec(dims, lambda b: (0,) * len(dims))
    part = lambda g: pl.BlockSpec(
        (1, rows, 3 * width), lambda b: (jnp.clip(b - begins[g], 0, djs[g].shape[0] - 1), 0, 0)
    )
    vm = pltpu.VMEM
    return pl.pallas_call(
        partial(weigh_kernel, begins),
        grid=(count,),
        in_specs=[
            one(length, width),
            one(PAD, width),
            pl.BlockSpec((1, PAD, width), lambda b: (b, length // PAD, 0)),
            whole(width, 3 * width + LANES),
        ]
        + [part(g) for g in range(len(djs))],
        out_specs=[final(width, cut), final(width, 3 * width + LANES - cut)],
        out_shape=[
            jax.ShapeDtypeStruct((width, cut), BF),
            jax.ShapeDtypeStruct((width, 3 * width + LANES - cut), BF),
        ],
        scratch_shapes=[
            vm((width + ONES, 3 * width), FL),
            vm((width + ONES, length), BF),
            vm((count * PAD, width), BF),
            vm((count * PAD, 3 * width), BF),
            vm((LANES, width), FL),
            vm((LANES, width), FL),
        ],
        compiler_params=pltpu.CompilerParams(vmem_limit_bytes=48 << 20),
        cost_estimate=pl.CostEstimate(flops=count * 10**9, bytes_accessed=count * 3 * 10**6, transcendentals=0),
        name="weigh",
    )(tok, state, one_grad, near, *djs)


def descend_kernel(one_ref, dj_ref, inw_ref, grad_ref):
    width = one_ref.shape[2]
    grad_ref[0] = one_ref[0] + dot(dj_ref[0], inw_ref[:, : 3 * width], 1, 1)


def descend(total, begin, one_grad, dj, near, into):
    count, rows, wide = dj.shape
    width = one_grad.shape[2]
    length = rows - PAD
    shift = lambda *dims: pl.BlockSpec((1,) + dims, lambda b: (b + begin, 0, 0))
    kept = () if into is None else (into,)

    def kernel(one_ref, dj_ref, inw_ref, *rest):
        descend_kernel(one_ref, dj_ref, inw_ref, rest[-1])

    return pl.pallas_call(
        kernel,
        grid=(count,),
        in_specs=[
            shift(length, width),
            pl.BlockSpec((1, length, wide), lambda b: (b, 0, 0)),
            pl.BlockSpec((width, wide + LANES), lambda b: (0, 0), pipeline_mode=pl.Buffered(1)),
        ]
        + [pl.BlockSpec(memory_space=pl.ANY)] * len(kept),
        out_specs=shift(length, width),
        out_shape=jax.ShapeDtypeStruct((total, length, width), FL),
        input_output_aliases={3: 0} if kept else {},
        compiler_params=pltpu.CompilerParams(vmem_limit_bytes=32 << 20),
        cost_estimate=pl.CostEstimate(flops=count * 10**9, bytes_accessed=count * 4 * 10**6, transcendentals=0),
        name="descend",
    )(one_grad, dj, near, *kept)


def pack_kernel(in_ref, up_ref, down_ref, out_ref, vec_ref, bias_ref, mem_ref, near_ref, far_ref, flip_ref):
    shard, cols = in_ref.shape
    hid, width = up_ref.shape[1], out_ref.shape[1]
    flip_ref[...] = jnp.zeros_like(flip_ref)
    flip_ref[PAD : PAD + 8, :shard] = vec_ref[...]
    flip_ref[...] = flip_ref[...].T
    flip_ref[:shard, : mem_ref.shape[1]] = mem_ref[...]
    flip_ref[0:1, BIAS : BIAS + bias_ref.shape[1]] = bias_ref[...]
    near_ref[:, :cols] = in_ref[...].astype(BF)
    near_ref[:, cols:] = flip_ref[:shard].astype(BF)
    far_ref[:, :hid] = up_ref[...].astype(BF)
    far_ref[:, hid : 2 * hid] = down_ref[...].astype(BF)
    far_ref[:, 2 * hid :] = out_ref[...].astype(BF)


def pack(in_w, up_w, down_t, out_t, vectors, bias, mem_t):
    shard, cols = in_w.shape
    wide = 2 * up_w.shape[1] + out_t.shape[1]
    return pl.pallas_call(
        pack_kernel,
        out_shape=[
            jax.ShapeDtypeStruct((shard, cols + LANES), BF),
            jax.ShapeDtypeStruct((shard, wide), BF),
        ],
        scratch_shapes=[pltpu.VMEM((LANES, LANES), FL)],
        name="pack",
    )(in_w, up_w, down_t, out_t, vectors, bias, mem_t)


def square_kernel(cols, *refs):
    held_refs, got_refs, (far_ref, near_ref, sum_ref) = refs[:2], refs[2:4], refs[4:]
    at = 0
    for held_ref, got_ref in zip(held_refs, got_refs):
        size = held_ref.shape[1]
        near_ref[:, at : at + size] = held_ref[...] + got_ref[...].astype(FL)
        at += size
    wide = far_ref.shape[1] - LANES
    near, far = near_ref[:, :cols], far_ref[:, :wide]
    side = near_ref[:, cols:] + far_ref[:, wide:]
    total = jnp.sum(near * near) + jnp.sum(far * far) + jnp.sum(side * side)
    sum_ref[...] = jnp.full(sum_ref.shape, total, FL)


def adam_kernel(sizes, rates, decays, near_ref, far_ref, total_ref, *refs):
    cols, hid, width = sizes
    state_refs, new_refs, norm_ref, flip_ref = refs[:21], refs[21:42], refs[42], refs[43]
    shard = near_ref.shape[0]
    norm = jnp.sqrt(total_ref[...])
    norm_ref[...] = norm[0:1, 0:1]
    factor = (1.0 / jnp.maximum(norm, 1.0))[0:1, 0:1]
    side = near_ref[:, cols:] + far_ref[:, 2 * hid + width :]
    flip_ref[...] = jnp.zeros_like(flip_ref)
    flip_ref[:shard] = side
    turned = flip_ref[...].T
    bias = pltpu.roll(side, LANES - BIAS, 1)
    grads = (
        near_ref[:, :cols],
        far_ref[:, 2 * hid : 2 * hid + width],
        far_ref[:, :hid],
        far_ref[:, hid : 2 * hid],
        turned[PAD : PAD + 8, :shard],
        bias[0:1, : state_refs[15].shape[1]],
        side[:, : state_refs[18].shape[1]],
    )
    correction = 1.0 - 0.5**STEP
    for i in range(7):
        weight, first, second = (state_refs[3 * i + k][...] for k in range(3))
        grad = grads[i] * factor
        first_new = 0.5 * first + 0.5 * grad
        second_new = 0.5 * second + 0.5 * grad * grad
        step = first_new / correction / (jnp.sqrt(second_new / correction) + 1e-08)
        new_refs[3 * i][...] = weight - rates[i] * (step + decays[i] * weight)
        new_refs[3 * i + 1][...] = first_new
        new_refs[3 * i + 2][...] = second_new


def exchange(x, bit, devices):
    return lax.ppermute(x, AXES, [(i, i ^ bit) for i in range(devices)])


def beside(got, sent, work):
    if work is None:
        return got, None
    made = work(lambda value: lax.optimization_barrier((value, sent))[0])
    return lax.optimization_barrier((got, made))


def gather(x, devices, index, works):
    rows, cols = x.shape
    held = x[None]
    results = []
    bits = devices.bit_length() - 1
    for step in range(bits):
        bit = devices >> (step + 1)
        got = exchange(held, bit, devices)
        got, made = beside(got, held, works[step] if step < len(works) else None)
        results.append(made)
        upper = (index & bit) != 0
        held = jnp.stack([jnp.where(upper, got, held), jnp.where(upper, held, got)], axis=1)
        held = held.reshape(-1, rows, cols)
    return held.reshape(devices * rows, cols), [made for made in results if made is not None]


def halve(held, got, place, upper):
    total = held if got is None else held.astype(FL) + got.astype(FL)
    low, high = (lax.index_in_dim(total, i, place, keepdims=False) for i in range(2))
    return jnp.where(upper, high, low), jnp.where(upper, low, high).astype(BF)


def scatter_sum(halves, devices, index, works):
    rows = halves[0].shape[0] // devices
    bits = devices.bit_length() - 1
    orders = [list(range(bits)) for _ in range(2)]
    if bits > 2:
        orders[1][1:3] = [2, 1]
    held = [half.reshape((2,) * bits + (rows, -1)) for half in halves]
    got = [None, None]
    results = []
    for step in range(bits):
        send = [None, None]
        for half, order in enumerate(orders):
            bit = order[step]
            place = sum(1 for other in order[step:] if other > bit)
            upper = (index & (1 << bit)) != 0
            held[half], send[half] = halve(held[half], got[half], place, upper)
        if step < 3:
            got = [exchange(value, 1 << order[step], devices) for value, order in zip(send, orders)]
            got, made = beside(got, send, works[step] if step < len(works) else None)
        else:
            sent = jnp.concatenate(send, axis=-1)
            both, made = beside(exchange(sent, 1 << orders[0][step], devices), sent, works[step] if step < len(works) else None)
            cut = send[0].shape[-1]
            got = [both[..., :cut], both[..., cut:]]
        results.append(made)
    return [value.astype(FL).reshape(rows, -1) for value in held], [value.reshape(rows, -1) for value in got], results


def butterfly(x, devices):
    for step in range(devices.bit_length() - 1):
        x = x + exchange(x, 1 << step, devices)
    return x


def per_device(
    devices,
    tokens,
    memory_state,
    cotangent,
    in_weight,
    in_first,
    in_second,
    out_weight,
    out_first,
    out_second,
    up_weight,
    up_first,
    up_second,
    down_weight,
    down_first,
    down_second,
    vectors,
    vectors_first,
    vectors_second,
    up_bias,
    up_bias_first,
    up_bias_second,
    memory_embed,
    memory_first,
    memory_second,
):
    index = lax.axis_index(AXES)
    micro, local, length, width = tokens.shape
    count = micro * local
    extra = memory_state.shape[2]
    shard = in_weight.shape[0]
    hid = up_weight.shape[1]
    per_bias = up_bias.shape[0] // shard

    near, far = pack(
        in_weight,
        up_weight,
        down_weight.T,
        out_weight.T,
        vectors,
        up_bias.reshape(1, -1),
        memory_embed.T,
    )
    wide = lax.all_gather(far, AXES, axis=0, tiled=True)

    def pad_state(tie):
        rows = tie(memory_state).reshape(count, extra, width)
        return jnp.pad(rows, ((0, 0), (0, PAD - extra), (0, 0)))

    def align(tie):
        cot = tie(cotangent).reshape(count, extra + length, width)
        return jnp.concatenate(
            [cot[:, extra:], cot[:, :extra], jnp.zeros((count, PAD - extra, width), BF)], axis=1
        )

    near, (state, cot) = gather(near, devices, index, [pad_state, None, None, align])

    tok = tokens.reshape(count, length, width)

    qkv, pt, ptk, ptq, mixed = attend(extra, tok, state, near)
    out, one_grad, gm, *gwide = feed(devices, tok, state, near, wide, mixed, cot)

    def split(sizes):
        begins = [0]
        for size in sizes:
            begins.append(begins[-1] + size)
        return list(zip(begins, sizes))

    djs = []

    def back(begin, size):
        def work(tie):
            djs.append(go_back(begin, size, tie(qkv), pt, ptk, ptq, gm))
            return djs[-1]

        return work

    def whole_weigh(tie):
        return weigh(tie(tok), state, near, one_grad, djs, [begin for begin, _ in runs])

    runs = split(BACK) if sum(BACK) == count else split([count])
    held, got, made = scatter_sum(gwide, devices, index, [back(*run) for run in runs] + [whole_weigh])
    gin = made[len(runs)]
    far_held, far_got = held, got
    grads = []

    def down(i):
        def work(tie):
            into = grads[-1] if grads else None
            grads.append(descend(count, runs[i][0], one_grad, tie(djs[i]), near, into))
            return grads[-1]

        return work

    def order(tie):
        rows = tie(out)
        rows = jnp.concatenate([rows[:, length : length + extra], rows[:, :length]], axis=1)
        return rows.reshape(micro, local, extra + length, width).transpose(0, 2, 1, 3)

    works = [down(i) for i in range(len(runs))] + [order]
    held, got, made = scatter_sum(gin, devices, index, works)
    input_grad = made[len(runs) - 1].reshape(micro, local, length, width)
    (far_held, far_got), _ = lax.optimization_barrier(((far_held, far_got), made[len(runs) - 1]))
    gfar = jnp.concatenate([mine + more.astype(FL) for mine, more in zip(far_held, far_got)], axis=1)

    gnear, squares = pl.pallas_call(
        partial(square_kernel, 3 * width),
        out_shape=[
            jax.ShapeDtypeStruct((shard, 3 * width + LANES), FL),
            jax.ShapeDtypeStruct((8, LANES), FL),
        ],
        name="squares",
    )(*held, *got, gfar)
    squares = butterfly(squares, devices)
    output = made[len(runs)].transpose(0, 2, 1, 3)
    total_rows = extra + length
    rates = (
        0.5 * width ** (-0.5),
        0.5 * (width * 32 // total_rows) ** (-0.5),
        0.5 * width ** (-0.5),
        0.5 * hid ** (-0.5),
        0.1,
        0.1,
        0.5,
    )
    decays = (0.1, 0.1, 0.1, 0.1, 0.0, 0.0, 0.0)
    same = lambda value: value
    turn = lambda value: value.T
    flat = lambda value: value.reshape(1, -1)
    views = (same, turn, same, turn, same, flat, turn)
    states = (
        (in_weight, in_first, in_second),
        (out_weight, out_first, out_second),
        (up_weight, up_first, up_second),
        (down_weight, down_first, down_second),
        (vectors, vectors_first, vectors_second),
        (up_bias, up_bias_first, up_bias_second),
        (memory_embed, memory_first, memory_second),
    )
    held = [view(value) for view, group in zip(views, states) for value in group]
    *new, norm = pl.pallas_call(
        partial(adam_kernel, (3 * width, hid, width), rates, decays),
        out_shape=[jax.ShapeDtypeStruct(value.shape, FL) for value in held]
        + [jax.ShapeDtypeStruct((1, 1), FL)],
        scratch_shapes=[pltpu.VMEM((LANES, LANES), FL)],
        name="adam",
    )(gnear, gfar, squares, *held)
    back_views = (same, turn, same, turn, same, lambda value: value.reshape(-1), turn)
    results = [back_views[i // 3](value) for i, value in enumerate(new)]
    return (output, input_grad, *results, norm.reshape(()))


def solution(mesh):
    blocks = P(None, AXES, None, None)
    lead = P(AXES, None)
    trail = P(None, AXES)
    flat = P(AXES)
    weights = (lead,) * 3 + (trail,) * 3 + (lead,) * 3 + (trail,) * 6 + (flat,) * 3 + (trail,) * 3
    devices = mesh.shape["dp"] * mesh.shape["fsdp"]
    return jax.shard_map(
        partial(per_device, devices),
        mesh=mesh,
        in_specs=(blocks,) * 3 + weights,
        out_specs=(blocks,) * 2 + weights + (P(),),
        check_vma=False,
    )
```

```python
from functools import partial

import jax
import jax.numpy as jnp
from jax import lax
from jax.experimental import pallas as pl
from jax.experimental.pallas import tpu as pltpu
from jax.sharding import PartitionSpec as P

STEP = 7
HDIM = 64
PAD = 32
HALF = 256
FCHUNK = 256
ROWS = 32
BF = jnp.bfloat16
FL = jnp.float32
AXES = ("dp", "fsdp")
NEG = -1e30
EPS = 1e-05
SCALE = HDIM ** (-0.5)
LANES = 128
BIAS = 64
SLOTS = 6
PLAN_MORE = (0, 2, 4, 5)
PLAN_LAST = (2, 4, 7, 5)
CUT = 3
ONES = 16
BACK = (2, 4, 2)


def dot(a, b, ca, cb):
    return lax.dot_general(a, b, (((ca,), (cb,)), ((), ())), preferred_element_type=FL)


def head_mask(rows, width):
    row = lax.broadcasted_iota(jnp.int32, (rows, width), 0) // PAD
    col = lax.broadcasted_iota(jnp.int32, (rows, width), 1) // HDIM
    return row == col


def spread(x, heads):
    tiled = jnp.concatenate([x.astype(FL)] * heads, axis=0)
    return jnp.where(head_mask(*tiled.shape), tiled, 0.0).astype(BF)


def fold(y, heads):
    own = jnp.where(head_mask(*y.shape), y, 0.0)
    return sum(own[h * PAD : (h + 1) * PAD] for h in range(heads))


def pair_masks(width):
    col = lax.broadcasted_iota(jnp.int32, (1, width), 1)
    low = jnp.where(col < HDIM, 1.0, 0.0)
    return low.astype(BF), (1.0 - low).astype(BF)


def attend_kernel(
    extra,
    tok_ref,
    state_ref,
    first_ref,
    first_state_ref,
    inw_ref,
    qkv_ref,
    pt_ref,
    ptk_ref,
    ptq_ref,
    mixed_ref,
    vt_ref,
    sk_ref,
    ot_ref,
    side_ref,
    inp_ref,
    s_ref,
    ahead_ref,
):
    length, width = tok_ref.shape[1:]
    rows = length + PAD
    group = HALF // HDIM
    gpad = group * PAD
    diag = lax.broadcasted_iota(jnp.int32, (LANES, LANES), 0) <= lax.broadcasted_iota(
        jnp.int32, (LANES, LANES), 1
    )
    key_live = lax.broadcasted_iota(jnp.int32, (gpad, 1), 0) % PAD < extra
    place_live = lax.broadcasted_iota(jnp.int32, (rows, 1), 0) < length + extra
    masks = pair_masks(2 * HDIM)

    def columns(g, which):
        return slice(which * width + g * HALF, which * width + (g + 1) * HALF)

    def ahead(which):
        return slice(which * HALF, (which + 1) * HALF)

    def take(source, source_state):
        inp_ref[:length] = source[0]
        inp_ref[length:] = (source_state[0].astype(FL) + side_ref[:PAD]).astype(BF)

    def project(g, which):
        feat = slice(g * HALF, (g + 1) * HALF)
        made = dot(inp_ref[...], inw_ref[:, columns(g, which)], 1, 0)
        if which == 0:
            made = (made + side_ref[PAD : PAD + 1, feat]) * SCALE
        if which == 2:
            made = made + side_ref[PAD + 1 : PAD + 2, feat]
        made = made.astype(BF)
        if g:
            qkv_ref[0, :, columns(g, which)] = made
        else:
            ahead_ref[:, ahead(which)] = made
        if which == 2:
            vt_ref[feat, :] = made[:length].T

    def memory_keys(g):
        if g:
            mem, query = qkv_ref[0, length:, columns(g, 1)], qkv_ref[0, :length, columns(g, 0)]
        else:
            mem, query = ahead_ref[length:, ahead(1)], ahead_ref[:length, ahead(0)]
        made = dot(spread(mem, group), query, 1, 1)
        sk_ref[g * gpad : (g + 1) * gpad, :] = jnp.where(key_live, made, NEG)

    def memory_queries(g):
        q_mem = spread(qkv_ref[0, length:, columns(g, 0)], group)
        sq = jnp.where(place_live, dot(qkv_ref[0, :, columns(g, 1)], q_mem, 1, 1), NEG)
        eq = jnp.exp(sq - jnp.max(sq, axis=0, keepdims=True))
        probs = (eq * (1.0 / jnp.sum(eq, axis=0, keepdims=True))).astype(BF)
        ptq_ref[0, :, g * gpad : (g + 1) * gpad] = probs
        om = dot(probs, qkv_ref[0, :, columns(g, 2)], 0, 0)
        mixed_ref[0, length:, g * HALF : (g + 1) * HALF] = fold(om, group).astype(BF)

    @pl.when(pl.program_id(0) == 0)
    def _():
        side_ref[...] = inw_ref[:, 3 * width :].astype(FL).T
        take(first_ref, first_state_ref)
        for which in range(3):
            project(0, which)
        memory_keys(0)

    def score(p, i, slot):
        low, live = i * LANES, (i + 1) * LANES
        at = p * 2 * HDIM
        qp = qkv_ref[0, low:live, at : at + 2 * HDIM]
        both = jnp.concatenate([qp * masks[0], qp * masks[1]], axis=0)
        s = dot(qkv_ref[0, :live, width + at : width + at + 2 * HDIM], both, 1, 1)
        tops = []
        for side in range(2):
            lanes = slice(side * LANES, (side + 1) * LANES)
            own = slice((2 * p + side) * PAD, (2 * p + side + 1) * PAD)
            edge = jnp.where(diag, s[low:live, lanes], NEG)
            s_ref[slot, low:live, lanes] = edge
            top = jnp.maximum(
                jnp.max(edge, axis=0, keepdims=True), jnp.max(sk_ref[own, low:live], axis=0, keepdims=True)
            )
            if low:
                s_ref[slot, :low, lanes] = s[:low, lanes]
                top = jnp.maximum(top, jnp.max(s[:low, lanes], axis=0, keepdims=True))
            tops.append(top)
        return tops

    def soften(p, i, slot, tops):
        low, live = i * LANES, (i + 1) * LANES
        base = i * (i + 1) // 2 * LANES
        made = []
        for side, top in enumerate(tops):
            own = slice((2 * p + side) * PAD, (2 * p + side + 1) * PAD)
            e = jnp.exp(s_ref[slot, :live, side * LANES : (side + 1) * LANES] - top)
            e_mem = jnp.exp(sk_ref[own, low:live] - top)
            total = jnp.sum(e, axis=0, keepdims=True) + jnp.sum(e_mem, axis=0, keepdims=True)
            share = 1.0 / total
            made.append(e * share)
            ptk_ref[0, own, low:live] = (e_mem * share).astype(BF)
        pt_ref[0, p, base : base + live, :] = jnp.concatenate(made, axis=1).astype(BF)

    def mix(p, i):
        low, live = i * LANES, (i + 1) * LANES
        base = i * (i + 1) // 2 * LANES
        at = p * 2 * HDIM
        made = dot(vt_ref[at : at + 2 * HDIM, :live], pt_ref[0, p, base : base + live, :], 1, 0)
        for side in range(2):
            ot_ref[at + side * HDIM : at + (side + 1) * HDIM, low:live] = made[
                side * HDIM : (side + 1) * HDIM, side * LANES : (side + 1) * LANES
            ]

    def finish(g):
        v_mem = spread(qkv_ref[0, length:, columns(g, 2)], group)
        feat = slice(g * HALF, (g + 1) * HALF)
        om_t = ot_ref[feat, :] + dot(v_mem, ptk_ref[0, g * gpad : (g + 1) * gpad, :], 0, 0)
        mixed_ref[0, :length, feat] = om_t.astype(BF).T

    groups = width // HALF
    blocks = length // LANES
    units = [(p, i) for p in range(width // (2 * HDIM)) for i in range(blocks)]
    per_group = group // 2 * blocks
    for which in range(3):
        qkv_ref[0, :, columns(0, which)] = ahead_ref[:, ahead(which)]
    works = {}
    for g in range(groups):
        at = g * per_group
        more = g + 1 < groups
        plan = PLAN_MORE if more else PLAN_LAST
        works.setdefault(at + 1, []).append((memory_queries, g))
        if g:
            works.setdefault(at + 4, []).append((finish, g - 1))
        if not more:
            works.setdefault(at, []).append((take, tok_ref, state_ref))
        for which in range(3):
            works.setdefault(at + plan[which], []).append((project, g + 1 if more else 0, which))
        works.setdefault(at + plan[3], []).append((memory_keys, g + 1 if more else 0))
    tops = {}
    for u in range(len(units) + 5):
        if u < len(units):
            tops[u] = score(*units[u], u % SLOTS)
        if 3 <= u <= len(units) + 2:
            soften(*units[u - 3], (u - 3) % SLOTS, tops.pop(u - 3))
        if u >= 5:
            mix(*units[u - 5])
        for work, *given in works.get(u, ()):
            work(*given)
    finish(groups - 1)


def attend(extra, tok, state, near):
    count, length, width = tok.shape
    heads = width // HDIM
    rows = length + PAD
    blocks = length // LANES
    ptrows = blocks * (blocks + 1) // 2 * LANES
    one = lambda *dims: pl.BlockSpec((1,) + dims, lambda b: (b,) + (0,) * len(dims))
    after = lambda *dims: pl.BlockSpec((1,) + dims, lambda b: (jnp.minimum(b + 1, count - 1), 0, 0))
    whole = lambda *dims: pl.BlockSpec(dims, lambda b: (0,) * len(dims), pipeline_mode=pl.Buffered(1))
    return pl.pallas_call(
        partial(attend_kernel, extra),
        grid=(count,),
        in_specs=[
            after(length, width),
            after(PAD, width),
            pl.BlockSpec((1, length, width), lambda b: (0, 0, 0), pipeline_mode=pl.Buffered(1)),
            pl.BlockSpec((1, PAD, width), lambda b: (0, 0, 0), pipeline_mode=pl.Buffered(1)),
            whole(width, 3 * width + LANES),
        ],
        out_specs=[
            one(rows, 3 * width),
            one(heads // 2, ptrows, HALF),
            one(heads * PAD, length),
            one(rows, heads * PAD),
            one(rows, width),
        ],
        out_shape=[
            jax.ShapeDtypeStruct((count, rows, 3 * width), BF),
            jax.ShapeDtypeStruct((count, heads // 2, ptrows, HALF), BF),
            jax.ShapeDtypeStruct((count, heads * PAD, length), BF),
            jax.ShapeDtypeStruct((count, rows, heads * PAD), BF),
            jax.ShapeDtypeStruct((count, rows, width), BF),
        ],
        scratch_shapes=[
            pltpu.VMEM((width, length), BF),
            pltpu.VMEM((heads * PAD, length), FL),
            pltpu.VMEM((width, length), FL),
            pltpu.VMEM((LANES, width), FL),
            pltpu.VMEM((rows, width), BF),
            pltpu.VMEM((SLOTS, length, HALF), FL),
            pltpu.VMEM((rows, 3 * HALF), BF),
        ],
        compiler_params=pltpu.CompilerParams(vmem_limit_bytes=56 << 20),
        name="attend",
    )(tok, state, tok, state, near)


def norm_rows(x):
    center = x - jnp.mean(x, axis=-1, keepdims=True)
    rstd = lax.rsqrt(jnp.mean(center * center, axis=-1, keepdims=True) + EPS)
    return center * rstd, rstd


def norm_back(grad, normed, rstd, gain):
    scaled = grad * gain
    return rstd * (
        scaled
        - jnp.mean(scaled, axis=-1, keepdims=True)
        - normed * jnp.mean(scaled * normed, axis=-1, keepdims=True)
    )


def by_eight(x):
    return jnp.sum(x.reshape(x.shape[0] // 8, 8, x.shape[1]), axis=0)


def feed_kernel(
    devices,
    tok_ref,
    state_ref,
    small_ref,
    wide_ref,
    mixed_ref,
    cot_ref,
    out_ref,
    one_ref,
    gm_ref,
    gone_ref,
    gtwo_ref,
    upb_ref,
    side_ref,
    gside_ref,
    acc_ref,
    sums_ref,
    upb_sum_ref,
    att_ref,
    n1_ref,
    r1_ref,
    low_ref,
    g2_ref,
    gb_ref,
    hidden_ref,
    slope_ref,
    gpre_ref,
    ga_ref,
    m_low_ref,
    m_gb_ref,
    m_ga_ref,
    m_mixed_ref,
    m_hidden_ref,
    m_gpre_ref,
    low_t_ref,
    gb_t_ref,
):
    step = pl.program_id(0)
    last = pl.num_programs(0) - 1
    length, width = tok_ref.shape[1:]
    hid = upb_ref.shape[1]
    rows = length + PAD
    shard, per = width // devices, hid // devices
    up = slice(0, hid)
    down = slice(hid, 2 * hid)
    outw = slice(2 * hid, 2 * hid + width)

    @pl.when(step == 0)
    def _():
        acc_ref[...] = jnp.zeros_like(acc_ref)
        sums_ref[...] = jnp.zeros_like(sums_ref)
        upb_sum_ref[...] = jnp.zeros_like(upb_sum_ref)
        gpre_ref[...] = jnp.zeros_like(gpre_ref)
        low_t_ref[:width] = jnp.zeros((width, length), BF)
        low_t_ref[width:] = jnp.ones((ONES, length), BF)
        gside_ref[...] = small_ref[...].astype(FL)
        side_ref[...] = gside_ref[...].T
        for i in range(devices):
            upb_ref[:, i * per : (i + 1) * per] = gside_ref[i * shard : i * shard + 1, BIAS : BIAS + per]

    def put(at, value):
        cut = gone_ref.shape[1]
        if at < cut:
            gone_ref[:, at : at + value.shape[1]] = value.astype(BF)
        else:
            gtwo_ref[:, at - cut : at - cut + value.shape[1]] = value.astype(BF)

    def up_piece(j):
        c = slice(j, j + FCHUNK)
        made = dot(low_t_ref[...], gpre_ref[:length, c], 1, 0)
        acc_ref[:, c] += made[:width]
        upb_sum_ref[:, c] += made[width : width + 8]

    def down_piece(j):
        c = slice(j, j + FCHUNK)
        d = slice(hid + j, hid + j + FCHUNK)
        acc_ref[:, d] += dot(gb_t_ref[...], hidden_ref[:length, c], 1, 0)

    pieces = range(0, hid, FCHUNK)
    chunks = range(0, rows, ROWS)
    fills = [(up_piece, j) for j in pieces]

    def weave(stage, sums, works):
        totals = None
        done = 0
        for i, at in enumerate(chunks):
            made = stage(slice(at, at + ROWS))
            totals = made if totals is None else [x + y for x, y in zip(totals, made)]
            while done < len(works) and done * len(chunks) < (i + 1) * len(works):
                work, arg = works[done]
                work(arg)
                done += 1
        for at, total in zip(sums, totals or ()):
            sums_ref[8 * at : 8 * at + 8] += total

    att_ref[...] = dot(mixed_ref[0], wide_ref[:, outw], 1, 1)
    bias_att, bias_ffn = side_ref[PAD + 2 : PAD + 3], side_ref[PAD + 3 : PAD + 4]
    gain_one, shift_one, gain_two, shift_two = (side_ref[PAD + i : PAD + i + 1] for i in range(4, 8))

    shift_ffn = shift_one + bias_ffn

    def norm_one(r):
        if r.start < length:
            full = tok_ref[0, r, :].astype(FL)
        else:
            full = state_ref[0].astype(FL) + side_ref[:PAD]
        normed, rstd = norm_rows(full + (att_ref[r, :] + bias_att))
        n1_ref[r, :] = normed
        r1_ref[r, :] = rstd
        low_ref[r, :] = (normed * gain_one + shift_one).astype(BF)
        return []

    weave(norm_one, (), fills[:CUT])

    root = 0.7978845608
    for j in pieces:
        c = slice(j, j + FCHUNK)
        v = dot(low_ref[...], wide_ref[:, c], 1, 0) + upb_ref[:, c]
        square = v * v
        half = 0.5 + 0.5 * jnp.tanh(v * (root + (root * 0.044715) * square))
        act = v * half
        hidden_ref[:, c] = act.astype(BF)
        slope_ref[:, c] = half + (act * (1.0 - half)) * (2 * root + (6 * root * 0.044715) * square)

    att_ref[...] = dot(hidden_ref[...], wide_ref[:, down], 1, 1)

    def norm_two(r):
        normed, rstd = norm_rows(n1_ref[r, :] * gain_one + (att_ref[r, :] + shift_ffn))
        out_ref[0, r, :] = (normed * gain_two + shift_two).astype(BF)
        cot = cot_ref[0, r, :].astype(FL)
        back = norm_back(cot, normed, rstd, gain_two)
        g2_ref[r, :] = back
        low = back.astype(BF)
        gb_ref[r, :] = low
        return [by_eight(low.astype(FL)), by_eight(cot * normed), by_eight(cot)]

    weave(norm_two, (3, 6, 7), fills[CUT:])
    gb_t_ref[...] = gb_ref[:length].T
    low_t_ref[:width] = low_ref[:length].T

    for j in pieces:
        c = slice(j, j + FCHUNK)
        d = slice(hid + j, hid + j + FCHUNK)
        gpre = (dot(gb_ref[...], wide_ref[:, d], 1, 0) * slope_ref[:, c]).astype(BF)
        gpre_ref[:, c] = gpre

    att_ref[...] = dot(gpre_ref[...], wide_ref[:, up], 1, 1)

    def norm_last(r):
        g1 = g2_ref[r, :] + att_ref[r, :]
        normed = n1_ref[r, :]
        back = norm_back(g1, normed, r1_ref[r, :], gain_one)
        one_ref[0, r, :] = back
        low = back.astype(BF)
        ga_ref[r, :] = low
        return [by_eight(low.astype(FL)), by_eight(g1 * normed), by_eight(g1)]

    weave(norm_last, (2, 4, 5), [(down_piece, j) for j in pieces])

    gm_ref[0] = dot(ga_ref[...], wide_ref[:, outw], 1, 0).astype(BF)
    acc_ref[:, outw] += dot(ga_ref[:length], mixed_ref[0, :length], 0, 0)

    mem = pl.ds(pl.multiple_of(step * PAD, PAD), PAD)
    m_low_ref[mem, :] = low_ref[length:, :]
    m_gb_ref[mem, :] = gb_ref[length:, :]
    m_ga_ref[mem, :] = ga_ref[length:, :]
    m_mixed_ref[mem, :] = mixed_ref[0, length:, :]
    m_hidden_ref[mem, :] = hidden_ref[length:, :]
    m_gpre_ref[mem, :] = gpre_ref[length:, :]

    @pl.when(step == last)
    def _():
        more = jnp.concatenate([m_low_ref[...].T, jnp.ones((ONES, m_low_ref.shape[0]), BF)], axis=0)
        left_low = jnp.concatenate([low_t_ref[...], more], axis=1)
        left_gb = m_gb_ref[...].T
        for j in pieces:
            c = slice(j, j + FCHUNK)
            d = slice(hid + j, hid + j + FCHUNK)
            right = jnp.concatenate([gpre_ref[:length, c], m_gpre_ref[:, c]], axis=0)
            made = dot(left_low, right, 1, 0)
            put(c.start, acc_ref[:, c] + made[:width])
            upb_sum_ref[:, c] += made[width : width + 8]
            put(d.start, acc_ref[:, d] + dot(left_gb, m_hidden_ref[:, c], 1, 0))
        put(2 * hid, acc_ref[:, outw] + dot(m_ga_ref[...], m_mixed_ref[...], 0, 0))
        side_ref[...] = jnp.zeros_like(side_ref)
        for i in range(8):
            side_ref[PAD + i : PAD + i + 1] = jnp.sum(sums_ref[8 * i : 8 * i + 8], axis=0, keepdims=True)
        gside_ref[...] = side_ref[...].T
        bias = upb_sum_ref[0:1]
        for i in range(devices):
            piece = bias[:, i * per : (i + 1) * per]
            gside_ref[i * shard : i * shard + 1, BIAS : BIAS + per] = piece
        put(2 * hid + width, gside_ref[...])


def halfway(cols):
    return cols // (2 * LANES) * LANES


def feed(devices, tok, state, near, wide, mixed, cot):
    count, length, width = tok.shape
    rows = length + PAD
    cols = wide.shape[1]
    hid = (cols - width) // 2
    cut = halfway(cols + LANES)
    one = lambda *dims: pl.BlockSpec((1,) + dims, lambda b: (b,) + (0,) * len(dims))
    whole = lambda *dims: pl.BlockSpec(dims, lambda b: (0,) * len(dims), pipeline_mode=pl.Buffered(1))
    final = lambda *dims: pl.BlockSpec(dims, lambda b: (0,) * len(dims))
    vm = pltpu.VMEM
    return pl.pallas_call(
        partial(feed_kernel, devices),
        grid=(count,),
        in_specs=[
            one(length, width),
            one(PAD, width),
            pl.BlockSpec(
                (width, LANES), lambda b: (0, 3 * width // LANES), pipeline_mode=pl.Buffered(1)
            ),
            whole(width, cols),
            one(rows, width),
            one(rows, width),
        ],
        out_specs=[
            one(rows, width),
            one(rows, width),
            one(rows, width),
            final(width, cut),
            final(width, cols + LANES - cut),
        ],
        out_shape=[
            jax.ShapeDtypeStruct((count, rows, width), BF),
            jax.ShapeDtypeStruct((count, rows, width), FL),
            jax.ShapeDtypeStruct((count, rows, width), BF),
            jax.ShapeDtypeStruct((width, cut), BF),
            jax.ShapeDtypeStruct((width, cols + LANES - cut), BF),
        ],
        scratch_shapes=[
            vm((1, hid), FL),
            vm((LANES, width), FL),
            vm((width, LANES), FL),
            vm((width, cols), FL),
            vm((64, width), FL),
            vm((8, hid), FL),
            vm((rows, width), FL),
            vm((rows, width), FL),
            vm((rows, 1), FL),
            vm((rows, width), BF),
            vm((rows, width), FL),
            vm((rows, width), BF),
            vm((rows, hid), BF),
            vm((rows, hid), FL),
            vm((rows, hid), BF),
            vm((rows, width), BF),
            vm((count * PAD, width), BF),
            vm((count * PAD, width), BF),
            vm((count * PAD, width), BF),
            vm((count * PAD, width), BF),
            vm((count * PAD, hid), BF),
            vm((count * PAD, hid), BF),
            vm((width + ONES, length), BF),
            vm((width, length), BF),
        ],
        compiler_params=pltpu.CompilerParams(vmem_limit_bytes=60 << 20),
        name="feed",
    )(tok, state, near, wide, mixed, cot)


def return_kernel(
    qkv_ref,
    pt_ref,
    ptk_ref,
    ptq_ref,
    gm_ref,
    dj_ref,
    kt_ref,
    dpk_ref,
    dsk_ref,
    dqt_ref,
    dk_ref,
    dv_ref,
    s_ref,
    ds_ref,
):
    width = gm_ref.shape[2]
    length = gm_ref.shape[1] - PAD
    group = HALF // HDIM
    blocks = length // LANES
    gpad = group * PAD
    pairs = width // (2 * HDIM)
    masks = pair_masks(2 * HDIM)

    def columns(g, which):
        return slice(which * width + g * HALF, which * width + (g + 1) * HALF)

    def features(g):
        return slice(g * HALF, (g + 1) * HALF)

    def memory_keys(g):
        v_mem = spread(qkv_ref[0, length:, columns(g, 2)], group)
        dpk_ref[g * gpad : (g + 1) * gpad, :] = dot(v_mem, gm_ref[0, :length, features(g)], 1, 1)
        kt_ref[features(g), :] = qkv_ref[0, :length, columns(g, 1)].T

    def memory_queries(g):
        do_mem = spread(gm_ref[0, length:, features(g)], group)
        q_mem = spread(qkv_ref[0, length:, columns(g, 0)], group)
        prob = ptq_ref[0, :, g * gpad : (g + 1) * gpad]
        pf = prob.astype(FL)
        t = pf * dot(qkv_ref[0, :, columns(g, 2)], do_mem, 1, 1)
        ds = (t - pf * jnp.sum(t, axis=0, keepdims=True)).astype(BF)
        dv_ref[:, features(g)] = dot(prob, do_mem, 1, 0)
        dk_ref[:, features(g)] = dot(ds, q_mem, 1, 0)
        dq = fold(dot(ds, qkv_ref[0, :, columns(g, 1)], 0, 0), group)
        dj_ref[0, length:, features(g)] = (dq * SCALE).astype(BF)

    def rise(p, i, slot):
        low, live = i * LANES, (i + 1) * LANES
        base = i * (i + 1) // 2 * LANES
        at = p * 2 * HDIM
        dop = gm_ref[0, low:live, at : at + 2 * HDIM]
        both = jnp.concatenate([dop * masks[0], dop * masks[1]], axis=0)
        dp = dot(qkv_ref[0, :live, 2 * width + at : 2 * width + at + 2 * HDIM], both, 1, 1)
        t = pt_ref[0, p, base : base + live, :].astype(FL) * dp
        s_ref[slot, :live, :] = t
        total = jnp.sum(t, axis=0, keepdims=True)
        deltas = []
        for side in range(2):
            own = slice((2 * p + side) * PAD, (2 * p + side + 1) * PAD)
            tm = ptk_ref[0, own, low:live].astype(FL) * dpk_ref[own, low:live]
            deltas.append(total[:, side * LANES : (side + 1) * LANES] + jnp.sum(tm, axis=0, keepdims=True))
        return deltas

    def settle(p, i, slot, deltas):
        low, live = i * LANES, (i + 1) * LANES
        base = i * (i + 1) // 2 * LANES
        pf = pt_ref[0, p, base : base + live, :].astype(FL)
        ds = s_ref[slot, :live, :] - pf * jnp.concatenate(deltas, axis=1)
        ds_ref[p % 2, base : base + live, :] = ds.astype(BF)
        for side, delta in enumerate(deltas):
            own = slice((2 * p + side) * PAD, (2 * p + side + 1) * PAD)
            pm = ptk_ref[0, own, low:live].astype(FL)
            dsk_ref[own, low:live] = (pm * (dpk_ref[own, low:live] - delta)).astype(BF)

    def gather_rows(p, source, other, into):
        lanes = slice(p * 2 * HDIM, (p + 1) * 2 * HDIM)
        both = []
        for i in range(blocks):
            rows = other[i * LANES : (i + 1) * LANES]
            both.append(jnp.concatenate([rows * masks[0], rows * masks[1]], axis=0))
        for begin in range(0, length, HALF):
            first = begin // LANES
            full = range(first + 1, blocks)
            starts = [i * (i + 1) // 2 * LANES + begin for i in full]
            into[begin : begin + HALF, lanes] += dot(
                jnp.concatenate([source(slice(at, at + HALF)) for at in starts], axis=1),
                jnp.concatenate([both[i] for i in full], axis=0),
                1,
                0,
            )
            at = first * (first + 1) // 2 * LANES + begin
            into[begin : begin + LANES, lanes] += dot(source(slice(at, at + LANES)), both[first], 1, 0)

    def values_back(p):
        lanes = slice(p * 2 * HDIM, (p + 1) * 2 * HDIM)
        gather_rows(p, lambda r: pt_ref[0, p, r, :], gm_ref[0, :length, lanes], dv_ref)

    def keys_back(p):
        lanes = slice(p * 2 * HDIM, (p + 1) * 2 * HDIM)
        gather_rows(p, lambda r: ds_ref[p % 2, r, :], qkv_ref[0, :length, lanes], dk_ref)

    def queries_back(p):
        at = p * 2 * HDIM
        for i in range(blocks):
            low, live = i * LANES, (i + 1) * LANES
            base = i * (i + 1) // 2 * LANES
            made = dot(kt_ref[at : at + 2 * HDIM, :live], ds_ref[p % 2, base : base + live, :], 1, 0)
            for side in range(2):
                dqt_ref[at + side * HDIM : at + (side + 1) * HDIM, low:live] = made[
                    side * HDIM : (side + 1) * HDIM, side * LANES : (side + 1) * LANES
                ]

    def finish(g):
        own = slice(g * gpad, (g + 1) * gpad)
        k_mem = spread(qkv_ref[0, length:, columns(g, 1)], group)
        dq_t = dqt_ref[features(g), :] + dot(k_mem, dsk_ref[own, :], 0, 0)
        dj_ref[0, :length, features(g)] = (dq_t * SCALE).astype(BF).T
        dv_mem = fold(dot(ptk_ref[0, own, :], gm_ref[0, :length, features(g)], 1, 0), group)
        dk_mem = fold(dot(dsk_ref[own, :], qkv_ref[0, :length, columns(g, 0)], 1, 0), group)
        dj_ref[0, :length, columns(g, 1)] = dk_ref[:length, features(g)].astype(BF)
        dj_ref[0, :length, columns(g, 2)] = dv_ref[:length, features(g)].astype(BF)
        dj_ref[0, length:, columns(g, 1)] = (dk_ref[length:, features(g)] + dk_mem).astype(BF)
        dj_ref[0, length:, columns(g, 2)] = (dv_ref[length:, features(g)] + dv_mem).astype(BF)

    groups = width // HALF
    memory_keys(0)
    units = [(p, i) for p in range(pairs) for i in reversed(range(blocks))]
    per_pair = blocks
    deltas = {}
    later = []
    for u in range(len(units) + 2):
        if u < len(units):
            deltas[u] = rise(*units[u], u % SLOTS)
        if u >= 2:
            settle(*units[u - 2], (u - 2) % SLOTS, deltas.pop(u - 2))
            if (u - 1) % per_pair == 0:
                p = (u - 1) // per_pair - 1
                later += [(queries_back, p), (keys_back, p)]
                if p % 2 == 1:
                    later.append((finish, p // 2))
        if u < len(units):
            p, at = u // per_pair, u % per_pair
            if at == 0 and p % 2 == 0:
                memory_queries(p // 2)
            if at == 3:
                values_back(p)
            if at == 2 and p % 2 == 1 and p // 2 + 1 < groups:
                memory_keys(p // 2 + 1)
        if later:
            work, arg = later.pop(0)
            work(arg)
    for work, arg in later:
        work(arg)


def go_back(begin, count, qkv, pt, ptk, ptq, gm):
    rows, width = gm.shape[1:]
    length = rows - PAD
    heads = width // HDIM
    one = lambda *dims: pl.BlockSpec((1,) + dims, lambda b: (b + begin,) + (0,) * len(dims))
    vm = pltpu.VMEM
    return pl.pallas_call(
        return_kernel,
        grid=(count,),
        in_specs=[
            one(rows, 3 * width),
            one(*pt.shape[1:]),
            one(heads * PAD, length),
            one(rows, heads * PAD),
            one(rows, width),
        ],
        out_specs=pl.BlockSpec((1, rows, 3 * width), lambda b: (b, 0, 0)),
        out_shape=jax.ShapeDtypeStruct((count, rows, 3 * width), BF),
        scratch_shapes=[
            vm((width, length), BF),
            vm((heads * PAD, length), FL),
            vm((heads * PAD, length), BF),
            vm((width, length), FL),
            vm((rows, width), FL),
            vm((rows, width), FL),
            vm((SLOTS, length, HALF), FL),
            vm((2, pt.shape[2], HALF), BF),
        ],
        compiler_params=pltpu.CompilerParams(vmem_limit_bytes=48 << 20),
        cost_estimate=pl.CostEstimate(flops=count * 10**10, bytes_accessed=count * 10**7, transcendentals=0),
        name="go_back",
    )(qkv, pt, ptk, ptq, gm)


def weigh_kernel(
    begins,
    tok_ref,
    state_ref,
    one_ref,
    inw_ref,
    *refs,
):
    dj_refs, refs = refs[: len(begins)], refs[len(begins) :]
    gone_ref, gtwo_ref, acc_ref, left_ref, m_in_ref, m_dj_ref, side_ref, memb_ref = refs
    cut = gone_ref.shape[1]
    step = pl.program_id(0)
    last = pl.num_programs(0) - 1
    length, width = tok_ref.shape[1:]
    ends = begins[1:] + [last + 1]

    @pl.when(step == 0)
    def _():
        acc_ref[...] = jnp.zeros_like(acc_ref)
        side_ref[...] = jnp.zeros_like(side_ref)
        memb_ref[...] = inw_ref[:, 3 * width :].astype(FL).T
        left_ref[width:, :] = jnp.ones((ONES, length), BF)

    mem = pl.ds(pl.multiple_of(step * PAD, PAD), PAD)
    m_in_ref[mem, :] = (state_ref[0].astype(FL) + memb_ref[:PAD]).astype(BF)
    side_ref[0:PAD, :] += one_ref[0]
    left_ref[:width, :] = tok_ref[0].T
    for g, dj_ref in enumerate(dj_refs):

        @pl.when((step >= begins[g]) & (step < ends[g]))
        def _(dj_ref=dj_ref):
            m_dj_ref[mem, :] = dj_ref[0, length:, :]
            for j in range(0, 3 * width, FCHUNK):
                c = slice(j, j + FCHUNK)
                acc_ref[:, c] += dot(left_ref[...], dj_ref[0, :length, c], 1, 0)

    @pl.when(step == last)
    def _():
        more = jnp.concatenate([m_in_ref[...].T, jnp.ones((ONES, m_in_ref.shape[0]), BF)], axis=0)
        for j in range(0, 3 * width, FCHUNK):
            c = slice(j, j + FCHUNK)
            acc_ref[:, c] += dot(more, m_dj_ref[:, c], 1, 0)
        gone_ref[...] = acc_ref[:width, :cut].astype(BF)
        gtwo_ref[:, : 3 * width - cut] = acc_ref[:width, cut:].astype(BF)
        back = dot(m_dj_ref[...], inw_ref[:, : 3 * width], 1, 1)
        side_ref[0:PAD, :] += jnp.sum(back.reshape(last + 1, PAD, width), axis=0)
        side_ref[PAD : PAD + 1, :] = acc_ref[width : width + 1, :width]
        side_ref[PAD + 1 : PAD + 2, :] = acc_ref[width : width + 1, 2 * width :]
        gtwo_ref[:, 3 * width - cut :] = side_ref[...].T.astype(BF)


def weigh(tok, state, near, one_grad, djs, begins):
    count, length, width = tok.shape
    rows = length + PAD
    cut = halfway(3 * width + LANES)
    one = lambda *dims: pl.BlockSpec((1,) + dims, lambda b: (b,) + (0,) * len(dims))
    whole = lambda *dims: pl.BlockSpec(dims, lambda b: (0,) * len(dims), pipeline_mode=pl.Buffered(1))
    final = lambda *dims: pl.BlockSpec(dims, lambda b: (0,) * len(dims))
    part = lambda g: pl.BlockSpec(
        (1, rows, 3 * width), lambda b: (jnp.clip(b - begins[g], 0, djs[g].shape[0] - 1), 0, 0)
    )
    vm = pltpu.VMEM
    return pl.pallas_call(
        partial(weigh_kernel, begins),
        grid=(count,),
        in_specs=[
            one(length, width),
            one(PAD, width),
            pl.BlockSpec((1, PAD, width), lambda b: (b, length // PAD, 0)),
            whole(width, 3 * width + LANES),
        ]
        + [part(g) for g in range(len(djs))],
        out_specs=[final(width, cut), final(width, 3 * width + LANES - cut)],
        out_shape=[
            jax.ShapeDtypeStruct((width, cut), BF),
            jax.ShapeDtypeStruct((width, 3 * width + LANES - cut), BF),
        ],
        scratch_shapes=[
            vm((width + ONES, 3 * width), FL),
            vm((width + ONES, length), BF),
            vm((count * PAD, width), BF),
            vm((count * PAD, 3 * width), BF),
            vm((LANES, width), FL),
            vm((LANES, width), FL),
        ],
        compiler_params=pltpu.CompilerParams(vmem_limit_bytes=48 << 20),
        cost_estimate=pl.CostEstimate(flops=count * 10**9, bytes_accessed=count * 3 * 10**6, transcendentals=0),
        name="weigh",
    )(tok, state, one_grad, near, *djs)


def descend_kernel(one_ref, dj_ref, inw_ref, grad_ref):
    width = one_ref.shape[2]
    grad_ref[0] = one_ref[0] + dot(dj_ref[0], inw_ref[:, : 3 * width], 1, 1)


def descend(total, begin, one_grad, dj, near, into):
    count, rows, wide = dj.shape
    width = one_grad.shape[2]
    length = rows - PAD
    shift = lambda *dims: pl.BlockSpec((1,) + dims, lambda b: (b + begin, 0, 0))
    kept = () if into is None else (into,)

    def kernel(one_ref, dj_ref, inw_ref, *rest):
        descend_kernel(one_ref, dj_ref, inw_ref, rest[-1])

    return pl.pallas_call(
        kernel,
        grid=(count,),
        in_specs=[
            shift(length, width),
            pl.BlockSpec((1, length, wide), lambda b: (b, 0, 0)),
            pl.BlockSpec((width, wide + LANES), lambda b: (0, 0), pipeline_mode=pl.Buffered(1)),
        ]
        + [pl.BlockSpec(memory_space=pl.ANY)] * len(kept),
        out_specs=shift(length, width),
        out_shape=jax.ShapeDtypeStruct((total, length, width), FL),
        input_output_aliases={3: 0} if kept else {},
        compiler_params=pltpu.CompilerParams(vmem_limit_bytes=32 << 20),
        cost_estimate=pl.CostEstimate(flops=count * 10**9, bytes_accessed=count * 4 * 10**6, transcendentals=0),
        name="descend",
    )(one_grad, dj, near, *kept)


def pack_kernel(in_ref, up_ref, down_ref, out_ref, vec_ref, bias_ref, mem_ref, near_ref, far_ref, flip_ref):
    shard, cols = in_ref.shape
    hid, width = up_ref.shape[1], out_ref.shape[1]
    flip_ref[...] = jnp.zeros_like(flip_ref)
    flip_ref[PAD : PAD + 8, :shard] = vec_ref[...]
    flip_ref[...] = flip_ref[...].T
    flip_ref[:shard, : mem_ref.shape[1]] = mem_ref[...]
    flip_ref[0:1, BIAS : BIAS + bias_ref.shape[1]] = bias_ref[...]
    near_ref[:, :cols] = in_ref[...].astype(BF)
    near_ref[:, cols:] = flip_ref[:shard].astype(BF)
    far_ref[:, :hid] = up_ref[...].astype(BF)
    far_ref[:, hid : 2 * hid] = down_ref[...].astype(BF)
    far_ref[:, 2 * hid :] = out_ref[...].astype(BF)


def pack(in_w, up_w, down_t, out_t, vectors, bias, mem_t):
    shard, cols = in_w.shape
    wide = 2 * up_w.shape[1] + out_t.shape[1]
    return pl.pallas_call(
        pack_kernel,
        out_shape=[
            jax.ShapeDtypeStruct((shard, cols + LANES), BF),
            jax.ShapeDtypeStruct((shard, wide), BF),
        ],
        scratch_shapes=[pltpu.VMEM((LANES, LANES), FL)],
        name="pack",
    )(in_w, up_w, down_t, out_t, vectors, bias, mem_t)


def square_kernel(cols, *refs):
    held_refs, got_refs, (far_ref, near_ref, sum_ref) = refs[:2], refs[2:4], refs[4:]
    at = 0
    for held_ref, got_ref in zip(held_refs, got_refs):
        size = held_ref.shape[1]
        near_ref[:, at : at + size] = held_ref[...] + got_ref[...].astype(FL)
        at += size
    wide = far_ref.shape[1] - LANES
    near, far = near_ref[:, :cols], far_ref[:, :wide]
    side = near_ref[:, cols:] + far_ref[:, wide:]
    total = jnp.sum(near * near) + jnp.sum(far * far) + jnp.sum(side * side)
    sum_ref[...] = jnp.full(sum_ref.shape, total, FL)


def adam_kernel(sizes, rates, decays, near_ref, far_ref, total_ref, *refs):
    cols, hid, width = sizes
    state_refs, new_refs, norm_ref, flip_ref = refs[:21], refs[21:42], refs[42], refs[43]
    shard = near_ref.shape[0]
    norm = jnp.sqrt(total_ref[...])
    norm_ref[...] = norm[0:1, 0:1]
    factor = (1.0 / jnp.maximum(norm, 1.0))[0:1, 0:1]
    side = near_ref[:, cols:] + far_ref[:, 2 * hid + width :]
    flip_ref[...] = jnp.zeros_like(flip_ref)
    flip_ref[:shard] = side
    turned = flip_ref[...].T
    bias = pltpu.roll(side, LANES - BIAS, 1)
    grads = (
        near_ref[:, :cols],
        far_ref[:, 2 * hid : 2 * hid + width],
        far_ref[:, :hid],
        far_ref[:, hid : 2 * hid],
        turned[PAD : PAD + 8, :shard],
        bias[0:1, : state_refs[15].shape[1]],
        side[:, : state_refs[18].shape[1]],
    )
    correction = 1.0 - 0.5**STEP
    for i in range(7):
        weight, first, second = (state_refs[3 * i + k][...] for k in range(3))
        grad = grads[i] * factor
        first_new = 0.5 * first + 0.5 * grad
        second_new = 0.5 * second + 0.5 * grad * grad
        step = first_new / correction / (jnp.sqrt(second_new / correction) + 1e-08)
        new_refs[3 * i][...] = weight - rates[i] * (step + decays[i] * weight)
        new_refs[3 * i + 1][...] = first_new
        new_refs[3 * i + 2][...] = second_new


def exchange(x, bit, devices):
    return lax.ppermute(x, AXES, [(i, i ^ bit) for i in range(devices)])


def beside(got, sent, work):
    if work is None:
        return got, None
    made = work(lambda value: lax.optimization_barrier((value, sent))[0])
    return lax.optimization_barrier((got, made))


def gather(x, devices, index, works):
    rows, cols = x.shape
    held = x[None]
    results = []
    bits = devices.bit_length() - 1
    for step in range(bits):
        bit = devices >> (step + 1)
        got = exchange(held, bit, devices)
        got, made = beside(got, held, works[step] if step < len(works) else None)
        results.append(made)
        upper = (index & bit) != 0
        held = jnp.stack([jnp.where(upper, got, held), jnp.where(upper, held, got)], axis=1)
        held = held.reshape(-1, rows, cols)
    return held.reshape(devices * rows, cols), [made for made in results if made is not None]


def halve(held, got, place, upper):
    total = held if got is None else held.astype(FL) + got.astype(FL)
    low, high = (lax.index_in_dim(total, i, place, keepdims=False) for i in range(2))
    return jnp.where(upper, high, low), jnp.where(upper, low, high).astype(BF)


def scatter_sum(halves, devices, index, works, then=None):
    rows = halves[0].shape[0] // devices
    bits = devices.bit_length() - 1
    orders = [list(range(bits)) for _ in range(2)]
    if bits > 2:
        orders[1][1:3] = [2, 1]
    held = [half.reshape((2,) * bits + (rows, -1)) for half in halves]
    got = [None, None]
    results = []
    for step in range(bits):
        work = works[step] if step < len(works) else None
        send = [None, None]
        for half, order in enumerate(orders):
            bit = order[step]
            place = sum(1 for other in order[step:] if other > bit)
            upper = (index & (1 << bit)) != 0
            held[half], send[half] = halve(held[half], got[half], place, upper)
        if step < 3:
            got = [exchange(value, 1 << order[step], devices) for value, order in zip(send, orders)]
            got, made = beside(got, send, work)
        else:
            sent = jnp.concatenate(send, axis=-1)
            if step == bits - 1 and then is None:
                return [value.astype(FL).reshape(rows, -1) for value in held], sent, results
            both, made = beside(exchange(sent, 1 << orders[0][step], devices), sent, work)
            cut = send[0].shape[-1]
            got = [both[..., :cut], both[..., cut:]]
        results.append(made)
        if step == 0 and then is not None:
            then(got)
    return [value.astype(FL).reshape(rows, -1) for value in held], [value.reshape(rows, -1) for value in got], results


def butterfly(x, devices):
    for step in range(devices.bit_length() - 1):
        x = x + exchange(x, 1 << step, devices)
    return x


def per_device(
    devices,
    tokens,
    memory_state,
    cotangent,
    in_weight,
    in_first,
    in_second,
    out_weight,
    out_first,
    out_second,
    up_weight,
    up_first,
    up_second,
    down_weight,
    down_first,
    down_second,
    vectors,
    vectors_first,
    vectors_second,
    up_bias,
    up_bias_first,
    up_bias_second,
    memory_embed,
    memory_first,
    memory_second,
):
    index = lax.axis_index(AXES)
    micro, local, length, width = tokens.shape
    count = micro * local
    extra = memory_state.shape[2]
    shard = in_weight.shape[0]
    hid = up_weight.shape[1]
    per_bias = up_bias.shape[0] // shard

    near, far = pack(
        in_weight,
        up_weight,
        down_weight.T,
        out_weight.T,
        vectors,
        up_bias.reshape(1, -1),
        memory_embed.T,
    )
    wide = lax.all_gather(far, AXES, axis=0, tiled=True)

    def pad_state(tie):
        rows = tie(memory_state).reshape(count, extra, width)
        return jnp.pad(rows, ((0, 0), (0, PAD - extra), (0, 0)))

    def align(tie):
        cot = tie(cotangent).reshape(count, extra + length, width)
        return jnp.concatenate(
            [cot[:, extra:], cot[:, :extra], jnp.zeros((count, PAD - extra, width), BF)], axis=1
        )

    near, (state, cot) = gather(near, devices, index, [pad_state, None, None, align])

    tok = tokens.reshape(count, length, width)

    qkv, pt, ptk, ptq, mixed = attend(extra, tok, state, near)
    out, one_grad, gm, *gwide = feed(devices, tok, state, near, wide, mixed, cot)

    def split(sizes):
        begins = [0]
        for size in sizes:
            begins.append(begins[-1] + size)
        return list(zip(begins, sizes))

    djs = []

    def back(begin, size):
        def work(tie):
            djs.append(go_back(begin, size, tie(qkv), pt, ptk, ptq, gm))
            return djs[-1]

        return work

    def whole_weigh(tie):
        return weigh(tie(tok), state, near, one_grad, djs, [begin for begin, _ in runs])

    runs = split(BACK) if sum(BACK) == count else split([count])
    held, got, made = scatter_sum(gwide, devices, index, [back(*run) for run in runs] + [whole_weigh])
    gin = made[len(runs)]
    far_held, far_sent = held, got
    far_got = []

    def last_far(first_got):
        tied = lax.optimization_barrier((far_sent, first_got))[0]
        both = exchange(tied, devices // 2, devices).reshape(shard, -1)
        cut = far_held[0].shape[-1]
        far_got.extend([both[:, :cut], both[:, cut:]])

    grads = []

    def down(i):
        def work(tie):
            into = grads[-1] if grads else None
            grads.append(descend(count, runs[i][0], one_grad, tie(djs[i]), near, into))
            return grads[-1]

        return work

    def order(tie):
        rows = tie(out)
        rows = jnp.concatenate([rows[:, length : length + extra], rows[:, :length]], axis=1)
        return rows.reshape(micro, local, extra + length, width).transpose(0, 2, 1, 3)

    works = [down(i) for i in range(len(runs))] + [order]
    held, got, made = scatter_sum(gin, devices, index, works, last_far)
    input_grad = made[len(runs) - 1].reshape(micro, local, length, width)
    (far_held, far_got), _ = lax.optimization_barrier(((far_held, far_got), made[len(runs) - 1]))
    gfar = jnp.concatenate([mine + more.astype(FL) for mine, more in zip(far_held, far_got)], axis=1)

    gnear, squares = pl.pallas_call(
        partial(square_kernel, 3 * width),
        out_shape=[
            jax.ShapeDtypeStruct((shard, 3 * width + LANES), FL),
            jax.ShapeDtypeStruct((8, LANES), FL),
        ],
        name="squares",
    )(*held, *got, gfar)
    squares = butterfly(squares, devices)
    output = made[len(runs)].transpose(0, 2, 1, 3)
    total_rows = extra + length
    rates = (
        0.5 * width ** (-0.5),
        0.5 * (width * 32 // total_rows) ** (-0.5),
        0.5 * width ** (-0.5),
        0.5 * hid ** (-0.5),
        0.1,
        0.1,
        0.5,
    )
    decays = (0.1, 0.1, 0.1, 0.1, 0.0, 0.0, 0.0)
    same = lambda value: value
    turn = lambda value: value.T
    flat = lambda value: value.reshape(1, -1)
    views = (same, turn, same, turn, same, flat, turn)
    states = (
        (in_weight, in_first, in_second),
        (out_weight, out_first, out_second),
        (up_weight, up_first, up_second),
        (down_weight, down_first, down_second),
        (vectors, vectors_first, vectors_second),
        (up_bias, up_bias_first, up_bias_second),
        (memory_embed, memory_first, memory_second),
    )
    held = [view(value) for view, group in zip(views, states) for value in group]
    *new, norm = pl.pallas_call(
        partial(adam_kernel, (3 * width, hid, width), rates, decays),
        out_shape=[jax.ShapeDtypeStruct(value.shape, FL) for value in held]
        + [jax.ShapeDtypeStruct((1, 1), FL)],
        scratch_shapes=[pltpu.VMEM((LANES, LANES), FL)],
        name="adam",
    )(gnear, gfar, squares, *held)
    back_views = (same, turn, same, turn, same, lambda value: value.reshape(-1), turn)
    results = [back_views[i // 3](value) for i, value in enumerate(new)]
    return (output, input_grad, *results, norm.reshape(()))


def solution(mesh):
    blocks = P(None, AXES, None, None)
    lead = P(AXES, None)
    trail = P(None, AXES)
    flat = P(AXES)
    weights = (lead,) * 3 + (trail,) * 3 + (lead,) * 3 + (trail,) * 6 + (flat,) * 3 + (trail,) * 3
    devices = mesh.shape["dp"] * mesh.shape["fsdp"]
    return jax.shard_map(
        partial(per_device, devices),
        mesh=mesh,
        in_specs=(blocks,) * 3 + weights,
        out_specs=(blocks,) * 2 + weights + (P(),),
        check_vma=False,
    )
```

```python
from functools import partial

import jax
import jax.numpy as jnp
from jax import lax
from jax.experimental import pallas as pl
from jax.experimental.pallas import tpu as pltpu
from jax.sharding import PartitionSpec as P

STEP = 7
HDIM = 64
PAD = 32
HALF = 256
FCHUNK = 256
ROWS = 32
BF = jnp.bfloat16
FL = jnp.float32
AXES = ("dp", "fsdp")
NEG = -1e30
EPS = 1e-05
SCALE = HDIM ** (-0.5)
LANES = 128
BIAS = 64
SLOTS = 6
PLAN_MORE = (0, 2, 4, 5)
PLAN_LAST = (2, 4, 7, 5)
CUT = 3
ONES = 16
BACK = (2, 4, 2)


def dot(a, b, ca, cb):
    return lax.dot_general(a, b, (((ca,), (cb,)), ((), ())), preferred_element_type=FL)


def head_mask(rows, width):
    row = lax.broadcasted_iota(jnp.int32, (rows, width), 0) // PAD
    col = lax.broadcasted_iota(jnp.int32, (rows, width), 1) // HDIM
    return row == col


def spread(x, heads):
    tiled = jnp.concatenate([x.astype(FL)] * heads, axis=0)
    return jnp.where(head_mask(*tiled.shape), tiled, 0.0).astype(BF)


def fold(y, heads):
    own = jnp.where(head_mask(*y.shape), y, 0.0)
    return sum(own[h * PAD : (h + 1) * PAD] for h in range(heads))


def pair_masks(width):
    col = lax.broadcasted_iota(jnp.int32, (1, width), 1)
    low = jnp.where(col < HDIM, 1.0, 0.0)
    return low.astype(BF), (1.0 - low).astype(BF)


def attend_kernel(
    extra,
    tok_ref,
    state_ref,
    first_ref,
    first_state_ref,
    inw_ref,
    qkv_ref,
    pt_ref,
    ptk_ref,
    ptq_ref,
    mixed_ref,
    vt_ref,
    sk_ref,
    ot_ref,
    side_ref,
    inp_ref,
    s_ref,
    ahead_ref,
):
    length, width = tok_ref.shape[1:]
    rows = length + PAD
    group = HALF // HDIM
    gpad = group * PAD
    diag = lax.broadcasted_iota(jnp.int32, (LANES, LANES), 0) <= lax.broadcasted_iota(
        jnp.int32, (LANES, LANES), 1
    )
    key_live = lax.broadcasted_iota(jnp.int32, (gpad, 1), 0) % PAD < extra
    place_live = lax.broadcasted_iota(jnp.int32, (rows, 1), 0) < length + extra
    masks = pair_masks(2 * HDIM)

    def columns(g, which):
        return slice(which * width + g * HALF, which * width + (g + 1) * HALF)

    def ahead(which):
        return slice(which * HALF, (which + 1) * HALF)

    def take(source, source_state):
        inp_ref[:length] = source[0]
        inp_ref[length:] = (source_state[0].astype(FL) + side_ref[:PAD]).astype(BF)

    def project(g, which):
        feat = slice(g * HALF, (g + 1) * HALF)
        made = dot(inp_ref[...], inw_ref[:, columns(g, which)], 1, 0)
        if which == 0:
            made = (made + side_ref[PAD : PAD + 1, feat]) * SCALE
        if which == 2:
            made = made + side_ref[PAD + 1 : PAD + 2, feat]
        made = made.astype(BF)
        if g:
            qkv_ref[0, :, columns(g, which)] = made
        else:
            ahead_ref[:, ahead(which)] = made
        if which == 2:
            vt_ref[feat, :] = made[:length].T

    def memory_keys(g):
        if g:
            mem, query = qkv_ref[0, length:, columns(g, 1)], qkv_ref[0, :length, columns(g, 0)]
        else:
            mem, query = ahead_ref[length:, ahead(1)], ahead_ref[:length, ahead(0)]
        made = dot(spread(mem, group), query, 1, 1)
        sk_ref[g * gpad : (g + 1) * gpad, :] = jnp.where(key_live, made, NEG)

    def memory_queries(g):
        q_mem = spread(qkv_ref[0, length:, columns(g, 0)], group)
        sq = jnp.where(place_live, dot(qkv_ref[0, :, columns(g, 1)], q_mem, 1, 1), NEG)
        eq = jnp.exp(sq - jnp.max(sq, axis=0, keepdims=True))
        probs = (eq * (1.0 / jnp.sum(eq, axis=0, keepdims=True))).astype(BF)
        ptq_ref[0, :, g * gpad : (g + 1) * gpad] = probs
        om = dot(probs, qkv_ref[0, :, columns(g, 2)], 0, 0)
        mixed_ref[0, length:, g * HALF : (g + 1) * HALF] = fold(om, group).astype(BF)

    @pl.when(pl.program_id(0) == 0)
    def _():
        side_ref[...] = inw_ref[:, 3 * width :].astype(FL).T
        take(first_ref, first_state_ref)
        for which in range(3):
            project(0, which)
        memory_keys(0)

    def score(p, i, slot):
        low, live = i * LANES, (i + 1) * LANES
        at = p * 2 * HDIM
        qp = qkv_ref[0, low:live, at : at + 2 * HDIM]
        both = jnp.concatenate([qp * masks[0], qp * masks[1]], axis=0)
        s = dot(qkv_ref[0, :live, width + at : width + at + 2 * HDIM], both, 1, 1)
        tops = []
        for side in range(2):
            lanes = slice(side * LANES, (side + 1) * LANES)
            own = slice((2 * p + side) * PAD, (2 * p + side + 1) * PAD)
            edge = jnp.where(diag, s[low:live, lanes], NEG)
            s_ref[slot, low:live, lanes] = edge
            top = jnp.maximum(
                jnp.max(edge, axis=0, keepdims=True), jnp.max(sk_ref[own, low:live], axis=0, keepdims=True)
            )
            if low:
                s_ref[slot, :low, lanes] = s[:low, lanes]
                top = jnp.maximum(top, jnp.max(s[:low, lanes], axis=0, keepdims=True))
            tops.append(top)
        return tops

    def soften(p, i, slot, tops):
        low, live = i * LANES, (i + 1) * LANES
        base = i * (i + 1) // 2 * LANES
        made = []
        for side, top in enumerate(tops):
            own = slice((2 * p + side) * PAD, (2 * p + side + 1) * PAD)
            e = jnp.exp(s_ref[slot, :live, side * LANES : (side + 1) * LANES] - top)
            e_mem = jnp.exp(sk_ref[own, low:live] - top)
            total = jnp.sum(e, axis=0, keepdims=True) + jnp.sum(e_mem, axis=0, keepdims=True)
            share = 1.0 / total
            made.append(e * share)
            ptk_ref[0, own, low:live] = (e_mem * share).astype(BF)
        pt_ref[0, p, base : base + live, :] = jnp.concatenate(made, axis=1).astype(BF)

    def mix(p, i):
        low, live = i * LANES, (i + 1) * LANES
        base = i * (i + 1) // 2 * LANES
        at = p * 2 * HDIM
        made = dot(vt_ref[at : at + 2 * HDIM, :live], pt_ref[0, p, base : base + live, :], 1, 0)
        for side in range(2):
            ot_ref[at + side * HDIM : at + (side + 1) * HDIM, low:live] = made[
                side * HDIM : (side + 1) * HDIM, side * LANES : (side + 1) * LANES
            ]

    def finish(g):
        v_mem = spread(qkv_ref[0, length:, columns(g, 2)], group)
        feat = slice(g * HALF, (g + 1) * HALF)
        om_t = ot_ref[feat, :] + dot(v_mem, ptk_ref[0, g * gpad : (g + 1) * gpad, :], 0, 0)
        mixed_ref[0, :length, feat] = om_t.astype(BF).T

    groups = width // HALF
    blocks = length // LANES
    units = [(p, i) for p in range(width // (2 * HDIM)) for i in range(blocks)]
    per_group = group // 2 * blocks
    for which in range(3):
        qkv_ref[0, :, columns(0, which)] = ahead_ref[:, ahead(which)]
    works = {}
    for g in range(groups):
        at = g * per_group
        more = g + 1 < groups
        plan = PLAN_MORE if more else PLAN_LAST
        works.setdefault(at + 1, []).append((memory_queries, g))
        if g:
            works.setdefault(at + 4, []).append((finish, g - 1))
        if not more:
            works.setdefault(at, []).append((take, tok_ref, state_ref))
        for which in range(3):
            works.setdefault(at + plan[which], []).append((project, g + 1 if more else 0, which))
        works.setdefault(at + plan[3], []).append((memory_keys, g + 1 if more else 0))
    tops = {}
    for u in range(len(units) + 5):
        if u < len(units):
            tops[u] = score(*units[u], u % SLOTS)
        if 3 <= u <= len(units) + 2:
            soften(*units[u - 3], (u - 3) % SLOTS, tops.pop(u - 3))
        if u >= 5:
            mix(*units[u - 5])
        for work, *given in works.get(u, ()):
            work(*given)
    finish(groups - 1)


def attend(extra, tok, state, near):
    count, length, width = tok.shape
    heads = width // HDIM
    rows = length + PAD
    blocks = length // LANES
    ptrows = blocks * (blocks + 1) // 2 * LANES
    one = lambda *dims: pl.BlockSpec((1,) + dims, lambda b: (b,) + (0,) * len(dims))
    after = lambda *dims: pl.BlockSpec((1,) + dims, lambda b: (jnp.minimum(b + 1, count - 1), 0, 0))
    whole = lambda *dims: pl.BlockSpec(dims, lambda b: (0,) * len(dims), pipeline_mode=pl.Buffered(1))
    return pl.pallas_call(
        partial(attend_kernel, extra),
        grid=(count,),
        in_specs=[
            after(length, width),
            after(PAD, width),
            pl.BlockSpec((1, length, width), lambda b: (0, 0, 0), pipeline_mode=pl.Buffered(1)),
            pl.BlockSpec((1, PAD, width), lambda b: (0, 0, 0), pipeline_mode=pl.Buffered(1)),
            whole(width, 3 * width + LANES),
        ],
        out_specs=[
            one(rows, 3 * width),
            one(heads // 2, ptrows, HALF),
            one(heads * PAD, length),
            one(rows, heads * PAD),
            one(rows, width),
        ],
        out_shape=[
            jax.ShapeDtypeStruct((count, rows, 3 * width), BF),
            jax.ShapeDtypeStruct((count, heads // 2, ptrows, HALF), BF),
            jax.ShapeDtypeStruct((count, heads * PAD, length), BF),
            jax.ShapeDtypeStruct((count, rows, heads * PAD), BF),
            jax.ShapeDtypeStruct((count, rows, width), BF),
        ],
        scratch_shapes=[
            pltpu.VMEM((width, length), BF),
            pltpu.VMEM((heads * PAD, length), FL),
            pltpu.VMEM((width, length), FL),
            pltpu.VMEM((LANES, width), FL),
            pltpu.VMEM((rows, width), BF),
            pltpu.VMEM((SLOTS, length, HALF), FL),
            pltpu.VMEM((rows, 3 * HALF), BF),
        ],
        compiler_params=pltpu.CompilerParams(vmem_limit_bytes=40 << 20),
        name="attend",
    )(tok, state, tok, state, near)


def norm_rows(x):
    center = x - jnp.mean(x, axis=-1, keepdims=True)
    rstd = lax.rsqrt(jnp.mean(center * center, axis=-1, keepdims=True) + EPS)
    return center * rstd, rstd


def norm_back(grad, normed, rstd, gain):
    scaled = grad * gain
    return rstd * (
        scaled
        - jnp.mean(scaled, axis=-1, keepdims=True)
        - normed * jnp.mean(scaled * normed, axis=-1, keepdims=True)
    )


def by_eight(x):
    return jnp.sum(x.reshape(x.shape[0] // 8, 8, x.shape[1]), axis=0)


def feed_kernel(
    devices,
    tok_ref,
    state_ref,
    small_ref,
    wide_ref,
    mixed_ref,
    cot_ref,
    out_ref,
    one_ref,
    gm_ref,
    gone_ref,
    gtwo_ref,
    upb_ref,
    side_ref,
    gside_ref,
    acc_ref,
    sums_ref,
    upb_sum_ref,
    att_ref,
    n1_ref,
    r1_ref,
    low_ref,
    g2_ref,
    gb_ref,
    hidden_ref,
    slope_ref,
    gpre_ref,
    ga_ref,
    m_low_ref,
    m_gb_ref,
    m_ga_ref,
    m_mixed_ref,
    m_hidden_ref,
    m_gpre_ref,
    low_t_ref,
    gb_t_ref,
):
    step = pl.program_id(0)
    last = pl.num_programs(0) - 1
    length, width = tok_ref.shape[1:]
    hid = upb_ref.shape[1]
    rows = length + PAD
    shard, per = width // devices, hid // devices
    up = slice(0, hid)
    down = slice(hid, 2 * hid)
    outw = slice(2 * hid, 2 * hid + width)

    @pl.when(step == 0)
    def _():
        acc_ref[...] = jnp.zeros_like(acc_ref)
        sums_ref[...] = jnp.zeros_like(sums_ref)
        upb_sum_ref[...] = jnp.zeros_like(upb_sum_ref)
        gpre_ref[...] = jnp.zeros_like(gpre_ref)
        low_t_ref[:width] = jnp.zeros((width, length), BF)
        low_t_ref[width:] = jnp.ones((ONES, length), BF)
        gside_ref[...] = small_ref[...].astype(FL)
        side_ref[...] = gside_ref[...].T
        for i in range(devices):
            upb_ref[:, i * per : (i + 1) * per] = gside_ref[i * shard : i * shard + 1, BIAS : BIAS + per]

    def put(at, value):
        cut = gone_ref.shape[1]
        if at < cut:
            gone_ref[:, at : at + value.shape[1]] = value.astype(BF)
        else:
            gtwo_ref[:, at - cut : at - cut + value.shape[1]] = value.astype(BF)

    def up_piece(j):
        c = slice(j, j + FCHUNK)
        made = dot(low_t_ref[...], gpre_ref[:length, c], 1, 0)
        acc_ref[:, c] += made[:width]
        upb_sum_ref[:, c] += made[width : width + 8]

    def down_piece(j):
        c = slice(j, j + FCHUNK)
        d = slice(hid + j, hid + j + FCHUNK)
        acc_ref[:, d] += dot(gb_t_ref[...], hidden_ref[:length, c], 1, 0)

    pieces = range(0, hid, FCHUNK)
    chunks = range(0, rows, ROWS)
    fills = [(up_piece, j) for j in pieces]

    def weave(stage, sums, works):
        totals = None
        done = 0
        for i, at in enumerate(chunks):
            made = stage(slice(at, at + ROWS))
            totals = made if totals is None else [x + y for x, y in zip(totals, made)]
            while done < len(works) and done * len(chunks) < (i + 1) * len(works):
                work, arg = works[done]
                work(arg)
                done += 1
        for at, total in zip(sums, totals or ()):
            sums_ref[8 * at : 8 * at + 8] += total

    att_ref[...] = dot(mixed_ref[0], wide_ref[:, outw], 1, 1)
    bias_att, bias_ffn = side_ref[PAD + 2 : PAD + 3], side_ref[PAD + 3 : PAD + 4]
    gain_one, shift_one, gain_two, shift_two = (side_ref[PAD + i : PAD + i + 1] for i in range(4, 8))

    shift_ffn = shift_one + bias_ffn

    def norm_one(r):
        if r.start < length:
            full = tok_ref[0, r, :].astype(FL)
        else:
            full = state_ref[0].astype(FL) + side_ref[:PAD]
        normed, rstd = norm_rows(full + (att_ref[r, :] + bias_att))
        n1_ref[r, :] = normed
        r1_ref[r, :] = rstd
        low_ref[r, :] = (normed * gain_one + shift_one).astype(BF)
        return []

    weave(norm_one, (), fills[:CUT])

    root = 0.7978845608
    for j in pieces:
        c = slice(j, j + FCHUNK)
        v = dot(low_ref[...], wide_ref[:, c], 1, 0) + upb_ref[:, c]
        square = v * v
        half = 0.5 + 0.5 * jnp.tanh(v * (root + (root * 0.044715) * square))
        act = v * half
        hidden_ref[:, c] = act.astype(BF)
        slope_ref[:, c] = half + (act * (1.0 - half)) * (2 * root + (6 * root * 0.044715) * square)

    att_ref[...] = dot(hidden_ref[...], wide_ref[:, down], 1, 1)

    def norm_two(r):
        normed, rstd = norm_rows(n1_ref[r, :] * gain_one + (att_ref[r, :] + shift_ffn))
        out_ref[0, r, :] = (normed * gain_two + shift_two).astype(BF)
        cot = cot_ref[0, r, :].astype(FL)
        back = norm_back(cot, normed, rstd, gain_two)
        g2_ref[r, :] = back
        low = back.astype(BF)
        gb_ref[r, :] = low
        return [by_eight(low.astype(FL)), by_eight(cot * normed), by_eight(cot)]

    weave(norm_two, (3, 6, 7), fills[CUT:])
    gb_t_ref[...] = gb_ref[:length].T
    low_t_ref[:width] = low_ref[:length].T

    for j in pieces:
        c = slice(j, j + FCHUNK)
        d = slice(hid + j, hid + j + FCHUNK)
        gpre = (dot(gb_ref[...], wide_ref[:, d], 1, 0) * slope_ref[:, c]).astype(BF)
        gpre_ref[:, c] = gpre

    att_ref[...] = dot(gpre_ref[...], wide_ref[:, up], 1, 1)

    def norm_last(r):
        g1 = g2_ref[r, :] + att_ref[r, :]
        normed = n1_ref[r, :]
        back = norm_back(g1, normed, r1_ref[r, :], gain_one)
        one_ref[0, r, :] = back
        low = back.astype(BF)
        ga_ref[r, :] = low
        return [by_eight(low.astype(FL)), by_eight(g1 * normed), by_eight(g1)]

    weave(norm_last, (2, 4, 5), [(down_piece, j) for j in pieces])

    gm_ref[0] = dot(ga_ref[...], wide_ref[:, outw], 1, 0).astype(BF)
    acc_ref[:, outw] += dot(ga_ref[:length], mixed_ref[0, :length], 0, 0)

    mem = pl.ds(pl.multiple_of(step * PAD, PAD), PAD)
    m_low_ref[mem, :] = low_ref[length:, :]
    m_gb_ref[mem, :] = gb_ref[length:, :]
    m_ga_ref[mem, :] = ga_ref[length:, :]
    m_mixed_ref[mem, :] = mixed_ref[0, length:, :]
    m_hidden_ref[mem, :] = hidden_ref[length:, :]
    m_gpre_ref[mem, :] = gpre_ref[length:, :]

    @pl.when(step == last)
    def _():
        more = jnp.concatenate([m_low_ref[...].T, jnp.ones((ONES, m_low_ref.shape[0]), BF)], axis=0)
        left_low = jnp.concatenate([low_t_ref[...], more], axis=1)
        left_gb = m_gb_ref[...].T
        for j in pieces:
            c = slice(j, j + FCHUNK)
            d = slice(hid + j, hid + j + FCHUNK)
            right = jnp.concatenate([gpre_ref[:length, c], m_gpre_ref[:, c]], axis=0)
            made = dot(left_low, right, 1, 0)
            put(c.start, acc_ref[:, c] + made[:width])
            upb_sum_ref[:, c] += made[width : width + 8]
            put(d.start, acc_ref[:, d] + dot(left_gb, m_hidden_ref[:, c], 1, 0))
        put(2 * hid, acc_ref[:, outw] + dot(m_ga_ref[...], m_mixed_ref[...], 0, 0))
        side_ref[...] = jnp.zeros_like(side_ref)
        for i in range(8):
            side_ref[PAD + i : PAD + i + 1] = jnp.sum(sums_ref[8 * i : 8 * i + 8], axis=0, keepdims=True)
        gside_ref[...] = side_ref[...].T
        bias = upb_sum_ref[0:1]
        for i in range(devices):
            piece = bias[:, i * per : (i + 1) * per]
            gside_ref[i * shard : i * shard + 1, BIAS : BIAS + per] = piece
        put(2 * hid + width, gside_ref[...])


def halfway(cols):
    return cols // (2 * LANES) * LANES


def feed(devices, tok, state, near, wide, mixed, cot):
    count, length, width = tok.shape
    rows = length + PAD
    cols = wide.shape[1]
    hid = (cols - width) // 2
    cut = halfway(cols + LANES)
    one = lambda *dims: pl.BlockSpec((1,) + dims, lambda b: (b,) + (0,) * len(dims))
    whole = lambda *dims: pl.BlockSpec(dims, lambda b: (0,) * len(dims), pipeline_mode=pl.Buffered(1))
    final = lambda *dims: pl.BlockSpec(dims, lambda b: (0,) * len(dims))
    vm = pltpu.VMEM
    return pl.pallas_call(
        partial(feed_kernel, devices),
        grid=(count,),
        in_specs=[
            one(length, width),
            one(PAD, width),
            pl.BlockSpec(
                (width, LANES), lambda b: (0, 3 * width // LANES), pipeline_mode=pl.Buffered(1)
            ),
            whole(width, cols),
            one(rows, width),
            one(rows, width),
        ],
        out_specs=[
            one(rows, width),
            one(rows, width),
            one(rows, width),
            final(width, cut),
            final(width, cols + LANES - cut),
        ],
        out_shape=[
            jax.ShapeDtypeStruct((count, rows, width), BF),
            jax.ShapeDtypeStruct((count, rows, width), FL),
            jax.ShapeDtypeStruct((count, rows, width), BF),
            jax.ShapeDtypeStruct((width, cut), BF),
            jax.ShapeDtypeStruct((width, cols + LANES - cut), BF),
        ],
        scratch_shapes=[
            vm((1, hid), FL),
            vm((LANES, width), FL),
            vm((width, LANES), FL),
            vm((width, cols), FL),
            vm((64, width), FL),
            vm((8, hid), FL),
            vm((rows, width), FL),
            vm((rows, width), FL),
            vm((rows, 1), FL),
            vm((rows, width), BF),
            vm((rows, width), FL),
            vm((rows, width), BF),
            vm((rows, hid), BF),
            vm((rows, hid), FL),
            vm((rows, hid), BF),
            vm((rows, width), BF),
            vm((count * PAD, width), BF),
            vm((count * PAD, width), BF),
            vm((count * PAD, width), BF),
            vm((count * PAD, width), BF),
            vm((count * PAD, hid), BF),
            vm((count * PAD, hid), BF),
            vm((width + ONES, length), BF),
            vm((width, length), BF),
        ],
        compiler_params=pltpu.CompilerParams(vmem_limit_bytes=60 << 20),
        name="feed",
    )(tok, state, near, wide, mixed, cot)


def return_kernel(
    qkv_ref,
    pt_ref,
    ptk_ref,
    ptq_ref,
    gm_ref,
    dj_ref,
    kt_ref,
    dpk_ref,
    dsk_ref,
    dqt_ref,
    dk_ref,
    dv_ref,
    s_ref,
    ds_ref,
):
    width = gm_ref.shape[2]
    length = gm_ref.shape[1] - PAD
    group = HALF // HDIM
    blocks = length // LANES
    gpad = group * PAD
    pairs = width // (2 * HDIM)
    masks = pair_masks(2 * HDIM)

    def columns(g, which):
        return slice(which * width + g * HALF, which * width + (g + 1) * HALF)

    def features(g):
        return slice(g * HALF, (g + 1) * HALF)

    def memory_keys(g):
        v_mem = spread(qkv_ref[0, length:, columns(g, 2)], group)
        dpk_ref[g * gpad : (g + 1) * gpad, :] = dot(v_mem, gm_ref[0, :length, features(g)], 1, 1)
        kt_ref[features(g), :] = qkv_ref[0, :length, columns(g, 1)].T

    def memory_queries(g):
        do_mem = spread(gm_ref[0, length:, features(g)], group)
        q_mem = spread(qkv_ref[0, length:, columns(g, 0)], group)
        prob = ptq_ref[0, :, g * gpad : (g + 1) * gpad]
        pf = prob.astype(FL)
        t = pf * dot(qkv_ref[0, :, columns(g, 2)], do_mem, 1, 1)
        ds = (t - pf * jnp.sum(t, axis=0, keepdims=True)).astype(BF)
        dv_ref[:, features(g)] = dot(prob, do_mem, 1, 0)
        dk_ref[:, features(g)] = dot(ds, q_mem, 1, 0)
        dq = fold(dot(ds, qkv_ref[0, :, columns(g, 1)], 0, 0), group)
        dj_ref[0, length:, features(g)] = (dq * SCALE).astype(BF)

    def rise(p, i, slot):
        low, live = i * LANES, (i + 1) * LANES
        base = i * (i + 1) // 2 * LANES
        at = p * 2 * HDIM
        dop = gm_ref[0, low:live, at : at + 2 * HDIM]
        both = jnp.concatenate([dop * masks[0], dop * masks[1]], axis=0)
        dp = dot(qkv_ref[0, :live, 2 * width + at : 2 * width + at + 2 * HDIM], both, 1, 1)
        t = pt_ref[0, p, base : base + live, :].astype(FL) * dp
        s_ref[slot, :live, :] = t
        total = jnp.sum(t, axis=0, keepdims=True)
        deltas = []
        for side in range(2):
            own = slice((2 * p + side) * PAD, (2 * p + side + 1) * PAD)
            tm = ptk_ref[0, own, low:live].astype(FL) * dpk_ref[own, low:live]
            deltas.append(total[:, side * LANES : (side + 1) * LANES] + jnp.sum(tm, axis=0, keepdims=True))
        return deltas

    def settle(p, i, slot, deltas):
        low, live = i * LANES, (i + 1) * LANES
        base = i * (i + 1) // 2 * LANES
        pf = pt_ref[0, p, base : base + live, :].astype(FL)
        ds = s_ref[slot, :live, :] - pf * jnp.concatenate(deltas, axis=1)
        ds_ref[p % 2, base : base + live, :] = ds.astype(BF)
        for side, delta in enumerate(deltas):
            own = slice((2 * p + side) * PAD, (2 * p + side + 1) * PAD)
            pm = ptk_ref[0, own, low:live].astype(FL)
            dsk_ref[own, low:live] = (pm * (dpk_ref[own, low:live] - delta)).astype(BF)

    def gather_rows(p, source, other, into):
        lanes = slice(p * 2 * HDIM, (p + 1) * 2 * HDIM)
        both = []
        for i in range(blocks):
            rows = other[i * LANES : (i + 1) * LANES]
            both.append(jnp.concatenate([rows * masks[0], rows * masks[1]], axis=0))
        for begin in range(0, length, HALF):
            first = begin // LANES
            full = range(first + 1, blocks)
            starts = [i * (i + 1) // 2 * LANES + begin for i in full]
            into[begin : begin + HALF, lanes] += dot(
                jnp.concatenate([source(slice(at, at + HALF)) for at in starts], axis=1),
                jnp.concatenate([both[i] for i in full], axis=0),
                1,
                0,
            )
            at = first * (first + 1) // 2 * LANES + begin
            into[begin : begin + LANES, lanes] += dot(source(slice(at, at + LANES)), both[first], 1, 0)

    def values_back(p):
        lanes = slice(p * 2 * HDIM, (p + 1) * 2 * HDIM)
        gather_rows(p, lambda r: pt_ref[0, p, r, :], gm_ref[0, :length, lanes], dv_ref)

    def keys_back(p):
        lanes = slice(p * 2 * HDIM, (p + 1) * 2 * HDIM)
        gather_rows(p, lambda r: ds_ref[p % 2, r, :], qkv_ref[0, :length, lanes], dk_ref)

    def queries_back(p):
        at = p * 2 * HDIM
        for i in range(blocks):
            low, live = i * LANES, (i + 1) * LANES
            base = i * (i + 1) // 2 * LANES
            made = dot(kt_ref[at : at + 2 * HDIM, :live], ds_ref[p % 2, base : base + live, :], 1, 0)
            for side in range(2):
                dqt_ref[at + side * HDIM : at + (side + 1) * HDIM, low:live] = made[
                    side * HDIM : (side + 1) * HDIM, side * LANES : (side + 1) * LANES
                ]

    def finish(g):
        own = slice(g * gpad, (g + 1) * gpad)
        k_mem = spread(qkv_ref[0, length:, columns(g, 1)], group)
        dq_t = dqt_ref[features(g), :] + dot(k_mem, dsk_ref[own, :], 0, 0)
        dj_ref[0, :length, features(g)] = (dq_t * SCALE).astype(BF).T
        dv_mem = fold(dot(ptk_ref[0, own, :], gm_ref[0, :length, features(g)], 1, 0), group)
        dk_mem = fold(dot(dsk_ref[own, :], qkv_ref[0, :length, columns(g, 0)], 1, 0), group)
        dj_ref[0, :length, columns(g, 1)] = dk_ref[:length, features(g)].astype(BF)
        dj_ref[0, :length, columns(g, 2)] = dv_ref[:length, features(g)].astype(BF)
        dj_ref[0, length:, columns(g, 1)] = (dk_ref[length:, features(g)] + dk_mem).astype(BF)
        dj_ref[0, length:, columns(g, 2)] = (dv_ref[length:, features(g)] + dv_mem).astype(BF)

    groups = width // HALF
    memory_keys(0)
    units = [(p, i) for p in range(pairs) for i in reversed(range(blocks))]
    per_pair = blocks
    deltas = {}
    later = []
    for u in range(len(units) + 2):
        if u < len(units):
            deltas[u] = rise(*units[u], u % SLOTS)
        if u >= 2:
            settle(*units[u - 2], (u - 2) % SLOTS, deltas.pop(u - 2))
            if (u - 1) % per_pair == 0:
                p = (u - 1) // per_pair - 1
                later += [(queries_back, p), (keys_back, p)]
                if p % 2 == 1:
                    later.append((finish, p // 2))
        if u < len(units):
            p, at = u // per_pair, u % per_pair
            if at == 0 and p % 2 == 0:
                memory_queries(p // 2)
            if at == 3:
                values_back(p)
            if at == 2 and p % 2 == 1 and p // 2 + 1 < groups:
                memory_keys(p // 2 + 1)
        if later:
            work, arg = later.pop(0)
            work(arg)
    for work, arg in later:
        work(arg)


def go_back(begin, count, qkv, pt, ptk, ptq, gm):
    rows, width = gm.shape[1:]
    length = rows - PAD
    heads = width // HDIM
    one = lambda *dims: pl.BlockSpec((1,) + dims, lambda b: (b + begin,) + (0,) * len(dims))
    vm = pltpu.VMEM
    return pl.pallas_call(
        return_kernel,
        grid=(count,),
        in_specs=[
            one(rows, 3 * width),
            one(*pt.shape[1:]),
            one(heads * PAD, length),
            one(rows, heads * PAD),
            one(rows, width),
        ],
        out_specs=pl.BlockSpec((1, rows, 3 * width), lambda b: (b, 0, 0)),
        out_shape=jax.ShapeDtypeStruct((count, rows, 3 * width), BF),
        scratch_shapes=[
            vm((width, length), BF),
            vm((heads * PAD, length), FL),
            vm((heads * PAD, length), BF),
            vm((width, length), FL),
            vm((rows, width), FL),
            vm((rows, width), FL),
            vm((SLOTS, length, HALF), FL),
            vm((2, pt.shape[2], HALF), BF),
        ],
        compiler_params=pltpu.CompilerParams(vmem_limit_bytes=36 << 20),
        cost_estimate=pl.CostEstimate(flops=count * 10**10, bytes_accessed=count * 10**7, transcendentals=0),
        name="go_back",
    )(qkv, pt, ptk, ptq, gm)


def weigh_kernel(
    begins,
    tok_ref,
    state_ref,
    one_ref,
    inw_ref,
    *refs,
):
    dj_refs, refs = refs[: len(begins)], refs[len(begins) :]
    gone_ref, gtwo_ref, acc_ref, left_ref, m_in_ref, m_dj_ref, side_ref, memb_ref = refs
    cut = gone_ref.shape[1]
    step = pl.program_id(0)
    last = pl.num_programs(0) - 1
    length, width = tok_ref.shape[1:]
    ends = begins[1:] + [last + 1]

    @pl.when(step == 0)
    def _():
        acc_ref[...] = jnp.zeros_like(acc_ref)
        side_ref[...] = jnp.zeros_like(side_ref)
        memb_ref[...] = inw_ref[:, 3 * width :].astype(FL).T
        left_ref[width:, :] = jnp.ones((ONES, length), BF)

    mem = pl.ds(pl.multiple_of(step * PAD, PAD), PAD)
    m_in_ref[mem, :] = (state_ref[0].astype(FL) + memb_ref[:PAD]).astype(BF)
    side_ref[0:PAD, :] += one_ref[0]
    left_ref[:width, :] = tok_ref[0].T
    for g, dj_ref in enumerate(dj_refs):

        @pl.when((step >= begins[g]) & (step < ends[g]))
        def _(dj_ref=dj_ref):
            m_dj_ref[mem, :] = dj_ref[0, length:, :]
            for j in range(0, 3 * width, FCHUNK):
                c = slice(j, j + FCHUNK)
                acc_ref[:, c] += dot(left_ref[...], dj_ref[0, :length, c], 1, 0)

    @pl.when(step == last)
    def _():
        more = jnp.concatenate([m_in_ref[...].T, jnp.ones((ONES, m_in_ref.shape[0]), BF)], axis=0)
        for j in range(0, 3 * width, FCHUNK):
            c = slice(j, j + FCHUNK)
            acc_ref[:, c] += dot(more, m_dj_ref[:, c], 1, 0)
        gone_ref[...] = acc_ref[:width, :cut].astype(BF)
        gtwo_ref[:, : 3 * width - cut] = acc_ref[:width, cut:].astype(BF)
        back = dot(m_dj_ref[...], inw_ref[:, : 3 * width], 1, 1)
        side_ref[0:PAD, :] += jnp.sum(back.reshape(last + 1, PAD, width), axis=0)
        side_ref[PAD : PAD + 1, :] = acc_ref[width : width + 1, :width]
        side_ref[PAD + 1 : PAD + 2, :] = acc_ref[width : width + 1, 2 * width :]
        gtwo_ref[:, 3 * width - cut :] = side_ref[...].T.astype(BF)


def weigh(tok, state, near, one_grad, djs, begins):
    count, length, width = tok.shape
    rows = length + PAD
    cut = halfway(3 * width + LANES)
    one = lambda *dims: pl.BlockSpec((1,) + dims, lambda b: (b,) + (0,) * len(dims))
    whole = lambda *dims: pl.BlockSpec(dims, lambda b: (0,) * len(dims), pipeline_mode=pl.Buffered(1))
    final = lambda *dims: pl.BlockSpec(dims, lambda b: (0,) * len(dims))
    part = lambda g: pl.BlockSpec(
        (1, rows, 3 * width), lambda b: (jnp.clip(b - begins[g], 0, djs[g].shape[0] - 1), 0, 0)
    )
    vm = pltpu.VMEM
    return pl.pallas_call(
        partial(weigh_kernel, begins),
        grid=(count,),
        in_specs=[
            one(length, width),
            one(PAD, width),
            pl.BlockSpec((1, PAD, width), lambda b: (b, length // PAD, 0)),
            whole(width, 3 * width + LANES),
        ]
        + [part(g) for g in range(len(djs))],
        out_specs=[final(width, cut), final(width, 3 * width + LANES - cut)],
        out_shape=[
            jax.ShapeDtypeStruct((width, cut), BF),
            jax.ShapeDtypeStruct((width, 3 * width + LANES - cut), BF),
        ],
        scratch_shapes=[
            vm((width + ONES, 3 * width), FL),
            vm((width + ONES, length), BF),
            vm((count * PAD, width), BF),
            vm((count * PAD, 3 * width), BF),
            vm((LANES, width), FL),
            vm((LANES, width), FL),
        ],
        compiler_params=pltpu.CompilerParams(vmem_limit_bytes=30 << 20),
        cost_estimate=pl.CostEstimate(flops=count * 10**9, bytes_accessed=count * 3 * 10**6, transcendentals=0),
        name="weigh",
    )(tok, state, one_grad, near, *djs)


def descend_kernel(one_ref, dj_ref, inw_ref, grad_ref):
    width = one_ref.shape[2]
    grad_ref[0] = one_ref[0] + dot(dj_ref[0], inw_ref[:, : 3 * width], 1, 1)


def descend(total, begin, one_grad, dj, near, into):
    count, rows, wide = dj.shape
    width = one_grad.shape[2]
    length = rows - PAD
    shift = lambda *dims: pl.BlockSpec((1,) + dims, lambda b: (b + begin, 0, 0))
    kept = () if into is None else (into,)

    def kernel(one_ref, dj_ref, inw_ref, *rest):
        descend_kernel(one_ref, dj_ref, inw_ref, rest[-1])

    return pl.pallas_call(
        kernel,
        grid=(count,),
        in_specs=[
            shift(length, width),
            pl.BlockSpec((1, length, wide), lambda b: (b, 0, 0)),
            pl.BlockSpec((width, wide + LANES), lambda b: (0, 0), pipeline_mode=pl.Buffered(1)),
        ]
        + [pl.BlockSpec(memory_space=pl.ANY)] * len(kept),
        out_specs=shift(length, width),
        out_shape=jax.ShapeDtypeStruct((total, length, width), FL),
        input_output_aliases={3: 0} if kept else {},
        compiler_params=pltpu.CompilerParams(vmem_limit_bytes=16 << 20),
        cost_estimate=pl.CostEstimate(flops=count * 10**9, bytes_accessed=count * 4 * 10**6, transcendentals=0),
        name="descend",
    )(one_grad, dj, near, *kept)


def pack_kernel(in_ref, up_ref, down_ref, out_ref, vec_ref, bias_ref, mem_ref, near_ref, far_ref, flip_ref):
    shard, cols = in_ref.shape
    hid, width = up_ref.shape[1], out_ref.shape[1]
    flip_ref[...] = jnp.zeros_like(flip_ref)
    flip_ref[PAD : PAD + 8, :shard] = vec_ref[...]
    flip_ref[...] = flip_ref[...].T
    flip_ref[:shard, : mem_ref.shape[1]] = mem_ref[...]
    flip_ref[0:1, BIAS : BIAS + bias_ref.shape[1]] = bias_ref[...]
    near_ref[:, :cols] = in_ref[...].astype(BF)
    near_ref[:, cols:] = flip_ref[:shard].astype(BF)
    far_ref[:, :hid] = up_ref[...].astype(BF)
    far_ref[:, hid : 2 * hid] = down_ref[...].astype(BF)
    far_ref[:, 2 * hid :] = out_ref[...].astype(BF)


def pack(in_w, up_w, down_t, out_t, vectors, bias, mem_t):
    shard, cols = in_w.shape
    wide = 2 * up_w.shape[1] + out_t.shape[1]
    return pl.pallas_call(
        pack_kernel,
        out_shape=[
            jax.ShapeDtypeStruct((shard, cols + LANES), BF),
            jax.ShapeDtypeStruct((shard, wide), BF),
        ],
        scratch_shapes=[pltpu.VMEM((LANES, LANES), FL)],
        name="pack",
    )(in_w, up_w, down_t, out_t, vectors, bias, mem_t)


def square_kernel(cols, *refs):
    held_refs, got_refs, (far_ref, near_ref, sum_ref) = refs[:2], refs[2:4], refs[4:]
    at = 0
    for held_ref, got_ref in zip(held_refs, got_refs):
        size = held_ref.shape[1]
        near_ref[:, at : at + size] = held_ref[...] + got_ref[...].astype(FL)
        at += size
    wide = far_ref.shape[1] - LANES
    near, far = near_ref[:, :cols], far_ref[:, :wide]
    side = near_ref[:, cols:] + far_ref[:, wide:]
    total = jnp.sum(near * near) + jnp.sum(far * far) + jnp.sum(side * side)
    sum_ref[...] = jnp.full(sum_ref.shape, total, FL)


def adam_kernel(sizes, rates, decays, near_ref, far_ref, total_ref, *refs):
    cols, hid, width = sizes
    state_refs, new_refs, norm_ref, flip_ref = refs[:21], refs[21:42], refs[42], refs[43]
    shard = near_ref.shape[0]
    norm = jnp.sqrt(total_ref[...])
    norm_ref[...] = norm[0:1, 0:1]
    factor = (1.0 / jnp.maximum(norm, 1.0))[0:1, 0:1]
    side = near_ref[:, cols:] + far_ref[:, 2 * hid + width :]
    flip_ref[...] = jnp.zeros_like(flip_ref)
    flip_ref[:shard] = side
    turned = flip_ref[...].T
    bias = pltpu.roll(side, LANES - BIAS, 1)
    grads = (
        near_ref[:, :cols],
        far_ref[:, 2 * hid : 2 * hid + width],
        far_ref[:, :hid],
        far_ref[:, hid : 2 * hid],
        turned[PAD : PAD + 8, :shard],
        bias[0:1, : state_refs[15].shape[1]],
        side[:, : state_refs[18].shape[1]],
    )
    correction = 1.0 - 0.5**STEP
    for i in range(7):
        weight, first, second = (state_refs[3 * i + k][...] for k in range(3))
        grad = grads[i] * factor
        first_new = 0.5 * first + 0.5 * grad
        second_new = 0.5 * second + 0.5 * grad * grad
        step = first_new / correction / (jnp.sqrt(second_new / correction) + 1e-08)
        new_refs[3 * i][...] = weight - rates[i] * (step + decays[i] * weight)
        new_refs[3 * i + 1][...] = first_new
        new_refs[3 * i + 2][...] = second_new


def exchange(x, bit, devices):
    return lax.ppermute(x, AXES, [(i, i ^ bit) for i in range(devices)])


def beside(got, sent, work):
    if work is None:
        return got, None
    made = work(lambda value: lax.optimization_barrier((value, sent))[0])
    return lax.optimization_barrier((got, made))


def gather(x, devices, index, works):
    rows, cols = x.shape
    held = x[None]
    results = []
    bits = devices.bit_length() - 1
    for step in range(bits):
        bit = devices >> (step + 1)
        got = exchange(held, bit, devices)
        got, made = beside(got, held, works[step] if step < len(works) else None)
        results.append(made)
        upper = (index & bit) != 0
        held = jnp.stack([jnp.where(upper, got, held), jnp.where(upper, held, got)], axis=1)
        held = held.reshape(-1, rows, cols)
    return held.reshape(devices * rows, cols), [made for made in results if made is not None]


def halve(held, got, place, upper):
    total = held if got is None else held.astype(FL) + got.astype(FL)
    low, high = (lax.index_in_dim(total, i, place, keepdims=False) for i in range(2))
    return jnp.where(upper, high, low), jnp.where(upper, low, high).astype(BF)


def scatter_sum(halves, devices, index, works, then=None):
    rows = halves[0].shape[0] // devices
    bits = devices.bit_length() - 1
    orders = [list(range(bits)) for _ in range(2)]
    if bits > 2:
        orders[1][1:3] = [2, 1]
    held = [half.reshape((2,) * bits + (rows, -1)) for half in halves]
    got = [None, None]
    results = []
    for step in range(bits):
        work = works[step] if step < len(works) else None
        send = [None, None]
        for half, order in enumerate(orders):
            bit = order[step]
            place = sum(1 for other in order[step:] if other > bit)
            upper = (index & (1 << bit)) != 0
            held[half], send[half] = halve(held[half], got[half], place, upper)
        if step < 3:
            got = [exchange(value, 1 << order[step], devices) for value, order in zip(send, orders)]
            got, made = beside(got, send, work)
        else:
            sent = jnp.concatenate(send, axis=-1)
            if step == bits - 1 and then is None:
                return [value.astype(FL).reshape(rows, -1) for value in held], sent, results
            both, made = beside(exchange(sent, 1 << orders[0][step], devices), sent, work)
            cut = send[0].shape[-1]
            got = [both[..., :cut], both[..., cut:]]
        results.append(made)
        if step == 0 and then is not None:
            then(got)
    return [value.astype(FL).reshape(rows, -1) for value in held], [value.reshape(rows, -1) for value in got], results


def butterfly(x, devices):
    for step in range(devices.bit_length() - 1):
        x = x + exchange(x, 1 << step, devices)
    return x


def per_device(
    devices,
    tokens,
    memory_state,
    cotangent,
    in_weight,
    in_first,
    in_second,
    out_weight,
    out_first,
    out_second,
    up_weight,
    up_first,
    up_second,
    down_weight,
    down_first,
    down_second,
    vectors,
    vectors_first,
    vectors_second,
    up_bias,
    up_bias_first,
    up_bias_second,
    memory_embed,
    memory_first,
    memory_second,
):
    index = lax.axis_index(AXES)
    micro, local, length, width = tokens.shape
    count = micro * local
    extra = memory_state.shape[2]
    shard = in_weight.shape[0]
    hid = up_weight.shape[1]
    per_bias = up_bias.shape[0] // shard

    near, far = pack(
        in_weight,
        up_weight,
        down_weight.T,
        out_weight.T,
        vectors,
        up_bias.reshape(1, -1),
        memory_embed.T,
    )
    wide = lax.all_gather(far, AXES, axis=0, tiled=True)

    def pad_state(tie):
        rows = tie(memory_state).reshape(count, extra, width)
        return jnp.pad(rows, ((0, 0), (0, PAD - extra), (0, 0)))

    def align(tie):
        cot = tie(cotangent).reshape(count, extra + length, width)
        return jnp.concatenate(
            [cot[:, extra:], cot[:, :extra], jnp.zeros((count, PAD - extra, width), BF)], axis=1
        )

    near, (state, cot) = gather(near, devices, index, [pad_state, None, None, align])

    tok = tokens.reshape(count, length, width)

    qkv, pt, ptk, ptq, mixed = attend(extra, tok, state, near)
    out, one_grad, gm, *gwide = feed(devices, tok, state, near, wide, mixed, cot)

    def split(sizes):
        begins = [0]
        for size in sizes:
            begins.append(begins[-1] + size)
        return list(zip(begins, sizes))

    djs = []

    def back(begin, size):
        def work(tie):
            djs.append(go_back(begin, size, tie(qkv), pt, ptk, ptq, gm))
            return djs[-1]

        return work

    def whole_weigh(tie):
        return weigh(tie(tok), state, near, one_grad, djs, [begin for begin, _ in runs])

    runs = split(BACK) if sum(BACK) == count else split([count])
    held, got, made = scatter_sum(gwide, devices, index, [back(*run) for run in runs] + [whole_weigh])
    gin = made[len(runs)]
    far_held, far_sent = held, got
    far_got = []

    def last_far(first_got):
        tied = lax.optimization_barrier((far_sent, first_got))[0]
        both = exchange(tied, devices // 2, devices).reshape(shard, -1)
        cut = far_held[0].shape[-1]
        far_got.extend([both[:, :cut], both[:, cut:]])

    grads = []

    def down(i):
        def work(tie):
            into = grads[-1] if grads else None
            grads.append(descend(count, runs[i][0], one_grad, tie(djs[i]), near, into))
            return grads[-1]

        return work

    def order(tie):
        rows = tie(out)
        rows = jnp.concatenate([rows[:, length : length + extra], rows[:, :length]], axis=1)
        return rows.reshape(micro, local, extra + length, width).transpose(0, 2, 1, 3)

    works = [down(i) for i in range(len(runs))] + [order]
    held, got, made = scatter_sum(gin, devices, index, works, last_far)
    input_grad = made[len(runs) - 1].reshape(micro, local, length, width)
    (far_held, far_got), _ = lax.optimization_barrier(((far_held, far_got), made[len(runs) - 1]))
    gfar = jnp.concatenate([mine + more.astype(FL) for mine, more in zip(far_held, far_got)], axis=1)

    gnear, squares = pl.pallas_call(
        partial(square_kernel, 3 * width),
        out_shape=[
            jax.ShapeDtypeStruct((shard, 3 * width + LANES), FL),
            jax.ShapeDtypeStruct((8, LANES), FL),
        ],
        name="squares",
    )(*held, *got, gfar)
    squares = butterfly(squares, devices)
    output = made[len(runs)].transpose(0, 2, 1, 3)
    total_rows = extra + length
    rates = (
        0.5 * width ** (-0.5),
        0.5 * (width * 32 // total_rows) ** (-0.5),
        0.5 * width ** (-0.5),
        0.5 * hid ** (-0.5),
        0.1,
        0.1,
        0.5,
    )
    decays = (0.1, 0.1, 0.1, 0.1, 0.0, 0.0, 0.0)
    same = lambda value: value
    turn = lambda value: value.T
    flat = lambda value: value.reshape(1, -1)
    views = (same, turn, same, turn, same, flat, turn)
    states = (
        (in_weight, in_first, in_second),
        (out_weight, out_first, out_second),
        (up_weight, up_first, up_second),
        (down_weight, down_first, down_second),
        (vectors, vectors_first, vectors_second),
        (up_bias, up_bias_first, up_bias_second),
        (memory_embed, memory_first, memory_second),
    )
    held = [view(value) for view, group in zip(views, states) for value in group]
    *new, norm = pl.pallas_call(
        partial(adam_kernel, (3 * width, hid, width), rates, decays),
        out_shape=[jax.ShapeDtypeStruct(value.shape, FL) for value in held]
        + [jax.ShapeDtypeStruct((1, 1), FL)],
        scratch_shapes=[pltpu.VMEM((LANES, LANES), FL)],
        name="adam",
    )(gnear, gfar, squares, *held)
    back_views = (same, turn, same, turn, same, lambda value: value.reshape(-1), turn)
    results = [back_views[i // 3](value) for i, value in enumerate(new)]
    return (output, input_grad, *results, norm.reshape(()))


def solution(mesh):
    blocks = P(None, AXES, None, None)
    lead = P(AXES, None)
    trail = P(None, AXES)
    flat = P(AXES)
    weights = (lead,) * 3 + (trail,) * 3 + (lead,) * 3 + (trail,) * 6 + (flat,) * 3 + (trail,) * 3
    devices = mesh.shape["dp"] * mesh.shape["fsdp"]
    return jax.shard_map(
        partial(per_device, devices),
        mesh=mesh,
        in_specs=(blocks,) * 3 + weights,
        out_specs=(blocks,) * 2 + weights + (P(),),
        check_vma=False,
    )
```
